32 devices in a mesh: gx: 2 (over y), gy: 4 (over x, core), gz: 4 (over z).
Axes of the slice: x: 2, y: 2, z: 4, core: 2. Of those that a mesh axis runs over, the one named last changes fastest.
Arguments:
- bold_data: bfloat16 [16, 64, 128, 512], P('gx', 'gy', 'gz'), may hold values from -6 to 6
- spatial_maps: float32 [64, 16, 64, 128], P(None, 'gx', 'gy', 'gz'), may hold values from -6 to 6
- live_blocks: int32 [2, 4, 4], P('gx', 'gy', 'gz'), may hold values from 16 to 128, as said below
Outputs:
- new_maps: float32 [64, 16, 64, 128], P(None, 'gx', 'gy', 'gz')
- time_courses: bfloat16 [64, 512], replicated
The draws below stay inside these ranges and needn't reach their ends.
Inputs may be any that keep to these rules, and one draw needn't show every extreme that they name: live_blocks counts live rows of a device's block; rows are numbered (x mod 8) * 16 + (y mod 16) and the live ones come first.
All inputs are finite; a program needn't handle non-finite values.
Results may differ from the reference program's by a relative error of at most 0.011.
Values may be sent and summed in bfloat16 or wider, within the bound.
No kernel may reach another device: no remote copies, remote signals or barrier semaphores. Data moves between devices by JAX's collectives and lax.ppermute only.
A program may use at most 192 MiB of HBM per device.

```python
import math
import jax
import jax.numpy as jnp
from jax import lax

K = 64
FRAMES = 512
RADIUS = 8
ITERS = 2
CX = 8
CY = 16
CZ = 32
NX = 16
NY = 64
NZ = 128
N_GX = 2
N_GY = 4
N_GZ = 4


def draw_live_blocks(key, part):
    first, second = jax.random.split(key)
    total = N_GX * N_GY * N_GZ
    values = jax.random.randint(first, (total,), CX * CY // 8, CX * CY + 1)
    picked = jax.random.randint(second, (), 0, total)
    values = jnp.where(jnp.arange(total) == picked, CX * CY, values)
    return values.reshape(N_GX, N_GY, N_GZ).astype(jnp.int32)


def steps_of(key, extent, shards, low, top_value):
    gain = 1.0
    for axis_at, parts in shards:
        steps = jax.random.uniform(jax.random.fold_in(jax.random.fold_in(key, 6), axis_at), (parts,), jnp.float32, low / len(shards), top_value / len(shards))
        gain = gain * jnp.repeat(jnp.exp(steps), extent[axis_at] // parts).reshape((-1,) + (1,) * (len(extent) - 1 - axis_at))
    return gain


def normal_values(key, dims, scale, most, cuts=(), kind=jnp.bfloat16):
    factor_of = steps_of(key, dims, cuts, -0.22, 0.18) if cuts else 1.0
    array = jax.random.normal(key, dims, jnp.float32) * scale * factor_of
    return jnp.minimum(jnp.maximum(array, -most), most).astype(kind)


def setup_inputs(seed: int = 0) -> dict:
    key_of = jax.random.split(jax.random.key(seed), 4)
    bold_data = normal_values(key_of[0], (NX, NY, NZ, FRAMES), 1.0, 6.0, ((0, 2), (1, 4), (2, 4)))
    spatial_maps = normal_values(key_of[1], (K, NX, NY, NZ), 1.0, 6.0, ((1, 2), (2, 4), (3, 4)), jnp.float32)
    live_blocks = draw_live_blocks(jax.random.fold_in(key_of[3], 71), 0)
    return dict(bold_data=bold_data, spatial_maps=spatial_maps, live_blocks=live_blocks)


def band_matrix(length, dtype):
    total = sum((math.exp(-float(d * d) / 32.0) for d in range(-RADIUS, RADIUS + 1)))
    count = length - 2 * RADIUS
    rows = lax.broadcasted_iota(jnp.int32, (length, count), 0)
    cols = lax.broadcasted_iota(jnp.int32, (length, count), 1)
    offset = (rows - cols - RADIUS).astype(dtype)
    inside = jnp.logical_and(rows - cols >= 0, rows - cols <= 2 * RADIUS)
    return jnp.where(inside, jnp.exp(-offset * offset / 32.0) / total, jnp.zeros_like(offset))

def filter_along(field, axis):
    band = band_matrix(field.shape[axis], field.dtype)
    result = jnp.tensordot(field, band, axes=((axis,), (0,)), precision=lax.Precision.HIGHEST)
    return jnp.moveaxis(result, -1, axis)

def smooth_one(single):
    padded = jnp.pad(single.astype(jnp.float32), RADIUS)
    return filter_along(filter_along(filter_along(padded, 0), 1), 2)

def reference(bold_data, spatial_maps, live_blocks):
    rows = (jnp.arange(NX, dtype=jnp.int32) % CX)[:, None] * CY + (jnp.arange(NY, dtype=jnp.int32) % CY)[None, :]
    counts = jnp.repeat(jnp.repeat(jnp.repeat(live_blocks, CX, axis=0), CY, axis=1), CZ, axis=2)
    live = rows[:, :, None] < counts
    live_half = live.astype(jnp.bfloat16)[None]
    live_flat = live.reshape(-1).astype(jnp.float32)
    flat_frames = bold_data.reshape(NX * NY * NZ, FRAMES)
    weights = spatial_maps.reshape(K, NX * NY * NZ)
    rounded = None
    for step in range(ITERS):
        plain = weights.reshape(K, NX, NY, NZ).astype(jnp.bfloat16)
        smoothed = lax.map(smooth_one, plain).astype(jnp.bfloat16) * live_half
        courses = jnp.dot(smoothed.reshape(K, -1), flat_frames, preferred_element_type=jnp.float32)
        gram = jnp.dot(courses, courses.T, precision=lax.Precision.HIGHEST)
        trace_value = jnp.trace(gram)
        rounded = courses.astype(jnp.bfloat16)
        raw_grad = (jnp.dot(rounded, flat_frames.T, preferred_element_type=jnp.float32) * live_flat[None, :]).astype(jnp.bfloat16)
        grad = lax.map(smooth_one, raw_grad.reshape(K, NX, NY, NZ)).reshape(K, -1)
        energy = jnp.sum(grad * grad) / float(K * NX * NY * NZ)
        scale = 1.0 / jnp.sqrt(energy + 1e-06)
        decay = jnp.dot(gram, weights, precision=lax.Precision.HIGHEST)
        weights = weights + 0.5 * (grad * scale - float(K) / trace_value * decay)
    return (weights.reshape(K, NX, NY, NZ), rounded)
```

```python
import functools
import math

import jax
import jax.numpy as jnp
import ml_dtypes
import numpy as np
from jax import lax
from jax.experimental import pallas as pl
from jax.experimental.pallas import tpu as pltpu
from jax.sharding import PartitionSpec as P

RADIUS = 8
F32 = jnp.float32
BF16 = jnp.bfloat16
AXES = ("gx", "gy", "gz")


def band(length):
    total = sum(math.exp(-float(d * d) / 32.0) for d in range(-RADIUS, RADIUS + 1))
    gap = np.abs(np.arange(length)[:, None] - np.arange(length)[None, :])
    return np.where(gap <= RADIUS, np.exp(-(gap.astype(np.float64) ** 2) / 32.0) / total, 0.0)


def windows(matrix, size, parts, reach):
    padded = np.pad(matrix, ((0, 0), (reach, reach)))
    return np.stack(
        [padded[p * size : (p + 1) * size, p * size : (p + 1) * size + 2 * reach] for p in range(parts)]
    )


def half(array):
    return np.asarray(array, dtype=ml_dtypes.bfloat16)


def inner_window(size):
    return windows(band(3 * size), size, 3, RADIUS)[1]


def vmem(count):
    return [pl.BlockSpec(memory_space=pltpu.VMEM)] * count


def call(body, shapes, smem, arrays, flops=10**8, name=None):
    total = sum(a.size * a.dtype.itemsize for a in arrays)
    return pl.pallas_call(
        body,
        out_shape=shapes,
        in_specs=[pl.BlockSpec(memory_space=pltpu.SMEM)] * len(smem) + vmem(len(arrays)),
        out_specs=jax.tree.map(lambda _: pl.BlockSpec(memory_space=pltpu.VMEM), shapes),
        compiler_params=pltpu.CompilerParams(vmem_limit_bytes=40 * 1024 * 1024),
        cost_estimate=pl.CostEstimate(flops=flops, bytes_accessed=total, transcendentals=0),
        name=name,
    )(*smem, *arrays)


def dot(a, b):
    return jnp.dot(a, b, preferred_element_type=F32)


def pack_maps(voxel_maps, layers, chans, plane):
    def body(src, out):
        unit = (
            lax.broadcasted_iota(jnp.int32, (chans, chans), 0)
            == lax.broadcasted_iota(jnp.int32, (chans, chans), 1)
        ).astype(F32).astype(BF16)
        for x in range(layers):
            turned = lax.dot_general(
                unit, src[x].astype(BF16), (((1,), (1,)), ((), ())), preferred_element_type=F32
            )
            out[x * chans : (x + 1) * chans, :] = turned.astype(BF16)

    return call(body, jax.ShapeDtypeStruct((layers * chans, plane), BF16), [], [voxel_maps], name="pack_maps")


def mix_layers(place, coefs, chans, sources, sums, out_types):
    rows, plane = sources[0].shape
    outs = len(out_types)
    base = len(sources)
    tall, wide = 16, 128

    def body(place_ref, *refs):
        ins, adds, results = refs[:base], refs[base : base + len(sums)], refs[base + len(sums) :]

        def run(tables):
            layers = tables[0][0].shape[0]
            for r in range(0, chans, tall):
                for c in range(0, plane, wide):
                    tiles = [
                        [
                            src[s * chans + r : s * chans + r + tall, c : c + wide].astype(F32)
                            for s in range(layers)
                        ]
                        for src in ins
                    ]
                    for o in range(outs):
                        for x in range(layers):
                            at = slice(x * chans + r, x * chans + r + tall)
                            total = adds[o][at, c : c + wide] if adds else None
                            for tile, table in zip(tiles, tables[o]):
                                for s in range(layers):
                                    weight = float(table[x, s])
                                    if weight != 0.0:
                                        term = tile[s] * weight
                                        total = term if total is None else total + term
                            if total is None:
                                total = jnp.zeros((tall, wide), F32)
                            results[o][at, c : c + wide] = total.astype(results[o].dtype)

        if len(coefs) == 1:
            run(coefs[0])
        else:
            for v in range(len(coefs)):
                pl.when(place_ref[0] == v)(functools.partial(run, coefs[v]))

    shapes = tuple(jax.ShapeDtypeStruct((rows, plane), t) for t in out_types)
    return call(body, shapes, [place], [*sources, *sums], name="mix_layers")


def blocks_dot(pieces, table, out_type, name):
    rows, plane = (pieces[0].shape[0], table.shape[1])

    def body(*refs):
        ins, weights, out = refs[:-2], refs[-2], refs[-1]
        at, total = 0, None
        for piece in ins:
            width = piece.shape[1]
            term = dot(piece[...], weights[at : at + width, :])
            total = term if total is None else total + term
            at += width
        out[...] = total.astype(out.dtype)

    return call(body, jax.ShapeDtypeStruct((rows, plane), out_type), [], [*pieces, table], name=name)


def live_lanes(count, layer, shape, size_y, size_z):
    row = layer * size_y + lax.broadcasted_iota(jnp.int32, shape, 1) // size_z
    return row < count


def courses_of(count, acc, pieces, table, bold, chans, size_y, size_z):
    frames = bold.shape[1]
    plane = size_y * size_z
    layers = bold.shape[0] // plane

    def body(count_ref, *refs):
        ins = refs[: len(pieces)]
        rest = refs[len(pieces) :]
        weights, frames_ref, out = rest[0], rest[1], rest[-1]
        start = rest[2] if acc is not None else None
        total = jnp.zeros((chans, frames), F32)
        for x in range(layers):
            rows = slice(x * chans, (x + 1) * chans)
            value = start[rows, :] if start is not None else None
            at = 0
            for piece in ins:
                width = piece.shape[1]
                term = dot(piece[rows, :], weights[at : at + width, :])
                value = term if value is None else value + term
                at += width
            keep = live_lanes(count_ref[0], x, value.shape, size_y, size_z)
            value = jnp.where(keep, value, 0.0).astype(BF16)
            total = total + dot(value, frames_ref[x * plane : (x + 1) * plane, :])
        out[...] = total

    arrays = [*pieces, table, bold] + ([acc] if acc is not None else [])
    return call(
        body, jax.ShapeDtypeStruct((chans, frames), F32), [count], arrays, flops=10**9, name="courses_of"
    )


def raw_gradient(count, courses, bold, size_y, size_z):
    chans, frames = courses.shape
    plane = size_y * size_z
    layers = bold.shape[0] // plane

    def body(count_ref, courses_ref, frames_ref, out):
        for x in range(layers):
            value = lax.dot_general(
                courses_ref[...],
                frames_ref[x * plane : (x + 1) * plane, :],
                (((1,), (1,)), ((), ())),
                preferred_element_type=F32,
            )
            keep = live_lanes(count_ref[0], x, value.shape, size_y, size_z)
            out[x * chans : (x + 1) * chans, :] = jnp.where(keep, value, 0.0).astype(BF16)

    return call(
        body,
        jax.ShapeDtypeStruct((layers * chans, plane), BF16),
        [count],
        [courses, bold],
        flops=10**9,
        name="raw_gradient",
    )


def gradient_of(acc, pieces, table, chans):
    rows, plane = acc.shape
    layers = rows // chans

    def body(start, *refs):
        ins, weights, out, energy = refs[:-3], refs[-3], refs[-2], refs[-1]
        total = jnp.zeros((chans, plane), F32)
        for x in range(layers):
            at, value = 0, start[x * chans : (x + 1) * chans, :]
            for piece in ins:
                width = piece.shape[1]
                value = value + dot(piece[x * chans : (x + 1) * chans, :], weights[at : at + width, :])
                at += width
            total = total + value * value
            out[x] = value.T
        energy[...] = jnp.sum(total).reshape(1, 1)

    shapes = (jax.ShapeDtypeStruct((layers, plane, chans), F32), jax.ShapeDtypeStruct((1, 1), F32))
    return call(body, shapes, [], [acc, *pieces, table], name="gradient_of")


def base_maps(voxel_maps, grad, first, second):
    layers, plane, chans = voxel_maps.shape

    def body(maps_ref, grad_ref, first_ref, second_ref, out):
        for x in range(layers):
            out[x] = lax.dot_general(
                maps_ref[x],
                first_ref[...],
                (((1,), (1,)), ((), ())),
                precision=lax.Precision.HIGHEST,
                preferred_element_type=F32,
            ) + lax.dot_general(
                grad_ref[x],
                second_ref[...],
                (((1,), (1,)), ((), ())),
                precision=lax.Precision.HIGHEST,
                preferred_element_type=F32,
            )

    return call(
        body,
        jax.ShapeDtypeStruct((layers, plane, chans), F32),
        [],
        [voxel_maps, grad, first, second],
        flops=10**9,
        name="base_maps",
    )


def final_maps(scale, base, grad):
    layers, plane, chans = base.shape

    def body(scale_ref, base_ref, grad_ref, out):
        out[...] = base_ref[...] + scale_ref[0] * grad_ref[...]

    return call(
        body, jax.ShapeDtypeStruct((layers, plane, chans), F32), [scale], [base, grad], name="final_maps"
    )


def shifted(lower, upper, axis):
    peers = lax.axis_size(axis)
    up = [(i, i + 1) for i in range(peers - 1)]
    down = [(j, i) for i, j in up]
    return lax.ppermute(upper, axis, up), lax.ppermute(lower, axis, down)


def hypercube_sum(value, narrow):
    steps = []
    for axis in AXES:
        peers = lax.axis_size(axis)
        if peers & (peers - 1):
            return lax.psum(value, AXES)
        steps += [(axis, 1 << b) for b in range(peers.bit_length() - 1)]
    for axis, bit in steps:
        pairs = [(i, i ^ bit) for i in range(lax.axis_size(axis))]
        if narrow:
            value = lax.reduce_precision(value, 8, 7)
            value = value + lax.ppermute(value.astype(BF16), axis, pairs).astype(F32)
        else:
            value = value + lax.ppermute(value, axis, pairs)
    return value


def per_device(bold_data, spatial_maps, live_blocks):
    chans, size_x, size_y, size_z = spatial_maps.shape
    frames = bold_data.shape[3]
    plane = size_y * size_z
    parts_x, parts_y, parts_z = (lax.axis_size(a) for a in AXES)
    place_x = lax.axis_index("gx").astype(jnp.int32).reshape(1)
    count = live_blocks.reshape(1)
    bold = bold_data.reshape(size_x * plane, frames)
    voxel_maps = jnp.transpose(spatial_maps, (1, 2, 3, 0)).reshape(size_x, plane, chans)
    all_cells = float(chans * size_x * plane * parts_x * parts_y * parts_z)

    win_x, win_y, win_z = (inner_window(s) for s in (size_x, size_y, size_z))
    unit_z = np.eye(size_z)
    ends = np.concatenate([np.kron(win_y.T, unit_z[:, :RADIUS]), np.kron(win_y.T, unit_z[:, -RADIUS:])], 1)
    table_ends = jnp.asarray(half(ends))
    table_own = jnp.asarray(half(np.kron(win_y.T, win_z[:, RADIUS:-RADIUS].T)))
    unit_y = np.eye(size_y)
    table_z = jnp.asarray(
        half(np.concatenate([np.kron(unit_y, win_z[:, :RADIUS].T), np.kron(unit_y, win_z[:, -RADIUS:].T)]))
    )
    face_y, face_z = RADIUS * size_z, RADIUS * size_y

    reach = 2 * RADIUS
    twice = parts_x == 2 and size_y == reach and size_z == 2 * reach
    pair_x = parts_x == 2
    full_x = band(size_x * parts_x)
    own_x = [slice(p * size_x, (p + 1) * size_x) for p in range(parts_x)]

    def coefs_x(matrices):
        mine = [[[m[own_x[p], own_x[p]]] for m in matrices] for p in range(2)]
        other = [[[m[own_x[p], own_x[1 - p]]] for m in matrices] for p in range(2)]
        return mine, other

    def along_x(block, matrices):
        if pair_x:
            mine, other = coefs_x(matrices)
            got = lax.ppermute(block, "gx", [(0, 1), (1, 0)])
            sums = mix_layers(place_x, mine, chans, [block], [], [F32] * len(matrices))
            return mix_layers(place_x, other, chans, [got], list(sums), [BF16] * len(matrices))
        depth = RADIUS * chans
        before, after = shifted(block[:depth], block[-depth:], "gx")
        rest = jnp.zeros((block.shape[0] - depth, plane), BF16)
        before, after = jnp.concatenate([rest, before]), jnp.concatenate([after, rest])
        tables = []
        for lo in (-size_x, 0, size_x):
            columns = np.arange(size_x) + lo + RADIUS
            inside = (columns >= 0) & (columns < win_x.shape[1])
            tables.append(np.where(inside[None], win_x[:, np.clip(columns, 0, win_x.shape[1] - 1)], 0.0))
        return mix_layers(place_x, [[tables]], chans, [before, block, after], [], [BF16])

    def along_rest(first):
        before, after = shifted(first[:, :face_y], first[:, -face_y:], "gy")
        pieces = [before, first, after]
        faces = blocks_dot(pieces, table_ends, BF16, "faces_z")
        below, above = shifted(faces[:, :face_z], faces[:, face_z:], "gz")
        acc = blocks_dot(pieces, table_own, F32, "filter_own")
        return acc, [below, above]

    def all_courses(acc, pieces, table):
        return hypercube_sum(
            courses_of(count, acc, pieces, table, bold, chans, size_y, size_z), narrow=True
        )

    plain = pack_maps(voxel_maps, size_x, chans, plane)
    (first,) = along_x(plain, [full_x])
    acc, pieces = along_rest(first)
    courses1 = all_courses(acc, pieces, table_z)
    half1 = courses1.astype(BF16)
    raw1 = raw_gradient(count, half1, bold, size_y, size_z)
    if twice:
        first, second = along_x(raw1, [full_x, full_x @ full_x])
        square_y = windows(np.linalg.matrix_power(band(size_y * parts_y), 2), size_y, parts_y, reach)
        square_z = windows(np.linalg.matrix_power(band(size_z * parts_z), 2), size_z, parts_z, reach)
        ordered = np.concatenate([unit_z[:, :reach], unit_z[:, reach:]], 1).reshape(size_z, 2, reach)
        tables_y = np.stack([
            np.concatenate([np.kron(w.T, ordered[:, h]) for h in range(2)], 1) for w in square_y
        ])
        tables_z = np.stack([
            np.concatenate([np.kron(unit_y, w[:, h * reach : (h + 1) * reach].T) for h in range(4)])
            for w in square_z
        ])
        table_y2 = lax.dynamic_index_in_dim(jnp.asarray(half(tables_y)), lax.axis_index("gy"), 0, False)
        table_z2 = lax.dynamic_index_in_dim(jnp.asarray(half(tables_z)), lax.axis_index("gz"), 0, False)
        before, after = shifted(second, second, "gy")
        both = blocks_dot([before, second, after], table_y2, BF16, "filter_y2")
        wide = reach * size_y
        lower, upper = both[:, :wide], both[:, wide:]
        below, above = shifted(lower, upper, "gz")
        change = all_courses(None, [below, lower, upper, above], table_z2)
        acc1, pieces1 = along_rest(first)
        grad1, _ = gradient_of(acc1, pieces1, table_z, chans)
    else:
        (first,) = along_x(raw1, [full_x])
        acc1, pieces1 = along_rest(first)
        grad1, _ = gradient_of(acc1, pieces1, table_z, chans)
        again = pack_maps(grad1, size_x, chans, plane)
        (second,) = along_x(again, [full_x])
        acc2, pieces2 = along_rest(second)
        change = all_courses(acc2, pieces2, table_z)

    def gram_of(courses):
        gram = jnp.dot(courses, courses.T, precision=lax.Precision.HIGHEST)
        return 0.5 * (float(chans) / jnp.trace(gram)) * gram

    unit = jnp.eye(chans, dtype=F32)
    gram1 = gram_of(courses1)
    energy1 = jnp.maximum(jnp.sum(half1.astype(F32) * change), 0.0) / all_cells
    scale1 = 0.5 / jnp.sqrt(energy1 + 1e-06)
    kept = courses1 - jnp.dot(gram1, courses1, precision=lax.Precision.HIGHEST)

    courses2 = kept + scale1 * change
    half2 = courses2.astype(BF16)
    raw2 = raw_gradient(count, half2, bold, size_y, size_z)
    (first,) = along_x(raw2, [full_x])
    acc, pieces = along_rest(first)
    grad2, squares = gradient_of(acc, pieces, table_z, chans)
    energy2 = hypercube_sum(squares, narrow=False) / all_cells
    scale2 = (0.5 / jnp.sqrt(energy2 + 1e-06)).reshape(1)

    fade2 = unit - gram_of(courses2)
    fades = jnp.dot(fade2, unit - gram1, precision=lax.Precision.HIGHEST)
    base = base_maps(voxel_maps, grad1, fades, scale1 * fade2)
    maps = final_maps(scale2, base, grad2).reshape(size_x, size_y, size_z, chans)
    return (jnp.transpose(maps, (3, 0, 1, 2)), half2)


def solution(mesh):
    return jax.shard_map(
        per_device,
        mesh=mesh,
        in_specs=(P("gx", "gy", "gz", None), P(None, "gx", "gy", "gz"), P("gx", "gy", "gz")),
        out_specs=(P(None, "gx", "gy", "gz"), P()),
        check_vma=False,
    )
```

```python
import functools
import math

import jax
import jax.numpy as jnp
import ml_dtypes
import numpy as np
from jax import lax
from jax.experimental import pallas as pl
from jax.experimental.pallas import tpu as pltpu
from jax.sharding import PartitionSpec as P

RADIUS = 8
F32 = jnp.float32
BF16 = jnp.bfloat16
AXES = ("gx", "gy", "gz")


def band(length):
    total = sum(math.exp(-float(d * d) / 32.0) for d in range(-RADIUS, RADIUS + 1))
    gap = np.abs(np.arange(length)[:, None] - np.arange(length)[None, :])
    return np.where(gap <= RADIUS, np.exp(-(gap.astype(np.float64) ** 2) / 32.0) / total, 0.0)


def windows(matrix, size, parts, reach):
    padded = np.pad(matrix, ((0, 0), (reach, reach)))
    return np.stack(
        [padded[p * size : (p + 1) * size, p * size : (p + 1) * size + 2 * reach] for p in range(parts)]
    )


def half(array):
    return np.asarray(array, dtype=ml_dtypes.bfloat16)


def inner_window(size):
    return windows(band(3 * size), size, 3, RADIUS)[1]


def vmem(count):
    return [pl.BlockSpec(memory_space=pltpu.VMEM)] * count


def call(body, shapes, smem, arrays, flops=10**8, name=None):
    total = sum(a.size * a.dtype.itemsize for a in arrays)
    return pl.pallas_call(
        body,
        out_shape=shapes,
        in_specs=[pl.BlockSpec(memory_space=pltpu.SMEM)] * len(smem) + vmem(len(arrays)),
        out_specs=jax.tree.map(lambda _: pl.BlockSpec(memory_space=pltpu.VMEM), shapes),
        compiler_params=pltpu.CompilerParams(vmem_limit_bytes=16 * 1024 * 1024),
        cost_estimate=pl.CostEstimate(flops=flops, bytes_accessed=total, transcendentals=0),
        name=name,
    )(*smem, *arrays)


def dot(a, b):
    return jnp.dot(a, b, preferred_element_type=F32)


def pack_maps(voxel_maps, layers, chans, plane):
    def body(src, out):
        unit = (
            lax.broadcasted_iota(jnp.int32, (chans, chans), 0)
            == lax.broadcasted_iota(jnp.int32, (chans, chans), 1)
        ).astype(F32).astype(BF16)
        for x in range(layers):
            turned = lax.dot_general(
                unit, src[x].astype(BF16), (((1,), (1,)), ((), ())), preferred_element_type=F32
            )
            out[x * chans : (x + 1) * chans, :] = turned.astype(BF16)

    return call(body, jax.ShapeDtypeStruct((layers * chans, plane), BF16), [], [voxel_maps], name="pack_maps")


def mix_layers(place, odd, coefs, chans, sources, sums, out_types, face=0):
    rows, plane = sources[0].shape
    outs = len(out_types)
    base = len(sources)
    tall, wide = 16, 128

    def body(place_ref, odd_ref, *refs):
        ins, adds, results = refs[:base], refs[base : base + len(sums)], refs[base + len(sums) :]

        def run(tables):
            layers = tables[0][0].shape[0]
            for r in range(0, chans, tall):
                for c in range(0, plane, wide):
                    tiles = [
                        [
                            src[s * chans + r : s * chans + r + tall, c : c + wide].astype(F32)
                            for s in range(layers)
                        ]
                        for src in ins
                    ]
                    for o in range(outs):
                        for x in range(layers):
                            at = slice(x * chans + r, x * chans + r + tall)
                            total = adds[o][at, c : c + wide] if adds else None
                            for tile, table in zip(tiles, tables[o]):
                                for s in range(layers):
                                    weight = float(table[x, s])
                                    if weight != 0.0:
                                        term = tile[s] * weight
                                        total = term if total is None else total + term
                            if total is None:
                                total = jnp.zeros((tall, wide), F32)
                            results[o][at, c : c + wide] = total.astype(results[o].dtype)

        if len(coefs) == 1:
            run(coefs[0])
        else:
            for v in range(len(coefs)):
                pl.when(place_ref[0] == v)(functools.partial(run, coefs[v]))
        if face:
            send_faces(odd_ref, results[0], face, *results[outs:])

    shapes = tuple(jax.ShapeDtypeStruct((rows, plane), t) for t in out_types)
    if face:
        shapes += tuple(jax.ShapeDtypeStruct((rows, face), out_types[0]) for _ in range(2))
    return call(body, shapes, [place, odd], [*sources, *sums], name="mix_layers")


def send_faces(odd_ref, field, face, first, second):
    plane = field.shape[1]

    def write(low, high):
        low[...] = field[:, :face].astype(low.dtype)
        high[...] = field[:, plane - face :].astype(high.dtype)

    pl.when(odd_ref[0] == 0)(lambda: write(second, first))
    pl.when(odd_ref[0] != 0)(lambda: write(first, second))


def swapped_dot(odd_ref, first, middle, second, weights, rows=slice(None)):
    width = first.shape[1]
    end = weights.shape[0] - width
    even = odd_ref[0] == 0
    from_first = pl.multiple_of(jnp.where(even, end, 0), width)
    from_second = pl.multiple_of(jnp.where(even, 0, end), width)
    total = dot(first[rows, :], weights[pl.ds(from_first, width), :])
    total = total + dot(second[rows, :], weights[pl.ds(from_second, width), :])
    at = width
    for piece in middle:
        total = total + dot(piece[rows, :], weights[at : at + piece.shape[1], :])
        at += piece.shape[1]
    return total


def filter_lanes(odd, first, middle, second, table, name):
    rows, plane = first.shape[0], table.shape[1]

    def body(odd_ref, first_ref, middle_ref, second_ref, weights, out):
        out[...] = swapped_dot(odd_ref, first_ref, [middle_ref], second_ref, weights)

    return call(
        body, jax.ShapeDtypeStruct((rows, plane), F32), [odd], [first, middle, second, table], name=name
    )


def filter_faces(odd_in, odd_out, first, middle, second, table, name):
    rows, face = first.shape[0], table.shape[1] // 2

    def body(odd_ref, odd_next, first_ref, middle_ref, second_ref, weights, out_first, out_second):
        total = swapped_dot(odd_ref, first_ref, [middle_ref], second_ref, weights)
        send_faces(odd_next, total, face, out_first, out_second)

    shapes = tuple(jax.ShapeDtypeStruct((rows, face), BF16) for _ in range(2))
    return call(body, shapes, [odd_in, odd_out], [first, middle, second, table], name=name)


def live_lanes(count, layer, shape, size_y, size_z):
    row = layer * size_y + lax.broadcasted_iota(jnp.int32, shape, 1) // size_z
    return row < count


def courses_of(count, odd, acc, first, middle, second, table, bold, chans, size_y, size_z):
    frames = bold.shape[1]
    plane = size_y * size_z
    layers = bold.shape[0] // plane
    between = len(middle)

    def body(count_ref, odd_ref, first_ref, *refs):
        ins, second_ref, weights, frames_ref = refs[:between], *refs[between : between + 3]
        out = refs[-1]
        total = jnp.zeros((chans, frames), F32)
        for x in range(layers):
            rows = slice(x * chans, (x + 1) * chans)
            value = swapped_dot(odd_ref, first_ref, ins, second_ref, weights, rows)
            if acc is not None:
                value = value + refs[between + 3][rows, :]
            keep = live_lanes(count_ref[0], x, value.shape, size_y, size_z)
            value = jnp.where(keep, value, 0.0).astype(BF16)
            total = total + dot(value, frames_ref[x * plane : (x + 1) * plane, :])
        out[...] = total

    arrays = [first, *middle, second, table, bold] + ([acc] if acc is not None else [])
    shape = jax.ShapeDtypeStruct((chans, frames), F32)
    return call(body, shape, [count, odd], arrays, flops=10**9, name="courses_of")


def raw_gradient(count, courses, bold, size_y, size_z):
    chans, frames = courses.shape
    plane = size_y * size_z
    layers = bold.shape[0] // plane

    def body(count_ref, courses_ref, frames_ref, out):
        for x in range(layers):
            value = lax.dot_general(
                courses_ref[...],
                frames_ref[x * plane : (x + 1) * plane, :],
                (((1,), (1,)), ((), ())),
                preferred_element_type=F32,
            )
            keep = live_lanes(count_ref[0], x, value.shape, size_y, size_z)
            out[x * chans : (x + 1) * chans, :] = jnp.where(keep, value, 0.0).astype(BF16)

    return call(
        body,
        jax.ShapeDtypeStruct((layers * chans, plane), BF16),
        [count],
        [courses, bold],
        flops=10**9,
        name="raw_gradient",
    )


def gradient_of(odd, acc, first, second, table, chans):
    rows, plane = acc.shape
    layers = rows // chans

    def body(odd_ref, start, first_ref, second_ref, weights, out, energy):
        total = jnp.zeros((chans, plane), F32)
        for x in range(layers):
            at = slice(x * chans, (x + 1) * chans)
            value = start[at, :] + swapped_dot(odd_ref, first_ref, [], second_ref, weights, at)
            total = total + value * value
            out[x] = value.T
        energy[...] = jnp.sum(total).reshape(1, 1)

    shapes = (jax.ShapeDtypeStruct((layers, plane, chans), F32), jax.ShapeDtypeStruct((1, 1), F32))
    return call(body, shapes, [odd], [acc, first, second, table], name="gradient_of")


def base_maps(voxel_maps, grad, first, second):
    layers, plane, chans = voxel_maps.shape

    def body(maps_ref, grad_ref, first_ref, second_ref, out):
        for x in range(layers):
            out[x] = lax.dot_general(
                maps_ref[x],
                first_ref[...],
                (((1,), (1,)), ((), ())),
                precision=lax.Precision.HIGHEST,
                preferred_element_type=F32,
            ) + lax.dot_general(
                grad_ref[x],
                second_ref[...],
                (((1,), (1,)), ((), ())),
                precision=lax.Precision.HIGHEST,
                preferred_element_type=F32,
            )

    return call(
        body,
        jax.ShapeDtypeStruct((layers, plane, chans), F32),
        [],
        [voxel_maps, grad, first, second],
        flops=10**9,
        name="base_maps",
    )


def final_maps(scale, base, grad):
    layers, plane, chans = base.shape

    def body(scale_ref, base_ref, grad_ref, out):
        out[...] = base_ref[...] + scale_ref[0] * grad_ref[...]

    return call(
        body, jax.ShapeDtypeStruct((layers, plane, chans), F32), [scale], [base, grad], name="final_maps"
    )


def swapped(first, second, axis):
    peers = lax.axis_size(axis)
    got = []
    for start, face in ((0, first), (1, second)):
        pairs = [(i, i + 1) for i in range(start, peers - 1, 2)]
        got.append(lax.ppermute(face, axis, pairs + [(j, i) for i, j in pairs]))
    return got


def shifted(lower, upper, axis):
    peers = lax.axis_size(axis)
    up = [(i, i + 1) for i in range(peers - 1)]
    down = [(j, i) for i, j in up]
    return lax.ppermute(upper, axis, up), lax.ppermute(lower, axis, down)


def hypercube_sum(value, narrow):
    steps = []
    for axis in AXES:
        peers = lax.axis_size(axis)
        if peers & (peers - 1):
            return lax.psum(value, AXES)
        steps += [(axis, 1 << b) for b in range(peers.bit_length() - 1)]
    for axis, bit in steps:
        pairs = [(i, i ^ bit) for i in range(lax.axis_size(axis))]
        if narrow:
            value = lax.reduce_precision(value, 8, 7)
            value = value + lax.ppermute(value.astype(BF16), axis, pairs).astype(F32)
        else:
            value = value + lax.ppermute(value, axis, pairs)
    return value


def scattered_sum(value):
    peers = lax.axis_size(AXES)
    spread = jnp.broadcast_to(value.reshape(1, 1), (peers, 128))
    return jnp.sum(lax.all_to_all(spread, AXES, 0, 0, tiled=True)[:, :1])


def per_device(bold_data, spatial_maps, live_blocks):
    chans, size_x, size_y, size_z = spatial_maps.shape
    frames = bold_data.shape[3]
    plane = size_y * size_z
    parts_x, parts_y, parts_z = (lax.axis_size(a) for a in AXES)
    place_x = lax.axis_index("gx").astype(jnp.int32).reshape(1)
    odd_y, odd_z = ((lax.axis_index(a) % 2).astype(jnp.int32).reshape(1) for a in AXES[1:])
    count = live_blocks.reshape(1)
    bold = bold_data.reshape(size_x * plane, frames)
    voxel_maps = jnp.transpose(spatial_maps, (1, 2, 3, 0)).reshape(size_x, plane, chans)
    all_cells = float(chans * size_x * plane * parts_x * parts_y * parts_z)

    win_x, win_y, win_z = (inner_window(s) for s in (size_x, size_y, size_z))
    unit_z = np.eye(size_z)
    ends = np.concatenate([np.kron(win_y.T, unit_z[:, :RADIUS]), np.kron(win_y.T, unit_z[:, -RADIUS:])], 1)
    table_ends = jnp.asarray(half(ends))
    table_own = jnp.asarray(half(np.kron(win_y.T, win_z[:, RADIUS:-RADIUS].T)))
    unit_y = np.eye(size_y)
    table_z = jnp.asarray(
        half(np.concatenate([np.kron(unit_y, win_z[:, :RADIUS].T), np.kron(unit_y, win_z[:, -RADIUS:].T)]))
    )
    face_y, face_z = RADIUS * size_z, RADIUS * size_y

    reach = 2 * RADIUS
    twice = parts_x == 2 and size_y == reach and size_z == 2 * reach
    pair_x = parts_x == 2
    full_x = band(size_x * parts_x)
    own_x = [slice(p * size_x, (p + 1) * size_x) for p in range(parts_x)]

    def coefs_x(matrices):
        mine = [[[m[own_x[p], own_x[p]]] for m in matrices] for p in range(2)]
        other = [[[m[own_x[p], own_x[1 - p]]] for m in matrices] for p in range(2)]
        return mine, other

    def along_x(block, matrices):
        if pair_x:
            mine, other = coefs_x(matrices)
            got = lax.ppermute(block, "gx", [(0, 1), (1, 0)])
            sums = mix_layers(place_x, odd_y, mine, chans, [block], [], [F32] * len(matrices))
            return mix_layers(
                place_x, odd_y, other, chans, [got], list(sums), [BF16] * len(matrices), face=face_y
            )
        depth = RADIUS * chans
        before, after = shifted(block[:depth], block[-depth:], "gx")
        rest = jnp.zeros((block.shape[0] - depth, plane), BF16)
        before, after = jnp.concatenate([rest, before]), jnp.concatenate([after, rest])
        tables = []
        for lo in (-size_x, 0, size_x):
            columns = np.arange(size_x) + lo + RADIUS
            inside = (columns >= 0) & (columns < win_x.shape[1])
            tables.append(np.where(inside[None], win_x[:, np.clip(columns, 0, win_x.shape[1] - 1)], 0.0))
        return mix_layers(
            place_x, odd_y, [[tables]], chans, [before, block, after], [], [BF16], face=face_y
        )

    def along_rest(field, first, second):
        first, second = swapped(first, second, "gy")
        ends = filter_faces(odd_y, odd_z, first, field, second, table_ends, "filter_faces")
        ends = swapped(*ends, "gz")
        return filter_lanes(odd_y, first, field, second, table_own, "filter_lanes"), *ends

    def all_courses(acc, first, middle, second, table):
        return hypercube_sum(
            courses_of(count, odd_z, acc, first, middle, second, table, bold, chans, size_y, size_z),
            narrow=True,
        )

    plain = pack_maps(voxel_maps, size_x, chans, plane)
    acc, first, second = along_rest(*along_x(plain, [full_x]))
    courses1 = all_courses(acc, first, [], second, table_z)
    half1 = courses1.astype(BF16)
    raw1 = raw_gradient(count, half1, bold, size_y, size_z)
    if twice:
        once_x, twice_x, *faces1 = along_x(raw1, [full_x, full_x @ full_x])
        square_y = windows(np.linalg.matrix_power(band(size_y * parts_y), 2), size_y, parts_y, reach)
        square_z = windows(np.linalg.matrix_power(band(size_z * parts_z), 2), size_z, parts_z, reach)
        ordered = np.concatenate([unit_z[:, :reach], unit_z[:, reach:]], 1).reshape(size_z, 2, reach)
        tables_y = np.stack([
            np.concatenate([np.kron(w.T, ordered[:, h]) for h in range(2)], 1) for w in square_y
        ])
        tables_z = np.stack([
            np.concatenate([np.kron(unit_y, w[:, h * reach : (h + 1) * reach].T) for h in range(4)])
            for w in square_z
        ])
        table_y2 = lax.dynamic_index_in_dim(jnp.asarray(half(tables_y)), lax.axis_index("gy"), 0, False)
        table_z2 = lax.dynamic_index_in_dim(jnp.asarray(half(tables_z)), lax.axis_index("gz"), 0, False)
        first, second = swapped(twice_x, twice_x, "gy")
        to_first, to_second = filter_faces(odd_y, odd_z, first, twice_x, second, table_y2, "filter_y2")
        first, second = swapped(to_first, to_second, "gz")
        even = odd_z[0] == 0
        between = [jnp.where(even, to_second, to_first), jnp.where(even, to_first, to_second)]
        change = all_courses(None, first, between, second, table_z2)
        grad1, _ = gradient_of(odd_z, *along_rest(once_x, *faces1), table_z, chans)
    else:
        grad1, _ = gradient_of(odd_z, *along_rest(*along_x(raw1, [full_x])), table_z, chans)
        again = pack_maps(grad1, size_x, chans, plane)
        acc2, first, second = along_rest(*along_x(again, [full_x]))
        change = all_courses(acc2, first, [], second, table_z)

    def gram_of(courses):
        gram = jnp.dot(courses, courses.T, precision=lax.Precision.HIGHEST)
        return 0.5 * (float(chans) / jnp.trace(gram)) * gram

    unit = jnp.eye(chans, dtype=F32)
    gram1 = gram_of(courses1)
    energy1 = jnp.maximum(jnp.sum(half1.astype(F32) * change), 0.0) / all_cells
    scale1 = 0.5 / jnp.sqrt(energy1 + 1e-06)
    kept = courses1 - jnp.dot(gram1, courses1, precision=lax.Precision.HIGHEST)

    courses2 = kept + scale1 * change
    half2 = courses2.astype(BF16)
    raw2 = raw_gradient(count, half2, bold, size_y, size_z)
    grad2, squares = gradient_of(odd_z, *along_rest(*along_x(raw2, [full_x])), table_z, chans)
    energy2 = scattered_sum(squares) / all_cells
    scale2 = (0.5 / jnp.sqrt(energy2 + 1e-06)).reshape(1)

    fade2 = unit - gram_of(courses2)
    fades = jnp.dot(fade2, unit - gram1, precision=lax.Precision.HIGHEST)
    base = base_maps(voxel_maps, grad1, fades, scale1 * fade2)
    maps = final_maps(scale2, base, grad2).reshape(size_x, size_y, size_z, chans)
    return (jnp.transpose(maps, (3, 0, 1, 2)), half2)


def solution(mesh):
    return jax.shard_map(
        per_device,
        mesh=mesh,
        in_specs=(P("gx", "gy", "gz", None), P(None, "gx", "gy", "gz"), P("gx", "gy", "gz")),
        out_specs=(P(None, "gx", "gy", "gz"), P()),
        check_vma=False,
    )
```

```python
import functools
import math

import jax
import jax.numpy as jnp
import ml_dtypes
import numpy as np
from jax import lax
from jax.experimental import pallas as pl
from jax.experimental.pallas import tpu as pltpu
from jax.sharding import PartitionSpec as P

RADIUS = 8
F32 = jnp.float32
BF16 = jnp.bfloat16
AXES = ("gx", "gy", "gz")


def band(length):
    total = sum(math.exp(-float(d * d) / 32.0) for d in range(-RADIUS, RADIUS + 1))
    gap = np.abs(np.arange(length)[:, None] - np.arange(length)[None, :])
    return np.where(gap <= RADIUS, np.exp(-(gap.astype(np.float64) ** 2) / 32.0) / total, 0.0)


def windows(matrix, size, parts, reach):
    padded = np.pad(matrix, ((0, 0), (reach, reach)))
    return np.stack(
        [padded[p * size : (p + 1) * size, p * size : (p + 1) * size + 2 * reach] for p in range(parts)]
    )


def half(array):
    return np.asarray(array, dtype=ml_dtypes.bfloat16)


def inner_window(size):
    return windows(band(3 * size), size, 3, RADIUS)[1]


PLACE_X, PLACE_Y, PLACE_Z, ODD_Y, ODD_Z, COUNT = range(6)
NT = (((1,), (1,)), ((), ()))
FULL = lax.Precision.HIGHEST


def shape(dims, kind):
    return jax.ShapeDtypeStruct(dims, kind)


def call(body, shapes, info, arrays, flops=10**8, name=None, spaces=None, scratch=()):
    total = sum(a.size * a.dtype.itemsize for a in arrays)
    whole = pl.BlockSpec(memory_space=pltpu.VMEM)
    return pl.pallas_call(
        body,
        out_shape=shapes,
        in_specs=[pl.BlockSpec(memory_space=pltpu.SMEM)] + [spaces or whole] * len(arrays),
        out_specs=jax.tree.map(lambda _: whole, shapes),
        scratch_shapes=scratch,
        compiler_params=pltpu.CompilerParams(vmem_limit_bytes=16 * 1024 * 1024),
        cost_estimate=pl.CostEstimate(flops=flops, bytes_accessed=total, transcendentals=0),
        name=name,
    )(info, *arrays)


def dot(a, b):
    return jnp.dot(a, b, preferred_element_type=F32)


def dot_nt(a, b, precision=None):
    return lax.dot_general(a, b, NT, precision=precision, preferred_element_type=F32)


def unit_of(size):
    return (
        lax.broadcasted_iota(jnp.int32, (size, size), 0) == lax.broadcasted_iota(jnp.int32, (size, size), 1)
    ).astype(F32)


def total_of(value):
    return jnp.sum(jnp.sum(value, axis=1, keepdims=True), axis=0, keepdims=True)


def pack_maps(info, voxel_maps):
    layers, plane, chans = voxel_maps.shape

    def body(_, src, out):
        unit = unit_of(chans).astype(BF16)
        for x in range(layers):
            out[x * chans : (x + 1) * chans, :] = dot_nt(unit, src[x].astype(BF16)).astype(BF16)

    return call(body, shape((layers * chans, plane), BF16), info, [voxel_maps], name="pack_maps")


def pick_tables(info, table_y, table_z):
    def body(info_ref, all_y, all_z, out_y, out_z, sem_y, sem_z):
        copies = [
            pltpu.make_async_copy(all_y.at[info_ref[PLACE_Y]], out_y, sem_y),
            pltpu.make_async_copy(all_z.at[info_ref[PLACE_Z]], out_z, sem_z),
        ]
        for copy in copies:
            copy.start()
        for copy in copies:
            copy.wait()

    shapes = (shape(table_y.shape[1:], BF16), shape(table_z.shape[1:], BF16))
    return call(
        body,
        shapes,
        info,
        [table_y, table_z],
        name="pick_tables",
        spaces=pl.BlockSpec(memory_space=pl.ANY),
        scratch=(pltpu.SemaphoreType.DMA, pltpu.SemaphoreType.DMA),
    )


def send_faces(info_ref, odd, field, face, first, second):
    plane = field.shape[1]

    def write(low, high):
        low[...] = field[:, :face].astype(low.dtype)
        high[...] = field[:, plane - face :].astype(high.dtype)

    pl.when(info_ref[odd] == 0)(lambda: write(second, first))
    pl.when(info_ref[odd] != 0)(lambda: write(first, second))


def swapped_dot(info_ref, odd, first, middle, second, weights, rows=slice(None), sent=False):
    width = first.shape[1]
    end = weights.shape[0] - width
    even = info_ref[odd] == 0

    def at(when_even, when_odd):
        return weights[pl.ds(pl.multiple_of(jnp.where(even, when_even, when_odd), width), width), :]

    total = dot(first[rows, :], at(end, 0)) + dot(second[rows, :], at(0, end))
    if sent:
        high = end - width
        return total + dot(middle[0][rows, :], at(high, width)) + dot(middle[1][rows, :], at(width, high))
    for piece in middle:
        total = total + dot(piece[rows, :], weights[width : width + piece.shape[1], :])
    return total


def mix_layers(info, coefs, chans, sources, sums, out_types, face=0):
    rows, plane = sources[0].shape
    outs = len(out_types)
    base = len(sources)
    tall, wide = 16, 128

    def body(info_ref, *refs):
        ins, adds, results = refs[:base], refs[base : base + len(sums)], refs[base + len(sums) :]

        def run(tables):
            layers = tables[0][0].shape[0]
            for r in range(0, chans, tall):
                for c in range(0, plane, wide):
                    tiles = [
                        [
                            src[s * chans + r : s * chans + r + tall, c : c + wide].astype(F32)
                            for s in range(layers)
                        ]
                        for src in ins
                    ]
                    for o in range(outs):
                        for x in range(layers):
                            at = slice(x * chans + r, x * chans + r + tall)
                            total = adds[o][at, c : c + wide] if adds else None
                            for tile, table in zip(tiles, tables[o]):
                                for s in range(layers):
                                    weight = float(table[x, s])
                                    if weight != 0.0:
                                        term = tile[s] * weight
                                        total = term if total is None else total + term
                            if total is None:
                                total = jnp.zeros((tall, wide), F32)
                            results[o][at, c : c + wide] = total.astype(results[o].dtype)

        if len(coefs) == 1:
            run(coefs[0])
        else:
            for v in range(len(coefs)):
                pl.when(info_ref[PLACE_X] == v)(functools.partial(run, coefs[v]))
        if face:
            send_faces(info_ref, ODD_Y, results[0], face, *results[outs:])

    shapes = tuple(shape((rows, plane), t) for t in out_types)
    if face:
        shapes += (shape((rows, face), out_types[0]),) * 2
    return call(body, shapes, info, [*sources, *sums], name="mix_layers")


def filter_lanes(info, first, middle, second, table):
    def body(info_ref, first_ref, middle_ref, second_ref, weights, out):
        out[...] = swapped_dot(info_ref, ODD_Y, first_ref, [middle_ref], second_ref, weights)

    shapes = shape((first.shape[0], table.shape[1]), F32)
    return call(body, shapes, info, [first, middle, second, table], name="filter_lanes")


def filter_faces(info, first, middle, second, table, below=()):
    rows, face = first.shape[0], table.shape[1] // 2
    extra = below[0].shape[0] if below else 0

    def body(info_ref, first_ref, middle_ref, second_ref, weights, *refs):
        outs = refs[-2:]
        total = swapped_dot(info_ref, ODD_Y, first_ref, [middle_ref], second_ref, weights)
        send_faces(info_ref, ODD_Z, total, face, *(out.at[:rows, :] for out in outs))
        for src, out in zip(refs[:-2], outs):
            out[rows:, :] = src[...]

    shapes = (shape((rows + extra, face), BF16),) * 2
    return call(body, shapes, info, [first, middle, second, table, *below], name="filter_faces")


def live_lanes(info_ref, layer, dims, size_y, size_z):
    row = layer * size_y + lax.broadcasted_iota(jnp.int32, dims, 1) // size_z
    return row < info_ref[COUNT]


def spread_rows(chans, frames, peers):
    rows = chans * frames // (peers * 128)
    return rows if rows and rows * peers * 128 == chans * frames and chans % rows == 0 else 0


def courses_of(info, acc, first, middle, second, table, bold, chans, size_y, size_z, peers):
    frames = bold.shape[1]
    plane = size_y * size_z
    layers = bold.shape[0] // plane
    between = len(middle)
    part = spread_rows(chans, frames, peers)

    def body(info_ref, first_ref, *refs):
        ins, second_ref, weights, frames_ref = refs[:between], *refs[between : between + 3]
        out = refs[-1]
        total = jnp.zeros((chans, frames), F32)
        for x in range(layers):
            rows = slice(x * chans, (x + 1) * chans)
            value = swapped_dot(info_ref, ODD_Z, first_ref, ins, second_ref, weights, rows, sent=between == 2)
            if acc is not None:
                value = value + refs[between + 3][rows, :]
            keep = live_lanes(info_ref, x, value.shape, size_y, size_z)
            value = jnp.where(keep, value, 0.0).astype(BF16)
            total = total + dot(value, frames_ref[x * plane : (x + 1) * plane, :])
        if not part:
            out[...] = total
            return
        across = frames // 128
        for d in range(peers):
            r, c = d // across * part, d % across * 128
            out[d] = total[r : r + part, c : c + 128].astype(BF16)

    arrays = [first, *middle, second, table, bold] + ([acc] if acc is not None else [])
    shapes = shape((peers, part, 128), BF16) if part else shape((chans, frames), F32)
    return call(body, shapes, info, arrays, flops=10**9, name="courses_of")


def sum_parts(info, parts):
    peers = parts.shape[0]

    def body(_, src, out):
        total = src[0].astype(F32)
        for d in range(1, peers):
            total = total + src[d].astype(F32)
        total = total.astype(BF16)
        for d in range(peers):
            out[d] = total

    return call(body, shape(parts.shape, BF16), info, [parts], name="sum_parts")


def whole_courses(src, chans, frames):
    if len(src.shape) == 2:
        return src[...].astype(F32)
    across = frames // 128
    down = src.shape[0] // across
    return jnp.concatenate(
        [
            jnp.concatenate([src[r * across + c].astype(F32) for c in range(across)], axis=1)
            for r in range(down)
        ],
        axis=0,
    )


def write_gradient(info_ref, courses, frames_ref, out, chans, size_y, size_z):
    plane = size_y * size_z
    for x in range(frames_ref.shape[0] // plane):
        value = dot_nt(courses, frames_ref[x * plane : (x + 1) * plane, :])
        keep = live_lanes(info_ref, x, value.shape, size_y, size_z)
        out[x * chans : (x + 1) * chans, :] = jnp.where(keep, value, 0.0).astype(BF16)


def first_gradient(info, parts, bold, chans, size_y, size_z):
    cells, frames = bold.shape

    def body(info_ref, parts_ref, frames_ref, out, half_ref):
        courses = whole_courses(parts_ref, chans, frames).astype(BF16)
        half_ref[...] = courses
        write_gradient(info_ref, courses, frames_ref, out, chans, size_y, size_z)

    shapes = (shape((cells * chans // (size_y * size_z), size_y * size_z), BF16), shape((chans, frames), BF16))
    return call(body, shapes, info, [parts, bold], flops=10**9, name="first_gradient")


def fade_of(courses):
    chans = courses.shape[0]
    wide = courses.astype(F32)
    scale = (0.5 * chans) / total_of(wide * wide)
    return unit_of(chans) - dot_nt(courses, courses) * scale


def first_fade(info, half1):
    chans, frames = half1.shape

    def body(_, half_ref, kept_ref, fade_ref):
        fade = fade_of(half_ref[...])
        fade_ref[...] = fade
        kept_ref[...] = jnp.dot(fade, half_ref[...].astype(F32), precision=FULL, preferred_element_type=F32)

    shapes = (shape((chans, frames), F32), shape((chans, chans), F32))
    return call(body, shapes, info, [half1], name="first_fade")


def second_gradient(info, parts, half1, kept, bold, chans, size_y, size_z, all_cells):
    cells, frames = bold.shape

    def body(info_ref, parts_ref, half1_ref, kept_ref, frames_ref, out, half_ref, scale_ref):
        change = whole_courses(parts_ref, chans, frames)
        energy = jnp.maximum(total_of(half1_ref[...].astype(F32) * change), 0.0) * (1.0 / all_cells)
        scale = 0.5 * lax.rsqrt(energy + 1e-06)
        scale_ref[...] = scale
        courses = (kept_ref[...] + scale * change).astype(BF16)
        half_ref[...] = courses
        write_gradient(info_ref, courses, frames_ref, out, chans, size_y, size_z)

    shapes = (
        shape((cells * chans // (size_y * size_z), size_y * size_z), BF16),
        shape((chans, frames), BF16),
        shape((1, 1), F32),
    )
    return call(body, shapes, info, [parts, half1, kept, bold], flops=10**9, name="second_gradient")


def second_fade(info, half2, fade1, scale1, field, face):
    chans = half2.shape[0]
    rows, plane = field.shape

    def body(info_ref, half_ref, fade_ref, scale_ref, field_ref, fades_ref, out, first, second):
        fade = fade_of(half_ref[...])
        fades_ref[...] = jnp.dot(fade, fade_ref[...], precision=FULL, preferred_element_type=F32)
        weights = fade * scale_ref[...]
        high = weights.astype(BF16)
        low = (weights - high.astype(F32)).astype(BF16)
        for x in range(rows // chans):
            at = slice(x * chans, (x + 1) * chans)
            block = field_ref[at, :]
            out[at, :] = (dot(high, block) + dot(low, block)).astype(BF16)
        send_faces(info_ref, ODD_Y, out, face, first, second)

    shapes = (
        shape((chans, chans), F32),
        shape((rows, plane), BF16),
        shape((rows, face), BF16),
        shape((rows, face), BF16),
    )
    return call(body, shapes, info, [half2, fade1, scale1, field], flops=10**9, name="second_fade")


def faded_maps(info, voxel_maps, fades):
    layers, plane, chans = voxel_maps.shape

    def body(_, maps_ref, fades_ref, out):
        for x in range(layers):
            out[x] = dot_nt(maps_ref[x], fades_ref[...], FULL)

    return call(
        body, shape((layers, plane, chans), F32), info, [voxel_maps, fades], flops=10**9, name="faded_maps"
    )


def whole_gradient(info, acc, first, second, table):
    def body(info_ref, start, first_ref, second_ref, weights, out):
        value = start[...] + swapped_dot(info_ref, ODD_Z, first_ref, [], second_ref, weights)
        out[...] = value.astype(BF16)

    return call(body, shape(acc.shape, BF16), info, [acc, first, second, table], name="whole_gradient")


def gradient_energy(info, acc, first, second, table, peers):
    rows, plane = acc.shape
    tall = min(rows, 128)

    def body(info_ref, start, first_ref, second_ref, weights, out, energy):
        total = jnp.zeros((tall, plane), F32)
        for r in range(0, rows, tall):
            at = slice(r, r + tall)
            value = start[at, :] + swapped_dot(info_ref, ODD_Z, first_ref, [], second_ref, weights, at)
            total = total + value * value
            out[at, :] = value
        energy[...] = jnp.broadcast_to(total_of(total).reshape(1, 1, 1), energy.shape)

    shapes = (shape((rows, plane), F32), shape((peers, 1, 128), F32))
    return call(body, shapes, info, [acc, first, second, table], name="gradient_energy")


def turned_gradients(info, acc, first, second, table, base, grad):
    layers, plane, chans = base.shape
    rows = acc.shape[0]

    def body(info_ref, start, first_ref, second_ref, weights, base_ref, grad_ref, out, turned):
        for x in range(layers):
            at = slice(x * chans, (x + 1) * chans)
            below = slice(rows + x * chans, rows + (x + 1) * chans)
            value = start[at, :] + swapped_dot(info_ref, ODD_Z, first_ref, [], second_ref, weights, below)
            out[x] = base_ref[x] + value.T
            turned[x] = grad_ref[at, :].T

    shapes = (shape(base.shape, F32),) * 2
    return call(body, shapes, info, [acc, first, second, table, base, grad], name="turned_gradients")


def final_maps(info, energies, base, grad, all_cells):
    layers, plane, chans = base.shape
    peers = energies.shape[0]

    def body(_, energies_ref, base_ref, grad_ref, out):
        energy = energies_ref[0]
        for d in range(1, peers):
            energy = energy + energies_ref[d]
        scale = 0.5 * lax.rsqrt(energy[:, :1] * (1.0 / all_cells) + 1e-06)
        for x in range(layers):
            out[x] = base_ref[x] + scale * grad_ref[x]

    return call(body, shape(base.shape, F32), info, [energies, base, grad], name="final_maps")


def swapped(first, second, axis, inner_first=False):
    peers = lax.axis_size(axis)
    got = {}
    for start in (1, 0) if inner_first else (0, 1):
        pairs = [(i, i + 1) for i in range(start, peers - 1, 2)]
        pairs += [(j, i) for i, j in pairs]
        got[start] = lax.ppermute((first, second)[start], axis, pairs)
    return got[0], got[1]


def shifted(lower, upper, axis):
    peers = lax.axis_size(axis)
    up = [(i, i + 1) for i in range(peers - 1)]
    down = [(j, i) for i, j in up]
    return lax.ppermute(upper, axis, up), lax.ppermute(lower, axis, down)


def exchanged(parts):
    return lax.all_to_all(parts, AXES, 0, 0, tiled=True)


def per_device(bold_data, spatial_maps, live_blocks):
    chans, size_x, size_y, size_z = spatial_maps.shape
    frames = bold_data.shape[3]
    plane = size_y * size_z
    parts_x, parts_y, parts_z = (lax.axis_size(a) for a in AXES)
    peers = parts_x * parts_y * parts_z
    places = [lax.axis_index(a).astype(jnp.int32) for a in AXES]
    info = jnp.stack([*places, places[1] % 2, places[2] % 2, live_blocks[0, 0, 0]])
    bold = bold_data.reshape(size_x * plane, frames)
    voxel_maps = jnp.transpose(spatial_maps, (1, 2, 3, 0)).reshape(size_x, plane, chans)
    all_cells = float(chans * size_x * plane * peers)

    win_x, win_y, win_z = (inner_window(s) for s in (size_x, size_y, size_z))
    unit_y, unit_z = np.eye(size_y), np.eye(size_z)
    ends = np.concatenate([np.kron(win_y.T, unit_z[:, :RADIUS]), np.kron(win_y.T, unit_z[:, -RADIUS:])], 1)
    table_ends = jnp.asarray(half(ends))
    table_own = jnp.asarray(half(np.kron(win_y.T, win_z[:, RADIUS:-RADIUS].T)))
    table_z = jnp.asarray(
        half(np.concatenate([np.kron(unit_y, win_z[:, :RADIUS].T), np.kron(unit_y, win_z[:, -RADIUS:].T)]))
    )
    face_y = RADIUS * size_z

    reach = 2 * RADIUS
    twice = parts_x == 2 and size_y == reach and size_z == 2 * reach
    full_x = band(size_x * parts_x)
    own_x = [slice(p * size_x, (p + 1) * size_x) for p in range(parts_x)]

    def along_x(block, matrices):
        kinds = [BF16] * len(matrices)
        if parts_x == 2:
            mine = [[[m[own_x[p], own_x[p]]] for m in matrices] for p in range(2)]
            other = [[[m[own_x[p], own_x[1 - p]]] for m in matrices] for p in range(2)]
            got = lax.ppermute(block, "gx", [(0, 1), (1, 0)])
            sums = mix_layers(info, mine, chans, [block], [], [F32] * len(matrices))
            return mix_layers(info, other, chans, [got], list(sums), kinds, face=face_y)
        depth = RADIUS * chans
        before, after = shifted(block[:depth], block[-depth:], "gx")
        rest = jnp.zeros((block.shape[0] - depth, plane), BF16)
        before, after = jnp.concatenate([rest, before]), jnp.concatenate([after, rest])
        tables = []
        for lo in (-size_x, 0, size_x):
            columns = np.arange(size_x) + lo + RADIUS
            inside = (columns >= 0) & (columns < win_x.shape[1])
            tables.append(np.where(inside[None], win_x[:, np.clip(columns, 0, win_x.shape[1] - 1)], 0.0))
        return mix_layers(info, [[tables]], chans, [before, block, after], [], kinds, face=face_y)

    def along_y(first, second):
        return swapped(first, second, "gy", inner_first=True)

    def along_rest(field, first, second):
        first, second = along_y(first, second)
        ends = swapped(*filter_faces(info, first, field, second, table_ends), "gz")
        return filter_lanes(info, first, field, second, table_own), *ends

    def all_courses(acc, first, middle, second, table):
        parts = courses_of(info, acc, first, middle, second, table, bold, chans, size_y, size_z, peers)
        if not spread_rows(chans, frames, peers):
            return lax.psum(parts, AXES)
        return exchanged(sum_parts(info, exchanged(parts)))

    plain = pack_maps(info, voxel_maps)
    acc, first, second = along_rest(*along_x(plain, [full_x]))
    parts1 = all_courses(acc, first, [], second, table_z)
    raw1, half1 = first_gradient(info, parts1, bold, chans, size_y, size_z)
    if twice:
        square_y = windows(np.linalg.matrix_power(band(size_y * parts_y), 2), size_y, parts_y, reach)
        square_z = windows(np.linalg.matrix_power(band(size_z * parts_z), 2), size_z, parts_z, reach)
        ordered = np.concatenate([unit_z[:, :reach], unit_z[:, reach:]], 1).reshape(size_z, 2, reach)
        tables_y = np.stack([
            np.concatenate([np.kron(w.T, ordered[:, h]) for h in range(2)], 1) for w in square_y
        ])
        tables_z = np.stack([
            np.concatenate([np.kron(unit_y, w[:, h * reach : (h + 1) * reach].T) for h in range(4)])
            for w in square_z
        ])
        table_y2, table_z2 = pick_tables(info, jnp.asarray(half(tables_y)), jnp.asarray(half(tables_z)))
        twice_x, once_x, *_ = along_x(raw1, [full_x @ full_x, full_x])
        first, second = along_y(twice_x, twice_x)
        sent = filter_faces(info, first, twice_x, second, table_y2)
        first, second = swapped(*sent, "gz")
        parts2 = all_courses(None, first, list(sent), second, table_z2)
    else:
        once_x, *faces1 = along_x(raw1, [full_x])
        again = whole_gradient(info, *along_rest(once_x, *faces1), table_z)
        acc2, first, second = along_rest(*along_x(again, [full_x]))
        parts2 = all_courses(acc2, first, [], second, table_z)

    kept, fade1 = first_fade(info, half1)
    raw2, half2, scale1 = second_gradient(
        info, parts2, half1, kept, bold, chans, size_y, size_z, all_cells
    )
    fades, field1, *faces1 = second_fade(info, half2, fade1, scale1, once_x, face_y)
    first1, second1 = along_y(*faces1)
    below = filter_faces(info, first1, field1, second1, table_ends)
    acc1 = filter_lanes(info, first1, field1, second1, table_own)
    base = faded_maps(info, voxel_maps, fades)

    field2, *faces2 = along_x(raw2, [full_x])
    first2, second2 = along_y(*faces2)
    ends = swapped(*filter_faces(info, first2, field2, second2, table_ends, below), "gz")
    acc2 = filter_lanes(info, first2, field2, second2, table_own)
    grad2, energies = gradient_energy(info, acc2, *ends, table_z, peers)
    energies = exchanged(energies)
    base, grad2 = turned_gradients(info, acc1, *ends, table_z, base, grad2)
    maps = final_maps(info, energies, base, grad2, all_cells).reshape(size_x, size_y, size_z, chans)
    return (jnp.transpose(maps, (3, 0, 1, 2)), half2)


def solution(mesh):
    return jax.shard_map(
        per_device,
        mesh=mesh,
        in_specs=(P("gx", "gy", "gz", None), P(None, "gx", "gy", "gz"), P("gx", "gy", "gz")),
        out_specs=(P(None, "gx", "gy", "gz"), P()),
        check_vma=False,
    )
```

```python
import functools
import math

import jax
import jax.numpy as jnp
import ml_dtypes
import numpy as np
from jax import lax
from jax.experimental import pallas as pl
from jax.experimental.pallas import tpu as pltpu
from jax.sharding import PartitionSpec as P

RADIUS = 8
F32 = jnp.float32
BF16 = jnp.bfloat16
AXES = ("gx", "gy", "gz")


def band(length):
    total = sum(math.exp(-float(d * d) / 32.0) for d in range(-RADIUS, RADIUS + 1))
    gap = np.abs(np.arange(length)[:, None] - np.arange(length)[None, :])
    return np.where(gap <= RADIUS, np.exp(-(gap.astype(np.float64) ** 2) / 32.0) / total, 0.0)


def windows(matrix, size, parts, reach):
    padded = np.pad(matrix, ((0, 0), (reach, reach)))
    return np.stack(
        [padded[p * size : (p + 1) * size, p * size : (p + 1) * size + 2 * reach] for p in range(parts)]
    )


def half(array):
    return np.asarray(array, dtype=ml_dtypes.bfloat16)


def inner_window(size):
    return windows(band(3 * size), size, 3, RADIUS)[1]


PLACE_X, PLACE_Y, PLACE_Z, ODD_Y, ODD_Z, COUNT = range(6)
NT = (((1,), (1,)), ((), ()))
FULL = lax.Precision.HIGHEST


def shape(dims, kind):
    return jax.ShapeDtypeStruct(dims, kind)


def call(body, shapes, info, needs, arrays, flops=10**8, name=None, spaces=None, outs=None, scratch=(), after=()):
    total = sum(a.size * a.dtype.itemsize for a in arrays)
    whole, anywhere = pl.BlockSpec(memory_space=pltpu.VMEM), pl.BlockSpec(memory_space=pl.ANY)
    count, ends = len(needs), len(needs) + len(arrays)

    def wrapped(*refs):
        numbers = {need: ref for need, ref in zip(needs, refs)}
        body(Numbers(numbers), *refs[count:ends], *refs[ends + len(after) :])

    return pl.pallas_call(
        wrapped,
        out_shape=shapes,
        in_specs=[pl.BlockSpec(memory_space=pltpu.SMEM)] * count
        + [spaces or whole] * len(arrays)
        + [anywhere] * len(after),
        out_specs=jax.tree.map(lambda _: outs or whole, shapes),
        scratch_shapes=scratch,
        compiler_params=pltpu.CompilerParams(vmem_limit_bytes=16 * 1024 * 1024),
        cost_estimate=pl.CostEstimate(flops=flops, bytes_accessed=total, transcendentals=0),
        name=name,
    )(*(info[need] for need in needs), *arrays, *after)


class Numbers:
    def __init__(self, refs):
        self.refs = refs

    def __getitem__(self, need):
        return self.refs[need][0]


def dot(a, b):
    return jnp.dot(a, b, preferred_element_type=F32)


def dot_nt(a, b, precision=None):
    return lax.dot_general(a, b, NT, precision=precision, preferred_element_type=F32)


def unit_of(size):
    return (
        lax.broadcasted_iota(jnp.int32, (size, size), 0) == lax.broadcasted_iota(jnp.int32, (size, size), 1)
    ).astype(F32)


def total_of(value):
    return jnp.sum(jnp.sum(value, axis=1, keepdims=True), axis=0, keepdims=True)


def pack_maps(info, voxel_maps):
    layers, plane, chans = voxel_maps.shape

    def body(_, src, out):
        unit = unit_of(chans).astype(BF16)
        for x in range(layers):
            out[x * chans : (x + 1) * chans, :] = dot_nt(unit, src[x].astype(BF16)).astype(BF16)

    return call(body, shape((layers * chans, plane), BF16), info, [], [voxel_maps], name="pack_maps")


def pick_tables(info, table_y, table_z):
    def body(info_ref, all_y, all_z, out_y, out_z, sem_y, sem_z):
        copies = [
            pltpu.make_async_copy(all_y.at[info_ref[PLACE_Y]], out_y, sem_y),
            pltpu.make_async_copy(all_z.at[info_ref[PLACE_Z]], out_z, sem_z),
        ]
        for copy in copies:
            copy.start()
        for copy in copies:
            copy.wait()

    shapes = (shape(table_y.shape[1:], BF16), shape(table_z.shape[1:], BF16))
    return call(
        body,
        shapes,
        info,
        [PLACE_Y, PLACE_Z],
        [table_y, table_z],
        name="pick_tables",
        spaces=pl.BlockSpec(memory_space=pl.ANY),
        scratch=(pltpu.SemaphoreType.DMA, pltpu.SemaphoreType.DMA),
    )


def send_faces(info_ref, odd, field, face, first, second):
    plane = field.shape[1]

    def write(low, high):
        low[...] = field[:, :face].astype(low.dtype)
        high[...] = field[:, plane - face :].astype(high.dtype)

    pl.when(info_ref[odd] == 0)(lambda: write(second, first))
    pl.when(info_ref[odd] != 0)(lambda: write(first, second))


def swapped_dot(info_ref, odd, first, middle, second, weights, rows=slice(None), sent=False):
    width = first.shape[1]
    end = weights.shape[0] - width
    even = info_ref[odd] == 0

    def at(when_even, when_odd):
        return weights[pl.ds(pl.multiple_of(jnp.where(even, when_even, when_odd), width), width), :]

    total = dot(first[rows, :], at(end, 0)) + dot(second[rows, :], at(0, end))
    if sent:
        high = end - width
        return total + dot(middle[0][rows, :], at(high, width)) + dot(middle[1][rows, :], at(width, high))
    for piece in middle:
        total = total + dot(piece[rows, :], weights[width : width + piece.shape[1], :])
    return total


def mix_layers(info, coefs, chans, sources, sums, out_types, face=0, after=()):
    rows, plane = sources[0].shape
    outs = len(out_types)
    base = len(sources)
    tall, wide = 16, 128

    def body(info_ref, *refs):
        ins, adds, results = refs[:base], refs[base : base + len(sums)], refs[base + len(sums) :]

        def run(tables):
            layers = tables[0][0].shape[0]
            for r in range(0, chans, tall):
                for c in range(0, plane, wide):
                    tiles = [
                        [
                            src[s * chans + r : s * chans + r + tall, c : c + wide].astype(F32)
                            for s in range(layers)
                        ]
                        for src in ins
                    ]
                    for o in range(outs):
                        for x in range(layers):
                            at = slice(x * chans + r, x * chans + r + tall)
                            total = adds[o][at, c : c + wide] if adds else None
                            for tile, table in zip(tiles, tables[o]):
                                for s in range(layers):
                                    weight = float(table[x, s])
                                    if weight != 0.0:
                                        term = tile[s] * weight
                                        total = term if total is None else total + term
                            if total is None:
                                total = jnp.zeros((tall, wide), F32)
                            results[o][at, c : c + wide] = total.astype(results[o].dtype)

        if len(coefs) == 1:
            run(coefs[0])
        else:
            for v in range(len(coefs)):
                pl.when(info_ref[PLACE_X] == v)(functools.partial(run, coefs[v]))
        if face:
            send_faces(info_ref, ODD_Y, results[0], face, *results[outs:])

    shapes = tuple(shape((rows, plane), t) for t in out_types)
    if face:
        shapes += (shape((rows, face), out_types[0]),) * 2
    needs = ([PLACE_X] if len(coefs) > 1 else []) + ([ODD_Y] if face else [])
    return call(body, shapes, info, needs, [*sources, *sums], name="mix_layers", after=after)


def filter_lanes(info, first, middle, second, table):
    def body(info_ref, first_ref, middle_ref, second_ref, weights, out):
        out[...] = swapped_dot(info_ref, ODD_Y, first_ref, [middle_ref], second_ref, weights)

    shapes = shape((first.shape[0], table.shape[1]), F32)
    return call(body, shapes, info, [ODD_Y], [first, middle, second, table], name="filter_lanes")


def filter_faces(info, first, middle, second, table, below=(), after=()):
    rows, face = first.shape[0], table.shape[1] // 2
    extra = below[0].shape[0] if below else 0

    def body(info_ref, first_ref, middle_ref, second_ref, weights, *refs):
        outs = refs[-2:]
        total = swapped_dot(info_ref, ODD_Y, first_ref, [middle_ref], second_ref, weights)
        send_faces(info_ref, ODD_Z, total, face, *(out.at[:rows, :] for out in outs))
        for src, out in zip(refs[:-2], outs):
            out[rows:, :] = src[...]

    shapes = (shape((rows + extra, face), BF16),) * 2
    arrays = [first, middle, second, table, *below]
    return call(body, shapes, info, [ODD_Y, ODD_Z], arrays, name="filter_faces", after=after)


def live_lanes(info_ref, layer, dims, size_y, size_z):
    row = layer * size_y + lax.broadcasted_iota(jnp.int32, dims, 1) // size_z
    return row < info_ref[COUNT]


def courses_of(info, acc, first, middle, second, table, bold, chans, size_y, size_z):
    frames = bold.shape[1]
    plane = size_y * size_z
    layers = bold.shape[0] // plane
    between = len(middle)

    def body(info_ref, first_ref, *refs):
        ins, second_ref, weights, frames_ref = refs[:between], *refs[between : between + 3]
        total = jnp.zeros((chans, frames), F32)
        for x in range(layers):
            rows = slice(x * chans, (x + 1) * chans)
            value = swapped_dot(info_ref, ODD_Z, first_ref, ins, second_ref, weights, rows, sent=between == 2)
            if acc is not None:
                value = value + refs[between + 3][rows, :]
            keep = live_lanes(info_ref, x, value.shape, size_y, size_z)
            value = jnp.where(keep, value, 0.0).astype(BF16)
            total = total + dot(value, frames_ref[x * plane : (x + 1) * plane, :])
        refs[-1][...] = total

    arrays = [first, *middle, second, table, bold] + ([acc] if acc is not None else [])
    shapes = shape((chans, frames), F32)
    return call(body, shapes, info, [COUNT, ODD_Z], arrays, flops=10**9, name="courses_of")


def write_gradient(info_ref, courses, frames_ref, out, chans, size_y, size_z):
    plane = size_y * size_z
    for x in range(frames_ref.shape[0] // plane):
        value = dot_nt(courses, frames_ref[x * plane : (x + 1) * plane, :])
        keep = live_lanes(info_ref, x, value.shape, size_y, size_z)
        out[x * chans : (x + 1) * chans, :] = jnp.where(keep, value, 0.0).astype(BF16)


def first_gradient(info, sums, bold, chans, size_y, size_z):
    cells, frames = bold.shape

    def body(info_ref, sums_ref, frames_ref, out, half_ref):
        courses = sums_ref[...].astype(BF16)
        half_ref[...] = courses
        write_gradient(info_ref, courses, frames_ref, out, chans, size_y, size_z)

    shapes = (shape((cells * chans // (size_y * size_z), size_y * size_z), BF16), shape((chans, frames), BF16))
    return call(body, shapes, info, [COUNT], [sums, bold], flops=10**9, name="first_gradient")


def fade_of(courses):
    chans = courses.shape[0]
    wide = courses.astype(F32)
    scale = (0.5 * chans) / total_of(wide * wide)
    return unit_of(chans) - dot_nt(courses, courses) * scale


def first_fade(info, half1):
    chans, frames = half1.shape

    def body(_, half_ref, kept_ref, fade_ref):
        fade = fade_of(half_ref[...])
        fade_ref[...] = fade
        kept_ref[...] = jnp.dot(fade, half_ref[...].astype(F32), precision=FULL, preferred_element_type=F32)

    shapes = (shape((chans, frames), F32), shape((chans, chans), F32))
    return call(body, shapes, info, [], [half1], name="first_fade")


def second_gradient(info, change, half1, kept, bold, chans, size_y, size_z, all_cells):
    cells, frames = bold.shape

    def body(info_ref, change_ref, half1_ref, kept_ref, frames_ref, out, half_ref, scale_ref):
        change = change_ref[...]
        energy = jnp.maximum(total_of(half1_ref[...].astype(F32) * change), 0.0) * (1.0 / all_cells)
        scale = 0.5 * lax.rsqrt(energy + 1e-06)
        scale_ref[...] = scale
        courses = (kept_ref[...] + scale * change).astype(BF16)
        half_ref[...] = courses
        write_gradient(info_ref, courses, frames_ref, out, chans, size_y, size_z)

    shapes = (
        shape((cells * chans // (size_y * size_z), size_y * size_z), BF16),
        shape((chans, frames), BF16),
        shape((1, 1), F32),
    )
    arrays = [change, half1, kept, bold]
    return call(body, shapes, info, [COUNT], arrays, flops=10**9, name="second_gradient")


def second_fade(info, half2, fade1, scale1, field, face):
    chans = half2.shape[0]
    rows, plane = field.shape

    def body(info_ref, half_ref, fade_ref, scale_ref, field_ref, fades_ref, out, first, second):
        fade = fade_of(half_ref[...])
        fades_ref[...] = jnp.dot(fade, fade_ref[...], precision=FULL, preferred_element_type=F32)
        weights = fade * scale_ref[...]
        high = weights.astype(BF16)
        low = (weights - high.astype(F32)).astype(BF16)
        for x in range(rows // chans):
            at = slice(x * chans, (x + 1) * chans)
            block = field_ref[at, :]
            out[at, :] = (dot(high, block) + dot(low, block)).astype(BF16)
        send_faces(info_ref, ODD_Y, out, face, first, second)

    shapes = (
        shape((chans, chans), F32),
        shape((rows, plane), BF16),
        shape((rows, face), BF16),
        shape((rows, face), BF16),
    )
    arrays = [half2, fade1, scale1, field]
    return call(body, shapes, info, [ODD_Y], arrays, flops=10**9, name="second_fade")


def faded_maps(info, voxel_maps, fades):
    layers, plane, chans = voxel_maps.shape

    def body(_, maps_ref, fades_ref, out):
        for x in range(layers):
            out[x] = dot_nt(maps_ref[x], fades_ref[...], FULL)

    shapes = shape((layers, plane, chans), F32)
    return call(body, shapes, info, [], [voxel_maps, fades], flops=10**9, name="faded_maps")


def whole_gradient(info, acc, first, second, table):
    def body(info_ref, start, first_ref, second_ref, weights, out):
        value = start[...] + swapped_dot(info_ref, ODD_Z, first_ref, [], second_ref, weights)
        out[...] = value.astype(BF16)

    arrays = [acc, first, second, table]
    return call(body, shape(acc.shape, BF16), info, [ODD_Z], arrays, name="whole_gradient")


def gradient_energy(info, acc, first, second, table, peers, after=()):
    rows, plane = acc.shape
    tall = min(rows, 128)

    def body(info_ref, start, first_ref, second_ref, weights, out, energy):
        total = jnp.zeros((tall, plane), F32)
        for r in range(0, rows, tall):
            at = slice(r, r + tall)
            value = start[at, :] + swapped_dot(info_ref, ODD_Z, first_ref, [], second_ref, weights, at)
            total = total + value * value
            out[at, :] = value
        energy[...] = jnp.broadcast_to(total_of(total).reshape(1, 1, 1), energy.shape)

    shapes = (shape((rows, plane), F32), shape((peers, 1, 128), F32))
    arrays = [acc, first, second, table]
    return call(body, shapes, info, [ODD_Z], arrays, name="gradient_energy", after=after)


def final_maps(info, energies, base, acc, first, second, table, grad, all_cells):
    layers, plane, chans = base.shape
    rows = acc.shape[0]
    peers = energies.shape[0]

    def body(info_ref, energies_ref, base_ref, start, first_ref, second_ref, weights, grad_ref, out, held, sems):
        energy = energies_ref[0]
        for d in range(1, peers):
            energy = energy + energies_ref[d]
        scale = 0.5 * lax.rsqrt(energy[:, :1] * (1.0 / all_cells) + 1e-06)
        copies = []
        for x in range(layers):
            at = slice(x * chans, (x + 1) * chans)
            below = slice(rows + x * chans, rows + (x + 1) * chans)
            value = start[at, :] + swapped_dot(info_ref, ODD_Z, first_ref, [], second_ref, weights, below)
            held[x] = base_ref[x] + (value + scale * grad_ref[at, :]).T
            copies.append(pltpu.make_async_copy(held.at[x], out.at[x], sems.at[x]))
            copies[-1].start()
        for copy in copies:
            copy.wait()

    return call(
        body,
        shape(base.shape, F32),
        info,
        [ODD_Z],
        [energies, base, acc, first, second, table, grad],
        name="final_maps",
        outs=pl.BlockSpec(memory_space=pl.ANY),
        scratch=(pltpu.VMEM(base.shape, F32), pltpu.SemaphoreType.DMA((layers,))),
    )


def swapped(first, second, axis, inner_first=False):
    peers = lax.axis_size(axis)
    got = {}
    for start in (1, 0) if inner_first else (0, 1):
        pairs = [(i, i + 1) for i in range(start, peers - 1, 2)]
        pairs += [(j, i) for i, j in pairs]
        got[start] = lax.ppermute((first, second)[start], axis, pairs)
    return got[0], got[1]


def shifted(lower, upper, axis):
    peers = lax.axis_size(axis)
    up = [(i, i + 1) for i in range(peers - 1)]
    down = [(j, i) for i, j in up]
    return lax.ppermute(upper, axis, up), lax.ppermute(lower, axis, down)


def exchanged(parts):
    return lax.all_to_all(parts, AXES, 0, 0, tiled=True)


def hypercube_sum(value):
    steps = []
    for axis in AXES:
        peers = lax.axis_size(axis)
        if peers & (peers - 1):
            return lax.psum(value, AXES)
        steps += [(axis, 1 << b) for b in range(peers.bit_length() - 1)]
    for axis, bit in steps:
        pairs = [(i, i ^ bit) for i in range(lax.axis_size(axis))]
        value = lax.reduce_precision(value, 8, 7)
        value = value + lax.ppermute(value.astype(BF16), axis, pairs).astype(F32)
    return value


def per_device(bold_data, spatial_maps, live_blocks):
    chans, size_x, size_y, size_z = spatial_maps.shape
    frames = bold_data.shape[3]
    plane = size_y * size_z
    parts_x, parts_y, parts_z = (lax.axis_size(a) for a in AXES)
    peers = parts_x * parts_y * parts_z
    places = [lax.axis_index(a).astype(jnp.int32) for a in AXES]
    numbers = [*places, places[1] % 2, places[2] % 2, live_blocks]
    info = [number.reshape(1) for number in numbers]
    bold = bold_data.reshape(size_x * plane, frames)
    voxel_maps = jnp.transpose(spatial_maps, (1, 2, 3, 0)).reshape(size_x, plane, chans)
    all_cells = float(chans * size_x * plane * peers)

    win_x, win_y, win_z = (inner_window(s) for s in (size_x, size_y, size_z))
    unit_y, unit_z = np.eye(size_y), np.eye(size_z)
    ends = np.concatenate([np.kron(win_y.T, unit_z[:, :RADIUS]), np.kron(win_y.T, unit_z[:, -RADIUS:])], 1)
    table_ends = jnp.asarray(half(ends))
    table_own = jnp.asarray(half(np.kron(win_y.T, win_z[:, RADIUS:-RADIUS].T)))
    table_z = jnp.asarray(
        half(np.concatenate([np.kron(unit_y, win_z[:, :RADIUS].T), np.kron(unit_y, win_z[:, -RADIUS:].T)]))
    )
    face_y = RADIUS * size_z

    reach = 2 * RADIUS
    twice = parts_x == 2 and size_y == reach and size_z == 2 * reach
    full_x = band(size_x * parts_x)
    own_x = [slice(p * size_x, (p + 1) * size_x) for p in range(parts_x)]

    def along_x(block, matrices, beside=()):
        kinds = [BF16] * len(matrices)
        if parts_x == 2:
            mine = [[[m[own_x[p], own_x[p]]] for m in matrices] for p in range(2)]
            other = [[[m[own_x[p], own_x[1 - p]]] for m in matrices] for p in range(2)]
            got = lax.ppermute(block, "gx", [(0, 1), (1, 0)])
            sums = mix_layers(info, mine, chans, [block], [], [F32] * len(matrices))
            return mix_layers(info, other, chans, [got], list(sums), kinds, face=face_y, after=beside)
        depth = RADIUS * chans
        before, after = shifted(block[:depth], block[-depth:], "gx")
        rest = jnp.zeros((block.shape[0] - depth, plane), BF16)
        before, after = jnp.concatenate([rest, before]), jnp.concatenate([after, rest])
        tables = []
        for lo in (-size_x, 0, size_x):
            columns = np.arange(size_x) + lo + RADIUS
            inside = (columns >= 0) & (columns < win_x.shape[1])
            tables.append(np.where(inside[None], win_x[:, np.clip(columns, 0, win_x.shape[1] - 1)], 0.0))
        return mix_layers(info, [[tables]], chans, [before, block, after], [], kinds, face=face_y)

    def along_y(first, second):
        return swapped(first, second, "gy", inner_first=True)

    def along_rest(field, first, second):
        first, second = along_y(first, second)
        ends = swapped(*filter_faces(info, first, field, second, table_ends), "gz")
        return filter_lanes(info, first, field, second, table_own), *ends

    def all_courses(acc, first, middle, second, table):
        return hypercube_sum(
            courses_of(info, acc, first, middle, second, table, bold, chans, size_y, size_z)
        )

    plain = pack_maps(info, voxel_maps)
    acc, first, second = along_rest(*along_x(plain, [full_x]))
    courses1 = all_courses(acc, first, [], second, table_z)
    raw1, half1 = first_gradient(info, courses1, bold, chans, size_y, size_z)
    kept, fade1 = first_fade(info, half1)
    if twice:
        square_y = windows(np.linalg.matrix_power(band(size_y * parts_y), 2), size_y, parts_y, reach)
        square_z = windows(np.linalg.matrix_power(band(size_z * parts_z), 2), size_z, parts_z, reach)
        ordered = np.concatenate([unit_z[:, :reach], unit_z[:, reach:]], 1).reshape(size_z, 2, reach)
        tables_y = np.stack([
            np.concatenate([np.kron(w.T, ordered[:, h]) for h in range(2)], 1) for w in square_y
        ])
        tables_z = np.stack([
            np.concatenate([np.kron(unit_y, w[:, h * reach : (h + 1) * reach].T) for h in range(4)])
            for w in square_z
        ])
        table_y2, table_z2 = pick_tables(info, jnp.asarray(half(tables_y)), jnp.asarray(half(tables_z)))
        twice_x, once_x, *_ = along_x(raw1, [full_x @ full_x, full_x], [kept])
        first, second = along_y(twice_x, twice_x)
        sent = filter_faces(info, first, twice_x, second, table_y2)
        first, second = swapped(*sent, "gz")
        change = all_courses(None, first, list(sent), second, table_z2)
    else:
        once_x, *faces1 = along_x(raw1, [full_x])
        again = whole_gradient(info, *along_rest(once_x, *faces1), table_z)
        acc2, first, second = along_rest(*along_x(again, [full_x]))
        change = all_courses(acc2, first, [], second, table_z)

    raw2, half2, scale1 = second_gradient(
        info, change, half1, kept, bold, chans, size_y, size_z, all_cells
    )
    fades, field1, *faces1 = second_fade(info, half2, fade1, scale1, once_x, face_y)
    first1, second1 = along_y(*faces1)
    below = filter_faces(info, first1, field1, second1, table_ends)
    acc1 = filter_lanes(info, first1, field1, second1, table_own)
    base = faded_maps(info, voxel_maps, fades)

    field2, *faces2 = along_x(raw2, [full_x], [base])
    first2, second2 = along_y(*faces2)
    ends = swapped(*filter_faces(info, first2, field2, second2, table_ends, below, [acc1]), "gz")
    acc2 = filter_lanes(info, first2, field2, second2, table_own)
    grad2, energies = gradient_energy(info, acc2, *ends, table_z, peers)
    maps = final_maps(info, exchanged(energies), base, acc1, *ends, table_z, grad2, all_cells)
    maps = maps.reshape(size_x, size_y, size_z, chans)
    return (jnp.transpose(maps, (3, 0, 1, 2)), half2)


def solution(mesh):
    return jax.shard_map(
        per_device,
        mesh=mesh,
        in_specs=(P("gx", "gy", "gz", None), P(None, "gx", "gy", "gz"), P("gx", "gy", "gz")),
        out_specs=(P(None, "gx", "gy", "gz"), P()),
        check_vma=False,
    )
```

```python
import functools
import math

import jax
import jax.numpy as jnp
import ml_dtypes
import numpy as np
from jax import lax
from jax.experimental import pallas as pl
from jax.experimental.pallas import tpu as pltpu
from jax.sharding import PartitionSpec as P

RADIUS = 8
F32 = jnp.float32
BF16 = jnp.bfloat16
AXES = ("gx", "gy", "gz")


def band(length):
    total = sum(math.exp(-float(d * d) / 32.0) for d in range(-RADIUS, RADIUS + 1))
    gap = np.abs(np.arange(length)[:, None] - np.arange(length)[None, :])
    return np.where(gap <= RADIUS, np.exp(-(gap.astype(np.float64) ** 2) / 32.0) / total, 0.0)


def windows(matrix, size, parts, reach):
    padded = np.pad(matrix, ((0, 0), (reach, reach)))
    return np.stack(
        [padded[p * size : (p + 1) * size, p * size : (p + 1) * size + 2 * reach] for p in range(parts)]
    )


def half(array):
    return np.asarray(array, dtype=ml_dtypes.bfloat16)


def inner_window(size):
    return windows(band(3 * size), size, 3, RADIUS)[1]


PLACE_X, PLACE_Y, PLACE_Z, ODD_Y, ODD_Z, COUNT = range(6)
NT = (((1,), (1,)), ((), ()))
FULL = lax.Precision.HIGHEST


def shape(dims, kind):
    return jax.ShapeDtypeStruct(dims, kind)


def call(body, shapes, info, needs, arrays, flops=10**8, name=None, spaces=None, outs=None, scratch=(), after=()):
    total = sum(a.size * a.dtype.itemsize for a in arrays)
    whole, anywhere = pl.BlockSpec(memory_space=pltpu.VMEM), pl.BlockSpec(memory_space=pl.ANY)
    count, ends = len(needs), len(needs) + len(arrays)

    def wrapped(*refs):
        numbers = {need: ref for need, ref in zip(needs, refs)}
        body(Numbers(numbers), *refs[count:ends], *refs[ends + len(after) :])

    return pl.pallas_call(
        wrapped,
        out_shape=shapes,
        in_specs=[pl.BlockSpec(memory_space=pltpu.SMEM)] * count
        + [spaces or whole] * len(arrays)
        + [anywhere] * len(after),
        out_specs=jax.tree.map(lambda _: outs or whole, shapes),
        scratch_shapes=scratch,
        compiler_params=pltpu.CompilerParams(vmem_limit_bytes=16 * 1024 * 1024),
        cost_estimate=pl.CostEstimate(flops=flops, bytes_accessed=total, transcendentals=0),
        name=name,
    )(*(info[need] for need in needs), *arrays, *after)


class Numbers:
    def __init__(self, refs):
        self.refs = refs

    def __getitem__(self, need):
        return self.refs[need][0]


def dot(a, b):
    return jnp.dot(a, b, preferred_element_type=F32)


def dot_nt(a, b, precision=None):
    return lax.dot_general(a, b, NT, precision=precision, preferred_element_type=F32)


def unit_of(size):
    return (
        lax.broadcasted_iota(jnp.int32, (size, size), 0) == lax.broadcasted_iota(jnp.int32, (size, size), 1)
    ).astype(F32)


def total_of(value):
    return jnp.sum(jnp.sum(value, axis=1, keepdims=True), axis=0, keepdims=True)


def pack_maps(info, voxel_maps):
    layers, plane, chans = voxel_maps.shape

    def body(_, src, out):
        unit = unit_of(chans).astype(BF16)
        for x in range(layers):
            out[x * chans : (x + 1) * chans, :] = dot_nt(unit, src[x].astype(BF16)).astype(BF16)

    return call(body, shape((layers * chans, plane), BF16), info, [], [voxel_maps], name="pack_maps")


def pick_tables(info, table_y, table_z):
    def body(info_ref, all_y, all_z, out_y, out_z, sem_y, sem_z):
        copies = [
            pltpu.make_async_copy(all_y.at[info_ref[PLACE_Y]], out_y, sem_y),
            pltpu.make_async_copy(all_z.at[info_ref[PLACE_Z]], out_z, sem_z),
        ]
        for copy in copies:
            copy.start()
        for copy in copies:
            copy.wait()

    shapes = (shape(table_y.shape[1:], BF16), shape(table_z.shape[1:], BF16))
    return call(
        body,
        shapes,
        info,
        [PLACE_Y, PLACE_Z],
        [table_y, table_z],
        name="pick_tables",
        spaces=pl.BlockSpec(memory_space=pl.ANY),
        scratch=(pltpu.SemaphoreType.DMA, pltpu.SemaphoreType.DMA),
    )


def send_faces(info_ref, odd, field, face, first, second):
    rows, plane = field.shape

    def write(target, lanes):
        for at, ref in zip((0, rows // 2), target) if isinstance(target, tuple) else [(0, target)]:
            ref[...] = field[at : at + ref.shape[0], lanes].astype(ref.dtype)

    low, high = slice(0, face), slice(plane - face, plane)

    @pl.when(info_ref[odd] == 0)
    def _():
        write(first, high)
        write(second, low)

    @pl.when(info_ref[odd] != 0)
    def _():
        write(first, low)
        write(second, high)


def swapped_dot(info_ref, odd, first, middle, second, weights, rows=slice(None), sent=False):
    width = first.shape[1]
    end = weights.shape[0] - width
    even = info_ref[odd] == 0

    def at(when_even, when_odd):
        return weights[pl.ds(pl.multiple_of(jnp.where(even, when_even, when_odd), width), width), :]

    total = dot(first[rows, :], at(end, 0))
    if isinstance(second, tuple):
        total = total + jnp.concatenate([dot(piece[...], at(0, end)) for piece in second], axis=0)
    else:
        total = total + dot(second[rows, :], at(0, end))
    if sent:
        high = end - width
        return total + dot(middle[0][rows, :], at(high, width)) + dot(middle[1][rows, :], at(width, high))
    for piece in middle:
        total = total + dot(piece[rows, :], weights[width : width + piece.shape[1], :])
    return total


def faces_shape(rows, face):
    return (shape((rows, face), BF16),) + (shape((rows // 2, face), BF16),) * 2


def mix_layers(info, coefs, chans, sources, sums, out_types, face=0, after=()):
    rows, plane = sources[0].shape
    outs = len(out_types)
    base = len(sources)
    tall, wide = 16, 128

    def body(info_ref, *refs):
        ins, adds, results = refs[:base], refs[base : base + len(sums)], refs[base + len(sums) :]

        def run(tables):
            layers = tables[0][0].shape[0]
            for r in range(0, chans, tall):
                for c in range(0, plane, wide):
                    tiles = [
                        [
                            src[s * chans + r : s * chans + r + tall, c : c + wide].astype(F32)
                            for s in range(layers)
                        ]
                        for src in ins
                    ]
                    for o in range(outs):
                        for x in range(layers):
                            at = slice(x * chans + r, x * chans + r + tall)
                            total = adds[o][at, c : c + wide] if adds else None
                            for tile, table in zip(tiles, tables[o]):
                                for s in range(layers):
                                    weight = float(table[x, s])
                                    if weight != 0.0:
                                        term = tile[s] * weight
                                        total = term if total is None else total + term
                            if total is None:
                                total = jnp.zeros((tall, wide), F32)
                            results[o][at, c : c + wide] = total.astype(results[o].dtype)

        if len(coefs) == 1:
            run(coefs[0])
        else:
            for v in range(len(coefs)):
                pl.when(info_ref[PLACE_X] == v)(functools.partial(run, coefs[v]))
        if face == plane:
            for at, ref in zip((0, rows // 2), results[outs:]):
                ref[...] = results[0][at : at + rows // 2, :]
        elif face:
            send_faces(info_ref, ODD_Y, results[0], face, results[outs], results[outs + 1 :])

    shapes = tuple(shape((rows, plane), t) for t in out_types)
    if face:
        shapes += faces_shape(rows, face)[face == plane :]
    needs = ([PLACE_X] if len(coefs) > 1 else []) + ([ODD_Y] if face else [])
    return call(body, shapes, info, needs, [*sources, *sums], name="mix_layers", after=after)


def filter_lanes(info, first, middle, second, table):
    def body(info_ref, first_ref, middle_ref, upper, lower, weights, out):
        out[...] = swapped_dot(info_ref, ODD_Y, first_ref, [middle_ref], (upper, lower), weights)

    shapes = shape((first.shape[0], table.shape[1]), F32)
    return call(body, shapes, info, [ODD_Y], [first, middle, *second, table], name="filter_lanes")


def filter_faces(info, first, middle, second, table, below=(), after=()):
    rows, face = first.shape[0], table.shape[1] // 2
    extra = below[0].shape[0] if below else 0

    def body(info_ref, first_ref, middle_ref, upper, lower, weights, *refs):
        outs = refs[-2:]
        total = swapped_dot(info_ref, ODD_Y, first_ref, [middle_ref], (upper, lower), weights)
        send_faces(info_ref, ODD_Z, total, face, *(out.at[:rows, :] for out in outs))
        for src, out in zip(refs[:-2], outs):
            out[rows:, :] = src[...]

    shapes = (shape((rows + extra, face), BF16),) * 2
    arrays = [first, middle, *second, table, *below]
    return call(body, shapes, info, [ODD_Y, ODD_Z], arrays, name="filter_faces", after=after)


def live_lanes(info_ref, layer, dims, size_y, size_z):
    row = layer * size_y + lax.broadcasted_iota(jnp.int32, dims, 1) // size_z
    return row < info_ref[COUNT]


def courses_of(info, acc, first, middle, second, table, bold, chans, size_y, size_z):
    frames = bold.shape[1]
    plane = size_y * size_z
    layers = bold.shape[0] // plane
    between = len(middle)

    def body(info_ref, first_ref, *refs):
        ins, second_ref, weights, frames_ref = refs[:between], *refs[between : between + 3]
        total = jnp.zeros((chans, frames), F32)
        for x in range(layers):
            rows = slice(x * chans, (x + 1) * chans)
            value = swapped_dot(info_ref, ODD_Z, first_ref, ins, second_ref, weights, rows, sent=between == 2)
            if acc is not None:
                value = value + refs[between + 3][rows, :]
            keep = live_lanes(info_ref, x, value.shape, size_y, size_z)
            value = jnp.where(keep, value, 0.0).astype(BF16)
            total = total + dot(value, frames_ref[x * plane : (x + 1) * plane, :])
        refs[-1][...] = total

    arrays = [first, *middle, second, table, bold] + ([acc] if acc is not None else [])
    shapes = shape((chans, frames), F32)
    return call(body, shapes, info, [COUNT, ODD_Z], arrays, flops=10**9, name="courses_of")


def write_gradient(info_ref, courses, frames_ref, out, chans, size_y, size_z):
    plane = size_y * size_z
    for x in range(frames_ref.shape[0] // plane):
        value = dot_nt(courses, frames_ref[x * plane : (x + 1) * plane, :])
        keep = live_lanes(info_ref, x, value.shape, size_y, size_z)
        out[x * chans : (x + 1) * chans, :] = jnp.where(keep, value, 0.0).astype(BF16)


def first_gradient(info, sums, bold, chans, size_y, size_z):
    cells, frames = bold.shape

    def body(info_ref, sums_ref, frames_ref, out, half_ref):
        courses = sums_ref[...].astype(BF16)
        half_ref[...] = courses
        write_gradient(info_ref, courses, frames_ref, out, chans, size_y, size_z)

    shapes = (shape((cells * chans // (size_y * size_z), size_y * size_z), BF16), shape((chans, frames), BF16))
    return call(body, shapes, info, [COUNT], [sums, bold], flops=10**9, name="first_gradient")


def fade_of(courses):
    chans = courses.shape[0]
    wide = courses.astype(F32)
    scale = (0.5 * chans) / total_of(wide * wide)
    return unit_of(chans) - dot_nt(courses, courses) * scale


def first_fade(info, half1):
    chans, frames = half1.shape

    def body(_, half_ref, kept_ref, fade_ref):
        fade = fade_of(half_ref[...])
        fade_ref[...] = fade
        kept_ref[...] = jnp.dot(fade, half_ref[...].astype(F32), precision=FULL, preferred_element_type=F32)

    shapes = (shape((chans, frames), F32), shape((chans, chans), F32))
    return call(body, shapes, info, [], [half1], name="first_fade")


def second_gradient(info, change, half1, kept, bold, chans, size_y, size_z, all_cells):
    cells, frames = bold.shape

    def body(info_ref, change_ref, half1_ref, kept_ref, frames_ref, out, half_ref, scale_ref):
        change = change_ref[...]
        energy = jnp.maximum(total_of(half1_ref[...].astype(F32) * change), 0.0) * (1.0 / all_cells)
        scale = 0.5 * lax.rsqrt(energy + 1e-06)
        scale_ref[...] = scale
        courses = (kept_ref[...] + scale * change).astype(BF16)
        half_ref[...] = courses
        write_gradient(info_ref, courses, frames_ref, out, chans, size_y, size_z)

    shapes = (
        shape((cells * chans // (size_y * size_z), size_y * size_z), BF16),
        shape((chans, frames), BF16),
        shape((1, 1), F32),
    )
    arrays = [change, half1, kept, bold]
    return call(body, shapes, info, [COUNT], arrays, flops=10**9, name="second_gradient")


def second_fade(info, half2, fade1, scale1, field, face):
    chans = half2.shape[0]
    rows, plane = field.shape

    def body(info_ref, half_ref, fade_ref, scale_ref, field_ref, fades_ref, out, first, *second):
        fade = fade_of(half_ref[...])
        fades_ref[...] = jnp.dot(fade, fade_ref[...], precision=FULL, preferred_element_type=F32)
        weights = fade * scale_ref[...]
        high = weights.astype(BF16)
        low = (weights - high.astype(F32)).astype(BF16)
        for x in range(rows // chans):
            at = slice(x * chans, (x + 1) * chans)
            block = field_ref[at, :]
            out[at, :] = (dot(high, block) + dot(low, block)).astype(BF16)
        send_faces(info_ref, ODD_Y, out, face, first, second)

    shapes = (shape((chans, chans), F32), shape((rows, plane), BF16), *faces_shape(rows, face))
    arrays = [half2, fade1, scale1, field]
    return call(body, shapes, info, [ODD_Y], arrays, flops=10**9, name="second_fade")


def faded_maps(info, voxel_maps, fades):
    layers, plane, chans = voxel_maps.shape

    def body(_, maps_ref, fades_ref, out):
        for x in range(layers):
            out[x] = dot_nt(maps_ref[x], fades_ref[...], FULL)

    shapes = shape((layers, plane, chans), F32)
    return call(body, shapes, info, [], [voxel_maps, fades], flops=10**9, name="faded_maps")


def whole_gradient(info, acc, first, second, table):
    def body(info_ref, start, first_ref, second_ref, weights, out):
        value = start[...] + swapped_dot(info_ref, ODD_Z, first_ref, [], second_ref, weights)
        out[...] = value.astype(BF16)

    arrays = [acc, first, second, table]
    return call(body, shape(acc.shape, BF16), info, [ODD_Z], arrays, name="whole_gradient")


def gradient_energy(info, acc, first, second, table, peers, after=()):
    rows, plane = acc.shape
    tall = min(rows, 128)

    def body(info_ref, start, first_ref, second_ref, weights, out, energy):
        total = jnp.zeros((tall, plane), F32)
        for r in range(0, rows, tall):
            at = slice(r, r + tall)
            value = start[at, :] + swapped_dot(info_ref, ODD_Z, first_ref, [], second_ref, weights, at)
            total = total + value * value
            out[at, :] = value
        energy[...] = jnp.broadcast_to(total_of(total).reshape(1, 1, 1), energy.shape)

    shapes = (shape((rows, plane), F32), shape((peers, 1, 128), F32))
    arrays = [acc, first, second, table]
    return call(body, shapes, info, [ODD_Z], arrays, name="gradient_energy", after=after)


def final_maps(info, energies, base, acc, first, second, table, grad, all_cells):
    layers, plane, chans = base.shape
    rows = acc.shape[0]
    peers = energies.shape[0]

    def body(info_ref, energies_ref, base_ref, start, first_ref, second_ref, weights, grad_ref, out, held, sems):
        energy = energies_ref[0]
        for d in range(1, peers):
            energy = energy + energies_ref[d]
        scale = 0.5 * lax.rsqrt(energy[:, :1] * (1.0 / all_cells) + 1e-06)
        copies = []
        for x in range(layers):
            at = slice(x * chans, (x + 1) * chans)
            below = slice(rows + x * chans, rows + (x + 1) * chans)
            value = start[at, :] + swapped_dot(info_ref, ODD_Z, first_ref, [], second_ref, weights, below)
            held[x] = base_ref[x] + (value + scale * grad_ref[at, :]).T
            copies.append(pltpu.make_async_copy(held.at[x], out.at[x], sems.at[x]))
            copies[-1].start()
        for copy in copies:
            copy.wait()

    return call(
        body,
        shape(base.shape, F32),
        info,
        [ODD_Z],
        [energies, base, acc, first, second, table, grad],
        name="final_maps",
        outs=pl.BlockSpec(memory_space=pl.ANY),
        scratch=(pltpu.VMEM(base.shape, F32), pltpu.SemaphoreType.DMA((layers,))),
    )


def swap(face, axis, start):
    pairs = [(i, i + 1) for i in range(start, lax.axis_size(axis) - 1, 2)]
    return lax.ppermute(face, axis, pairs + [(j, i) for i, j in pairs])


def swapped(first, second, axis):
    return swap(first, axis, 0), swap(second, axis, 1)


def shifted(lower, upper, axis):
    peers = lax.axis_size(axis)
    up = [(i, i + 1) for i in range(peers - 1)]
    down = [(j, i) for i, j in up]
    return lax.ppermute(upper, axis, up), lax.ppermute(lower, axis, down)


def exchanged(parts):
    return lax.all_to_all(parts, AXES, 0, 0, tiled=True)


def hypercube_sum(value):
    steps = []
    for axis in AXES:
        peers = lax.axis_size(axis)
        if peers & (peers - 1):
            return lax.psum(value, AXES)
        steps += [(axis, 1 << b) for b in range(peers.bit_length() - 1)]
    for axis, bit in steps:
        pairs = [(i, i ^ bit) for i in range(lax.axis_size(axis))]
        value = lax.reduce_precision(value, 8, 7)
        value = value + lax.ppermute(value.astype(BF16), axis, pairs).astype(F32)
    return value


def per_device(bold_data, spatial_maps, live_blocks):
    chans, size_x, size_y, size_z = spatial_maps.shape
    frames = bold_data.shape[3]
    plane = size_y * size_z
    parts_x, parts_y, parts_z = (lax.axis_size(a) for a in AXES)
    peers = parts_x * parts_y * parts_z
    places = [lax.axis_index(a).astype(jnp.int32) for a in AXES]
    numbers = [*places, places[1] % 2, places[2] % 2, live_blocks]
    info = [number.reshape(1) for number in numbers]
    bold = bold_data.reshape(size_x * plane, frames)
    voxel_maps = jnp.transpose(spatial_maps, (1, 2, 3, 0)).reshape(size_x, plane, chans)
    all_cells = float(chans * size_x * plane * peers)

    win_x, win_y, win_z = (inner_window(s) for s in (size_x, size_y, size_z))
    unit_y, unit_z = np.eye(size_y), np.eye(size_z)
    ends = np.concatenate([np.kron(win_y.T, unit_z[:, :RADIUS]), np.kron(win_y.T, unit_z[:, -RADIUS:])], 1)
    table_ends = jnp.asarray(half(ends))
    table_own = jnp.asarray(half(np.kron(win_y.T, win_z[:, RADIUS:-RADIUS].T)))
    table_z = jnp.asarray(
        half(np.concatenate([np.kron(unit_y, win_z[:, :RADIUS].T), np.kron(unit_y, win_z[:, -RADIUS:].T)]))
    )
    face_y = RADIUS * size_z

    reach = 2 * RADIUS
    twice = parts_x == 2 and size_y == reach and size_z == 2 * reach
    full_x = band(size_x * parts_x)
    own_x = [slice(p * size_x, (p + 1) * size_x) for p in range(parts_x)]

    def along_x(block, matrices, beside=(), face=face_y):
        kinds = [BF16] * len(matrices)
        if parts_x == 2:
            mine = [[[m[own_x[p], own_x[p]]] for m in matrices] for p in range(2)]
            other = [[[m[own_x[p], own_x[1 - p]]] for m in matrices] for p in range(2)]
            got = lax.ppermute(block, "gx", [(0, 1), (1, 0)])
            sums = mix_layers(info, mine, chans, [block], [], [F32] * len(matrices))
            return mix_layers(info, other, chans, [got], list(sums), kinds, face=face, after=beside)
        depth = RADIUS * chans
        before, after = shifted(block[:depth], block[-depth:], "gx")
        rest = jnp.zeros((block.shape[0] - depth, plane), BF16)
        before, after = jnp.concatenate([rest, before]), jnp.concatenate([after, rest])
        tables = []
        for lo in (-size_x, 0, size_x):
            columns = np.arange(size_x) + lo + RADIUS
            inside = (columns >= 0) & (columns < win_x.shape[1])
            tables.append(np.where(inside[None], win_x[:, np.clip(columns, 0, win_x.shape[1] - 1)], 0.0))
        return mix_layers(info, [[tables]], chans, [before, block, after], [], kinds, face=face_y)

    def along_y(first, *second):
        second = tuple(swap(piece, "gy", 1) for piece in second)
        return swap(first, "gy", 0), second

    def along_rest(field, *faces):
        first, second = along_y(*faces)
        ends = swapped(*filter_faces(info, first, field, second, table_ends), "gz")
        return filter_lanes(info, first, field, second, table_own), *ends

    def all_courses(acc, first, middle, second, table):
        return hypercube_sum(
            courses_of(info, acc, first, middle, second, table, bold, chans, size_y, size_z)
        )

    plain = pack_maps(info, voxel_maps)
    acc, first, second = along_rest(*along_x(plain, [full_x]))
    courses1 = all_courses(acc, first, [], second, table_z)
    raw1, half1 = first_gradient(info, courses1, bold, chans, size_y, size_z)
    kept, fade1 = first_fade(info, half1)
    if twice:
        square_y = windows(np.linalg.matrix_power(band(size_y * parts_y), 2), size_y, parts_y, reach)
        square_z = windows(np.linalg.matrix_power(band(size_z * parts_z), 2), size_z, parts_z, reach)
        ordered = np.concatenate([unit_z[:, :reach], unit_z[:, reach:]], 1).reshape(size_z, 2, reach)
        tables_y = np.stack([
            np.concatenate([np.kron(w.T, ordered[:, h]) for h in range(2)], 1) for w in square_y
        ])
        tables_z = np.stack([
            np.concatenate([np.kron(unit_y, w[:, h * reach : (h + 1) * reach].T) for h in range(4)])
            for w in square_z
        ])
        table_y2, table_z2 = pick_tables(info, jnp.asarray(half(tables_y)), jnp.asarray(half(tables_z)))
        twice_x, once_x, *faces = along_x(raw1, [full_x @ full_x, full_x], [kept], plane)
        first, second = along_y(twice_x, *faces)
        sent = filter_faces(info, first, twice_x, second, table_y2)
        first, second = swapped(*sent, "gz")
        change = all_courses(None, first, list(sent), second, table_z2)
    else:
        once_x, *faces1 = along_x(raw1, [full_x])
        again = whole_gradient(info, *along_rest(once_x, *faces1), table_z)
        acc2, first, second = along_rest(*along_x(again, [full_x]))
        change = all_courses(acc2, first, [], second, table_z)

    raw2, half2, scale1 = second_gradient(
        info, change, half1, kept, bold, chans, size_y, size_z, all_cells
    )
    fades, field1, *faces1 = second_fade(info, half2, fade1, scale1, once_x, face_y)
    first1, second1 = along_y(*faces1)
    below = filter_faces(info, first1, field1, second1, table_ends)
    acc1 = filter_lanes(info, first1, field1, second1, table_own)
    base = faded_maps(info, voxel_maps, fades)

    field2, *faces2 = along_x(raw2, [full_x], [base])
    first2, second2 = along_y(*faces2)
    ends = swapped(*filter_faces(info, first2, field2, second2, table_ends, below, [acc1]), "gz")
    acc2 = filter_lanes(info, first2, field2, second2, table_own)
    grad2, energies = gradient_energy(info, acc2, *ends, table_z, peers)
    maps = final_maps(info, exchanged(energies), base, acc1, *ends, table_z, grad2, all_cells)
    maps = maps.reshape(size_x, size_y, size_z, chans)
    return (jnp.transpose(maps, (3, 0, 1, 2)), half2)


def solution(mesh):
    return jax.shard_map(
        per_device,
        mesh=mesh,
        in_specs=(P("gx", "gy", "gz", None), P(None, "gx", "gy", "gz"), P("gx", "gy", "gz")),
        out_specs=(P(None, "gx", "gy", "gz"), P()),
        check_vma=False,
    )
```

```python
import functools
import math

import jax
import jax.numpy as jnp
import ml_dtypes
import numpy as np
from jax import lax
from jax.experimental import pallas as pl
from jax.experimental.pallas import tpu as pltpu
from jax.sharding import PartitionSpec as P

RADIUS = 8
F32 = jnp.float32
BF16 = jnp.bfloat16
AXES = ("gx", "gy", "gz")


def band(length):
    total = sum(math.exp(-float(d * d) / 32.0) for d in range(-RADIUS, RADIUS + 1))
    gap = np.abs(np.arange(length)[:, None] - np.arange(length)[None, :])
    return np.where(gap <= RADIUS, np.exp(-(gap.astype(np.float64) ** 2) / 32.0) / total, 0.0)


def windows(matrix, size, parts, reach):
    padded = np.pad(matrix, ((0, 0), (reach, reach)))
    return np.stack(
        [padded[p * size : (p + 1) * size, p * size : (p + 1) * size + 2 * reach] for p in range(parts)]
    )


def half(array):
    return np.asarray(array, dtype=ml_dtypes.bfloat16)


def inner_window(size):
    return windows(band(3 * size), size, 3, RADIUS)[1]


PLACE_X, PLACE_Y, PLACE_Z, ODD_Y, ODD_Z, COUNT = range(6)
NT = (((1,), (1,)), ((), ()))
FULL = lax.Precision.HIGHEST


def shape(dims, kind):
    return jax.ShapeDtypeStruct(dims, kind)


def call(body, shapes, info, needs, arrays, flops=10**8, name=None, spaces=None, outs=None, scratch=(), after=()):
    total = sum(a.size * a.dtype.itemsize for a in arrays)
    whole, anywhere = pl.BlockSpec(memory_space=pltpu.VMEM), pl.BlockSpec(memory_space=pl.ANY)
    count, ends = len(needs), len(needs) + len(arrays)

    def wrapped(*refs):
        numbers = {need: ref for need, ref in zip(needs, refs)}
        body(Numbers(numbers), *refs[count:ends], *refs[ends + len(after) :])

    return pl.pallas_call(
        wrapped,
        out_shape=shapes,
        in_specs=[pl.BlockSpec(memory_space=pltpu.SMEM)] * count
        + [spaces or whole] * len(arrays)
        + [anywhere] * len(after),
        out_specs=jax.tree.map(lambda _: outs or whole, shapes),
        scratch_shapes=scratch,
        compiler_params=pltpu.CompilerParams(vmem_limit_bytes=16 * 1024 * 1024),
        cost_estimate=pl.CostEstimate(flops=flops, bytes_accessed=total, transcendentals=0),
        name=name,
    )(*(info[need] for need in needs), *arrays, *after)


class Numbers:
    def __init__(self, refs):
        self.refs = refs

    def __getitem__(self, need):
        return self.refs[need][0]


def dot(a, b):
    return jnp.dot(a, b, preferred_element_type=F32)


def dot_nt(a, b, precision=None):
    return lax.dot_general(a, b, NT, precision=precision, preferred_element_type=F32)


def unit_of(size):
    return (
        lax.broadcasted_iota(jnp.int32, (size, size), 0) == lax.broadcasted_iota(jnp.int32, (size, size), 1)
    ).astype(F32)


def total_of(value):
    return jnp.sum(jnp.sum(value, axis=1, keepdims=True), axis=0, keepdims=True)


def pack_maps(info, voxel_maps):
    layers, plane, chans = voxel_maps.shape

    def body(_, src, out):
        unit = unit_of(chans).astype(BF16)
        for x in range(layers):
            out[x * chans : (x + 1) * chans, :] = dot_nt(unit, src[x].astype(BF16)).astype(BF16)

    return call(body, shape((layers * chans, plane), BF16), info, [], [voxel_maps], name="pack_maps")


def pick_tables(info, table_y, table_z):
    def body(info_ref, all_y, all_z, out_y, out_z, sem_y, sem_z):
        copies = [
            pltpu.make_async_copy(all_y.at[info_ref[PLACE_Y]], out_y, sem_y),
            pltpu.make_async_copy(all_z.at[info_ref[PLACE_Z]], out_z, sem_z),
        ]
        for copy in copies:
            copy.start()
        for copy in copies:
            copy.wait()

    shapes = (shape(table_y.shape[1:], BF16), shape(table_z.shape[1:], BF16))
    return call(
        body,
        shapes,
        info,
        [PLACE_Y, PLACE_Z],
        [table_y, table_z],
        name="pick_tables",
        spaces=pl.BlockSpec(memory_space=pl.ANY),
        scratch=(pltpu.SemaphoreType.DMA, pltpu.SemaphoreType.DMA),
    )


def send_faces(info_ref, odd, field, face, first=None, second=None):
    plane = field.shape[1]
    low, high = slice(0, face), slice(plane - face, plane)

    def write(of_first, of_second):
        for ref, lanes in ((first, of_first), (second, of_second)):
            if ref is not None:
                ref[...] = field[:, lanes].astype(ref.dtype)

    pl.when(info_ref[odd] == 0)(lambda: write(high, low))
    pl.when(info_ref[odd] != 0)(lambda: write(low, high))


def cut_face(info, field, face):
    def body(info_ref, field_ref, out):
        send_faces(info_ref, ODD_Y, field_ref, face, second=out)

    shapes = shape((field.shape[0], face), field.dtype)
    return call(body, shapes, info, [ODD_Y], [field], flops=10**9, name="cut_face")


def swapped_dot(info_ref, odd, first, middle, second, weights, rows=slice(None), sent=False):
    width = first.shape[1]
    end = weights.shape[0] - width
    even = info_ref[odd] == 0

    def at(when_even, when_odd):
        return weights[pl.ds(pl.multiple_of(jnp.where(even, when_even, when_odd), width), width), :]

    total = dot(first[rows, :], at(end, 0)) + dot(second[rows, :], at(0, end))
    if sent:
        high = end - width
        return total + dot(middle[0][rows, :], at(high, width)) + dot(middle[1][rows, :], at(width, high))
    for piece in middle:
        total = total + dot(piece[rows, :], weights[width : width + piece.shape[1], :])
    return total


def mix_layers(info, coefs, chans, sources, sums, out_types, face=0, after=()):
    rows, plane = sources[0].shape
    outs = len(out_types)
    base = len(sources)
    tall, wide = 16, 128

    def body(info_ref, *refs):
        ins, adds, results = refs[:base], refs[base : base + len(sums)], refs[base + len(sums) :]

        def run(tables):
            layers = tables[0][0].shape[0]
            for r in range(0, chans, tall):
                for c in range(0, plane, wide):
                    tiles = [
                        [
                            src[s * chans + r : s * chans + r + tall, c : c + wide].astype(F32)
                            for s in range(layers)
                        ]
                        for src in ins
                    ]
                    for o in range(outs):
                        for x in range(layers):
                            at = slice(x * chans + r, x * chans + r + tall)
                            total = adds[o][at, c : c + wide] if adds else None
                            for tile, table in zip(tiles, tables[o]):
                                for s in range(layers):
                                    weight = float(table[x, s])
                                    if weight != 0.0:
                                        term = tile[s] * weight
                                        total = term if total is None else total + term
                            if total is None:
                                total = jnp.zeros((tall, wide), F32)
                            results[o][at, c : c + wide] = total.astype(results[o].dtype)

        if len(coefs) == 1:
            run(coefs[0])
        else:
            for v in range(len(coefs)):
                pl.when(info_ref[PLACE_X] == v)(functools.partial(run, coefs[v]))
        if face:
            send_faces(info_ref, ODD_Y, results[0], face, first=results[outs])

    shapes = tuple(shape((rows, plane), t) for t in out_types)
    if face:
        shapes += (shape((rows, face), out_types[0]),)
    needs = ([PLACE_X] if len(coefs) > 1 else []) + ([ODD_Y] if face else [])
    return call(body, shapes, info, needs, [*sources, *sums], name="mix_layers", after=after)


def filter_lanes(info, first, middle, second, table):
    def body(info_ref, first_ref, middle_ref, second_ref, weights, out):
        out[...] = swapped_dot(info_ref, ODD_Y, first_ref, [middle_ref], second_ref, weights)

    shapes = shape((first.shape[0], table.shape[1]), F32)
    return call(body, shapes, info, [ODD_Y], [first, middle, second, table], name="filter_lanes")


def filter_faces(info, first, middle, second, table, below=(), after=()):
    rows, face = first.shape[0], table.shape[1] // 2
    extra = below[0].shape[0] if below else 0

    def body(info_ref, first_ref, middle_ref, second_ref, weights, *refs):
        outs = refs[-2:]
        total = swapped_dot(info_ref, ODD_Y, first_ref, [middle_ref], second_ref, weights)
        send_faces(info_ref, ODD_Z, total, face, *(out.at[:rows, :] for out in outs))
        for src, out in zip(refs[:-2], outs):
            out[rows:, :] = src[...]

    shapes = (shape((rows + extra, face), BF16),) * 2
    arrays = [first, middle, second, table, *below]
    return call(body, shapes, info, [ODD_Y, ODD_Z], arrays, name="filter_faces", after=after)


def live_lanes(info_ref, layer, dims, size_y, size_z):
    row = layer * size_y + lax.broadcasted_iota(jnp.int32, dims, 1) // size_z
    return row < info_ref[COUNT]


def courses_of(info, acc, first, middle, second, table, bold, chans, size_y, size_z):
    frames = bold.shape[1]
    plane = size_y * size_z
    layers = bold.shape[0] // plane
    between = len(middle)

    def body(info_ref, first_ref, *refs):
        ins, second_ref, weights, frames_ref = refs[:between], *refs[between : between + 3]
        total = jnp.zeros((chans, frames), F32)
        for x in range(layers):
            rows = slice(x * chans, (x + 1) * chans)
            value = swapped_dot(info_ref, ODD_Z, first_ref, ins, second_ref, weights, rows, sent=between == 2)
            if acc is not None:
                value = value + refs[between + 3][rows, :]
            keep = live_lanes(info_ref, x, value.shape, size_y, size_z)
            value = jnp.where(keep, value, 0.0).astype(BF16)
            total = total + dot(value, frames_ref[x * plane : (x + 1) * plane, :])
        refs[-1][...] = total

    arrays = [first, *middle, second, table, bold] + ([acc] if acc is not None else [])
    shapes = shape((chans, frames), F32)
    return call(body, shapes, info, [COUNT, ODD_Z], arrays, flops=10**9, name="courses_of")


def write_gradient(info_ref, courses, frames_ref, out, chans, size_y, size_z):
    plane = size_y * size_z
    for x in range(frames_ref.shape[0] // plane):
        value = dot_nt(courses, frames_ref[x * plane : (x + 1) * plane, :])
        keep = live_lanes(info_ref, x, value.shape, size_y, size_z)
        out[x * chans : (x + 1) * chans, :] = jnp.where(keep, value, 0.0).astype(BF16)


def first_gradient(info, sums, bold, chans, size_y, size_z):
    cells, frames = bold.shape

    def body(info_ref, sums_ref, frames_ref, out, half_ref):
        courses = sums_ref[...].astype(BF16)
        half_ref[...] = courses
        write_gradient(info_ref, courses, frames_ref, out, chans, size_y, size_z)

    shapes = (shape((cells * chans // (size_y * size_z), size_y * size_z), BF16), shape((chans, frames), BF16))
    return call(body, shapes, info, [COUNT], [sums, bold], flops=10**9, name="first_gradient")


def fade_of(courses):
    chans = courses.shape[0]
    wide = courses.astype(F32)
    scale = (0.5 * chans) / total_of(wide * wide)
    return unit_of(chans) - dot_nt(courses, courses) * scale


def first_fade(info, half1):
    chans, frames = half1.shape

    def body(_, half_ref, kept_ref, fade_ref):
        fade = fade_of(half_ref[...])
        fade_ref[...] = fade
        kept_ref[...] = jnp.dot(fade, half_ref[...].astype(F32), precision=FULL, preferred_element_type=F32)

    shapes = (shape((chans, frames), F32), shape((chans, chans), F32))
    return call(body, shapes, info, [], [half1], name="first_fade")


def second_gradient(info, change, half1, kept, bold, chans, size_y, size_z, all_cells):
    cells, frames = bold.shape

    def body(info_ref, change_ref, half1_ref, kept_ref, frames_ref, out, half_ref, scale_ref):
        change = change_ref[...]
        energy = jnp.maximum(total_of(half1_ref[...].astype(F32) * change), 0.0) * (1.0 / all_cells)
        scale = 0.5 * lax.rsqrt(energy + 1e-06)
        scale_ref[...] = scale
        courses = (kept_ref[...] + scale * change).astype(BF16)
        half_ref[...] = courses
        write_gradient(info_ref, courses, frames_ref, out, chans, size_y, size_z)

    shapes = (
        shape((cells * chans // (size_y * size_z), size_y * size_z), BF16),
        shape((chans, frames), BF16),
        shape((1, 1), F32),
    )
    arrays = [change, half1, kept, bold]
    return call(body, shapes, info, [COUNT], arrays, flops=10**9, name="second_gradient")


def second_fade(info, half2, fade1, scale1, field, face):
    chans = half2.shape[0]
    rows, plane = field.shape

    def body(info_ref, half_ref, fade_ref, scale_ref, field_ref, fades_ref, out, first):
        fade = fade_of(half_ref[...])
        fades_ref[...] = jnp.dot(fade, fade_ref[...], precision=FULL, preferred_element_type=F32)
        weights = fade * scale_ref[...]
        high = weights.astype(BF16)
        low = (weights - high.astype(F32)).astype(BF16)
        for x in range(rows // chans):
            at = slice(x * chans, (x + 1) * chans)
            block = field_ref[at, :]
            out[at, :] = (dot(high, block) + dot(low, block)).astype(BF16)
        send_faces(info_ref, ODD_Y, out, face, first=first)

    shapes = (
        shape((chans, chans), F32),
        shape((rows, plane), BF16),
        shape((rows, face), BF16),
    )
    arrays = [half2, fade1, scale1, field]
    return call(body, shapes, info, [ODD_Y], arrays, flops=10**9, name="second_fade")


def faded_maps(info, voxel_maps, fades):
    layers, plane, chans = voxel_maps.shape

    def body(_, maps_ref, fades_ref, out):
        for x in range(layers):
            out[x] = dot_nt(maps_ref[x], fades_ref[...], FULL)

    shapes = shape((layers, plane, chans), F32)
    return call(body, shapes, info, [], [voxel_maps, fades], flops=10**9, name="faded_maps")


def whole_gradient(info, acc, first, second, table):
    def body(info_ref, start, first_ref, second_ref, weights, out):
        value = start[...] + swapped_dot(info_ref, ODD_Z, first_ref, [], second_ref, weights)
        out[...] = value.astype(BF16)

    arrays = [acc, first, second, table]
    return call(body, shape(acc.shape, BF16), info, [ODD_Z], arrays, name="whole_gradient")


def gradient_energy(info, acc, first, second, table, peers, after=()):
    rows, plane = acc.shape
    tall = min(rows, 128)

    def body(info_ref, start, first_ref, second_ref, weights, out, energy):
        total = jnp.zeros((tall, plane), F32)
        for r in range(0, rows, tall):
            at = slice(r, r + tall)
            value = start[at, :] + swapped_dot(info_ref, ODD_Z, first_ref, [], second_ref, weights, at)
            total = total + value * value
            out[at, :] = value
        energy[...] = jnp.broadcast_to(total_of(total).reshape(1, 1, 1), energy.shape)

    shapes = (shape((rows, plane), F32), shape((peers, 1, 128), F32))
    arrays = [acc, first, second, table]
    return call(body, shapes, info, [ODD_Z], arrays, name="gradient_energy", after=after)


def final_maps(info, energies, base, acc, first, second, table, grad, all_cells):
    layers, plane, chans = base.shape
    rows = acc.shape[0]
    peers = energies.shape[0]

    def body(info_ref, energies_ref, base_ref, start, first_ref, second_ref, weights, grad_ref, out, held, sems):
        energy = energies_ref[0]
        for d in range(1, peers):
            energy = energy + energies_ref[d]
        scale = 0.5 * lax.rsqrt(energy[:, :1] * (1.0 / all_cells) + 1e-06)
        copies = []
        for x in range(layers):
            at = slice(x * chans, (x + 1) * chans)
            below = slice(rows + x * chans, rows + (x + 1) * chans)
            value = start[at, :] + swapped_dot(info_ref, ODD_Z, first_ref, [], second_ref, weights, below)
            held[x] = base_ref[x] + (value + scale * grad_ref[at, :]).T
            copies.append(pltpu.make_async_copy(held.at[x], out.at[x], sems.at[x]))
            copies[-1].start()
        for copy in copies:
            copy.wait()

    return call(
        body,
        shape(base.shape, F32),
        info,
        [ODD_Z],
        [energies, base, acc, first, second, table, grad],
        name="final_maps",
        outs=pl.BlockSpec(memory_space=pl.ANY),
        scratch=(pltpu.VMEM(base.shape, F32), pltpu.SemaphoreType.DMA((layers,))),
    )


def swapped(first, second, axis, inner_first=False):
    peers = lax.axis_size(axis)
    got = {}
    for start in (1, 0) if inner_first else (0, 1):
        pairs = [(i, i + 1) for i in range(start, peers - 1, 2)]
        pairs += [(j, i) for i, j in pairs]
        got[start] = lax.ppermute((first, second)[start], axis, pairs)
    return got[0], got[1]


def shifted(lower, upper, axis):
    peers = lax.axis_size(axis)
    up = [(i, i + 1) for i in range(peers - 1)]
    down = [(j, i) for i, j in up]
    return lax.ppermute(upper, axis, up), lax.ppermute(lower, axis, down)


def exchanged(parts):
    return lax.all_to_all(parts, AXES, 0, 0, tiled=True)


def hypercube_sum(value):
    steps = []
    for axis in AXES:
        peers = lax.axis_size(axis)
        if peers & (peers - 1):
            return lax.psum(value, AXES)
        steps += [(axis, 1 << b) for b in range(peers.bit_length() - 1)]
    for axis, bit in steps:
        pairs = [(i, i ^ bit) for i in range(lax.axis_size(axis))]
        value = lax.reduce_precision(value, 8, 7)
        value = value + lax.ppermute(value.astype(BF16), axis, pairs).astype(F32)
    return value


def per_device(bold_data, spatial_maps, live_blocks):
    chans, size_x, size_y, size_z = spatial_maps.shape
    frames = bold_data.shape[3]
    plane = size_y * size_z
    parts_x, parts_y, parts_z = (lax.axis_size(a) for a in AXES)
    peers = parts_x * parts_y * parts_z
    places = [lax.axis_index(a).astype(jnp.int32) for a in AXES]
    numbers = [*places, places[1] % 2, places[2] % 2, live_blocks]
    info = [number.reshape(1) for number in numbers]
    bold = bold_data.reshape(size_x * plane, frames)
    voxel_maps = jnp.transpose(spatial_maps, (1, 2, 3, 0)).reshape(size_x, plane, chans)
    all_cells = float(chans * size_x * plane * peers)

    win_x, win_y, win_z = (inner_window(s) for s in (size_x, size_y, size_z))
    unit_y, unit_z = np.eye(size_y), np.eye(size_z)
    ends = np.concatenate([np.kron(win_y.T, unit_z[:, :RADIUS]), np.kron(win_y.T, unit_z[:, -RADIUS:])], 1)
    table_ends = jnp.asarray(half(ends))
    table_own = jnp.asarray(half(np.kron(win_y.T, win_z[:, RADIUS:-RADIUS].T)))
    table_z = jnp.asarray(
        half(np.concatenate([np.kron(unit_y, win_z[:, :RADIUS].T), np.kron(unit_y, win_z[:, -RADIUS:].T)]))
    )
    face_y = RADIUS * size_z

    reach = 2 * RADIUS
    twice = parts_x == 2 and size_y == reach and size_z == 2 * reach
    full_x = band(size_x * parts_x)
    own_x = [slice(p * size_x, (p + 1) * size_x) for p in range(parts_x)]

    def along_x(block, matrices, beside=(), face=face_y):
        kinds = [BF16] * len(matrices)
        if parts_x == 2:
            mine = [[[m[own_x[p], own_x[p]]] for m in matrices] for p in range(2)]
            other = [[[m[own_x[p], own_x[1 - p]]] for m in matrices] for p in range(2)]
            got = lax.ppermute(block, "gx", [(0, 1), (1, 0)])
            sums = mix_layers(info, mine, chans, [block], [], [F32] * len(matrices))
            return mix_layers(info, other, chans, [got], list(sums), kinds, face=face, after=beside)
        depth = RADIUS * chans
        before, after = shifted(block[:depth], block[-depth:], "gx")
        rest = jnp.zeros((block.shape[0] - depth, plane), BF16)
        before, after = jnp.concatenate([rest, before]), jnp.concatenate([after, rest])
        tables = []
        for lo in (-size_x, 0, size_x):
            columns = np.arange(size_x) + lo + RADIUS
            inside = (columns >= 0) & (columns < win_x.shape[1])
            tables.append(np.where(inside[None], win_x[:, np.clip(columns, 0, win_x.shape[1] - 1)], 0.0))
        return mix_layers(info, [[tables]], chans, [before, block, after], [], kinds, face=face_y)

    def along_y(field, first):
        return swapped(first, cut_face(info, field, face_y), "gy", inner_first=True)

    def along_rest(field, first):
        first, second = along_y(field, first)
        ends = swapped(*filter_faces(info, first, field, second, table_ends), "gz")
        return filter_lanes(info, first, field, second, table_own), *ends

    def all_courses(acc, first, middle, second, table):
        return hypercube_sum(
            courses_of(info, acc, first, middle, second, table, bold, chans, size_y, size_z)
        )

    plain = pack_maps(info, voxel_maps)
    acc, first, second = along_rest(*along_x(plain, [full_x]))
    courses1 = all_courses(acc, first, [], second, table_z)
    raw1, half1 = first_gradient(info, courses1, bold, chans, size_y, size_z)
    kept, fade1 = first_fade(info, half1)
    if twice:
        square_y = windows(np.linalg.matrix_power(band(size_y * parts_y), 2), size_y, parts_y, reach)
        square_z = windows(np.linalg.matrix_power(band(size_z * parts_z), 2), size_z, parts_z, reach)
        ordered = np.concatenate([unit_z[:, :reach], unit_z[:, reach:]], 1).reshape(size_z, 2, reach)
        tables_y = np.stack([
            np.concatenate([np.kron(w.T, ordered[:, h]) for h in range(2)], 1) for w in square_y
        ])
        tables_z = np.stack([
            np.concatenate([np.kron(unit_y, w[:, h * reach : (h + 1) * reach].T) for h in range(4)])
            for w in square_z
        ])
        table_y2, table_z2 = pick_tables(info, jnp.asarray(half(tables_y)), jnp.asarray(half(tables_z)))
        twice_x, once_x = along_x(raw1, [full_x @ full_x, full_x], [kept], 0)
        first, second = swapped(twice_x, twice_x, "gy", inner_first=True)
        sent = filter_faces(info, first, twice_x, second, table_y2)
        first, second = swapped(*sent, "gz")
        change = all_courses(None, first, list(sent), second, table_z2)
    else:
        once_x, face1 = along_x(raw1, [full_x])
        again = whole_gradient(info, *along_rest(once_x, face1), table_z)
        acc2, first, second = along_rest(*along_x(again, [full_x]))
        change = all_courses(acc2, first, [], second, table_z)

    raw2, half2, scale1 = second_gradient(
        info, change, half1, kept, bold, chans, size_y, size_z, all_cells
    )
    fades, field1, face1 = second_fade(info, half2, fade1, scale1, once_x, face_y)
    first1, second1 = along_y(field1, face1)
    below = filter_faces(info, first1, field1, second1, table_ends)
    acc1 = filter_lanes(info, first1, field1, second1, table_own)
    base = faded_maps(info, voxel_maps, fades)

    field2, face2 = along_x(raw2, [full_x], [base])
    first2, second2 = along_y(field2, face2)
    ends = swapped(*filter_faces(info, first2, field2, second2, table_ends, below, [acc1]), "gz")
    acc2 = filter_lanes(info, first2, field2, second2, table_own)
    grad2, energies = gradient_energy(info, acc2, *ends, table_z, peers)
    maps = final_maps(info, exchanged(energies), base, acc1, *ends, table_z, grad2, all_cells)
    maps = maps.reshape(size_x, size_y, size_z, chans)
    return (jnp.transpose(maps, (3, 0, 1, 2)), half2)


def solution(mesh):
    return jax.shard_map(
        per_device,
        mesh=mesh,
        in_specs=(P("gx", "gy", "gz", None), P(None, "gx", "gy", "gz"), P("gx", "gy", "gz")),
        out_specs=(P(None, "gx", "gy", "gz"), P()),
        check_vma=False,
    )
```

```python
import functools
import math

import jax
import jax.numpy as jnp
import ml_dtypes
import numpy as np
from jax import lax
from jax.experimental import pallas as pl
from jax.experimental.pallas import tpu as pltpu
from jax.sharding import PartitionSpec as P

RADIUS = 8
F32 = jnp.float32
BF16 = jnp.bfloat16
AXES = ("gx", "gy", "gz")


def band(length):
    total = sum(math.exp(-float(d * d) / 32.0) for d in range(-RADIUS, RADIUS + 1))
    gap = np.abs(np.arange(length)[:, None] - np.arange(length)[None, :])
    return np.where(gap <= RADIUS, np.exp(-(gap.astype(np.float64) ** 2) / 32.0) / total, 0.0)


def windows(matrix, size, parts, reach):
    padded = np.pad(matrix, ((0, 0), (reach, reach)))
    return np.stack(
        [padded[p * size : (p + 1) * size, p * size : (p + 1) * size + 2 * reach] for p in range(parts)]
    )


def half(array):
    return np.asarray(array, dtype=ml_dtypes.bfloat16)


def inner_window(size):
    return windows(band(3 * size), size, 3, RADIUS)[1]


PLACE_X, PLACE_Y, PLACE_Z, ODD_Y, ODD_Z, COUNT = range(6)
NT = (((1,), (1,)), ((), ()))
FULL = lax.Precision.HIGHEST


def shape(dims, kind):
    return jax.ShapeDtypeStruct(dims, kind)


def call(body, shapes, info, needs, arrays, flops=10**8, name=None, spaces=None, outs=None, scratch=(), after=()):
    total = sum(a.size * a.dtype.itemsize for a in arrays)
    whole, anywhere = pl.BlockSpec(memory_space=pltpu.VMEM), pl.BlockSpec(memory_space=pl.ANY)
    count, ends = len(needs), len(needs) + len(arrays)

    def wrapped(*refs):
        numbers = {need: ref for need, ref in zip(needs, refs)}
        body(Numbers(numbers), *refs[count:ends], *refs[ends + len(after) :])

    return pl.pallas_call(
        wrapped,
        out_shape=shapes,
        in_specs=[pl.BlockSpec(memory_space=pltpu.SMEM)] * count
        + [spaces or whole] * len(arrays)
        + [anywhere] * len(after),
        out_specs=jax.tree.map(lambda _: outs or whole, shapes),
        scratch_shapes=scratch,
        compiler_params=pltpu.CompilerParams(vmem_limit_bytes=16 * 1024 * 1024),
        cost_estimate=pl.CostEstimate(flops=flops, bytes_accessed=total, transcendentals=0),
        name=name,
    )(*(info[need] for need in needs), *arrays, *after)


class Numbers:
    def __init__(self, refs):
        self.refs = refs

    def __getitem__(self, need):
        return self.refs[need][0]


def dot(a, b):
    return jnp.dot(a, b, preferred_element_type=F32)


def dot_nt(a, b, precision=None):
    return lax.dot_general(a, b, NT, precision=precision, preferred_element_type=F32)


def unit_of(size):
    return (
        lax.broadcasted_iota(jnp.int32, (size, size), 0) == lax.broadcasted_iota(jnp.int32, (size, size), 1)
    ).astype(F32)


def total_of(value):
    return jnp.sum(jnp.sum(value, axis=1, keepdims=True), axis=0, keepdims=True)


def pack_maps(info, voxel_maps):
    layers, plane, chans = voxel_maps.shape

    def body(_, src, out):
        unit = unit_of(chans).astype(BF16)
        for x in range(layers):
            out[x * chans : (x + 1) * chans, :] = dot_nt(unit, src[x].astype(BF16)).astype(BF16)

    return call(body, shape((layers * chans, plane), BF16), info, [], [voxel_maps], name="pack_maps")


def pick_tables(info, table_y, table_z):
    def body(info_ref, all_y, all_z, out_y, out_z, sem_y, sem_z):
        copies = [
            pltpu.make_async_copy(all_y.at[info_ref[PLACE_Y]], out_y, sem_y),
            pltpu.make_async_copy(all_z.at[info_ref[PLACE_Z]], out_z, sem_z),
        ]
        for copy in copies:
            copy.start()
        for copy in copies:
            copy.wait()

    shapes = (shape(table_y.shape[1:], BF16), shape(table_z.shape[1:], BF16))
    return call(
        body,
        shapes,
        info,
        [PLACE_Y, PLACE_Z],
        [table_y, table_z],
        name="pick_tables",
        spaces=pl.BlockSpec(memory_space=pl.ANY),
        scratch=(pltpu.SemaphoreType.DMA, pltpu.SemaphoreType.DMA),
    )


def send_faces(info_ref, odd, field, face, first=None, second=None):
    plane = field.shape[1]
    low, high = slice(0, face), slice(plane - face, plane)

    def write(of_first, of_second):
        for ref, lanes in ((first, of_first), (second, of_second)):
            if ref is not None:
                ref[...] = field[:, lanes].astype(ref.dtype)

    pl.when(info_ref[odd] == 0)(lambda: write(high, low))
    pl.when(info_ref[odd] != 0)(lambda: write(low, high))


def cut_face(info, field, face):
    def body(info_ref, field_ref, out):
        send_faces(info_ref, ODD_Y, field_ref, face, second=out)

    shapes = shape((field.shape[0], face), field.dtype)
    return call(body, shapes, info, [ODD_Y], [field], flops=10**9, name="cut_face")


def swapped_dot(info_ref, odd, first, middle, second, weights, rows=slice(None)):
    width = first.shape[1]
    end = weights.shape[0] - width
    even = info_ref[odd] == 0

    def at(when_even, when_odd):
        return weights[pl.ds(pl.multiple_of(jnp.where(even, when_even, when_odd), width), width), :]

    total = dot(first[rows, :], at(end, 0)) + dot(second[rows, :], at(0, end))
    for piece in middle:
        total = total + dot(piece[rows, :], weights[width : width + piece.shape[1], :])
    return total


def mix_layers(info, coefs, chans, sources, sums, out_types, face=0, after=()):
    rows, plane = sources[0].shape
    outs = len(out_types)
    base = len(sources)
    tall, wide = 16, 128

    def body(info_ref, *refs):
        ins, adds, results = refs[:base], refs[base : base + len(sums)], refs[base + len(sums) :]

        def run(tables):
            layers = tables[0][0].shape[0]
            for r in range(0, chans, tall):
                for c in range(0, plane, wide):
                    tiles = [
                        [
                            src[s * chans + r : s * chans + r + tall, c : c + wide].astype(F32)
                            for s in range(layers)
                        ]
                        for src in ins
                    ]
                    for o in range(outs):
                        for x in range(layers):
                            at = slice(x * chans + r, x * chans + r + tall)
                            total = adds[o][at, c : c + wide] if adds else None
                            for tile, table in zip(tiles, tables[o]):
                                for s in range(layers):
                                    weight = float(table[x, s])
                                    if weight != 0.0:
                                        term = tile[s] * weight
                                        total = term if total is None else total + term
                            if total is None:
                                total = jnp.zeros((tall, wide), F32)
                            results[o][at, c : c + wide] = total.astype(results[o].dtype)

        if len(coefs) == 1:
            run(coefs[0])
        else:
            for v in range(len(coefs)):
                pl.when(info_ref[PLACE_X] == v)(functools.partial(run, coefs[v]))
        if face:
            send_faces(info_ref, ODD_Y, results[0], face, first=results[outs])

    shapes = tuple(shape((rows, plane), t) for t in out_types)
    if face:
        shapes += (shape((rows, face), out_types[0]),)
    needs = ([PLACE_X] if len(coefs) > 1 else []) + ([ODD_Y] if face else [])
    return call(body, shapes, info, needs, [*sources, *sums], name="mix_layers", after=after)


def filter_lanes(info, first, middle, second, table):
    def body(info_ref, first_ref, middle_ref, second_ref, weights, out):
        out[...] = swapped_dot(info_ref, ODD_Y, first_ref, [middle_ref], second_ref, weights)

    shapes = shape((first.shape[0], table.shape[1]), F32)
    return call(body, shapes, info, [ODD_Y], [first, middle, second, table], name="filter_lanes")


def filter_faces(info, first, middle, second, table, below=(), after=()):
    rows, face = first.shape[0], table.shape[1] // 2
    extra = below[0].shape[0] if below else 0

    def body(info_ref, first_ref, middle_ref, second_ref, weights, *refs):
        outs = refs[-2:]
        total = swapped_dot(info_ref, ODD_Y, first_ref, [middle_ref], second_ref, weights)
        send_faces(info_ref, ODD_Z, total, face, *(out.at[:rows, :] for out in outs))
        for src, out in zip(refs[:-2], outs):
            out[rows:, :] = src[...]

    shapes = (shape((rows + extra, face), BF16),) * 2
    arrays = [first, middle, second, table, *below]
    return call(body, shapes, info, [ODD_Y, ODD_Z], arrays, name="filter_faces", after=after)


def filter_sent(info, sent, table):
    def body(info_ref, first_ref, second_ref, weights, out):
        width = first_ref.shape[1]
        even = info_ref[ODD_Z] == 0
        of_first = pl.multiple_of(jnp.where(even, 2 * width, width), width)
        of_second = pl.multiple_of(jnp.where(even, width, 2 * width), width)
        total = dot(first_ref[...], weights[pl.ds(of_first, width), :])
        out[...] = total + dot(second_ref[...], weights[pl.ds(of_second, width), :])

    shapes = shape((sent[0].shape[0], table.shape[1]), F32)
    return call(body, shapes, info, [ODD_Z], [*sent, table], name="filter_sent")


def live_lanes(info_ref, layer, dims, size_y, size_z):
    row = layer * size_y + lax.broadcasted_iota(jnp.int32, dims, 1) // size_z
    return row < info_ref[COUNT]


def courses_of(info, acc, first, second, table, bold, chans, size_y, size_z):
    frames = bold.shape[1]
    plane = size_y * size_z
    layers = bold.shape[0] // plane

    def body(info_ref, start, first_ref, second_ref, weights, frames_ref, out):
        total = jnp.zeros((chans, frames), F32)
        for x in range(layers):
            rows = slice(x * chans, (x + 1) * chans)
            value = start[rows, :] + swapped_dot(info_ref, ODD_Z, first_ref, [], second_ref, weights, rows)
            keep = live_lanes(info_ref, x, value.shape, size_y, size_z)
            value = jnp.where(keep, value, 0.0).astype(BF16)
            total = total + dot(value, frames_ref[x * plane : (x + 1) * plane, :])
        out[...] = total

    arrays = [acc, first, second, table, bold]
    shapes = shape((chans, frames), F32)
    return call(body, shapes, info, [COUNT, ODD_Z], arrays, flops=10**9, name="courses_of")


def write_gradient(info_ref, courses, frames_ref, out, chans, size_y, size_z):
    plane = size_y * size_z
    for x in range(frames_ref.shape[0] // plane):
        value = dot_nt(courses, frames_ref[x * plane : (x + 1) * plane, :])
        keep = live_lanes(info_ref, x, value.shape, size_y, size_z)
        out[x * chans : (x + 1) * chans, :] = jnp.where(keep, value, 0.0).astype(BF16)


def first_gradient(info, sums, bold, chans, size_y, size_z):
    cells, frames = bold.shape

    def body(info_ref, sums_ref, frames_ref, out, half_ref):
        courses = sums_ref[...].astype(BF16)
        half_ref[...] = courses
        write_gradient(info_ref, courses, frames_ref, out, chans, size_y, size_z)

    shapes = (shape((cells * chans // (size_y * size_z), size_y * size_z), BF16), shape((chans, frames), BF16))
    return call(body, shapes, info, [COUNT], [sums, bold], flops=10**9, name="first_gradient")


def fade_of(courses):
    chans = courses.shape[0]
    wide = courses.astype(F32)
    scale = (0.5 * chans) / total_of(wide * wide)
    return unit_of(chans) - dot_nt(courses, courses) * scale


def first_fade(info, half1):
    chans, frames = half1.shape

    def body(_, half_ref, kept_ref, fade_ref):
        fade = fade_of(half_ref[...])
        fade_ref[...] = fade
        kept_ref[...] = jnp.dot(fade, half_ref[...].astype(F32), precision=FULL, preferred_element_type=F32)

    shapes = (shape((chans, frames), F32), shape((chans, chans), F32))
    return call(body, shapes, info, [], [half1], name="first_fade")


def second_gradient(info, change, half1, kept, bold, chans, size_y, size_z, all_cells):
    cells, frames = bold.shape

    def body(info_ref, change_ref, half1_ref, kept_ref, frames_ref, out, half_ref, scale_ref):
        change = change_ref[...]
        energy = jnp.maximum(total_of(half1_ref[...].astype(F32) * change), 0.0) * (1.0 / all_cells)
        scale = 0.5 * lax.rsqrt(energy + 1e-06)
        scale_ref[...] = scale
        courses = (kept_ref[...] + scale * change).astype(BF16)
        half_ref[...] = courses
        write_gradient(info_ref, courses, frames_ref, out, chans, size_y, size_z)

    shapes = (
        shape((cells * chans // (size_y * size_z), size_y * size_z), BF16),
        shape((chans, frames), BF16),
        shape((1, 1), F32),
    )
    arrays = [change, half1, kept, bold]
    return call(body, shapes, info, [COUNT], arrays, flops=10**9, name="second_gradient")


def second_fade(info, half2, fade1, scale1, field, face):
    chans = half2.shape[0]
    rows, plane = field.shape

    def body(info_ref, half_ref, fade_ref, scale_ref, field_ref, fades_ref, out, first):
        fade = fade_of(half_ref[...])
        fades_ref[...] = jnp.dot(fade, fade_ref[...], precision=FULL, preferred_element_type=F32)
        weights = fade * scale_ref[...]
        high = weights.astype(BF16)
        low = (weights - high.astype(F32)).astype(BF16)
        for x in range(rows // chans):
            at = slice(x * chans, (x + 1) * chans)
            block = field_ref[at, :]
            out[at, :] = (dot(high, block) + dot(low, block)).astype(BF16)
        send_faces(info_ref, ODD_Y, out, face, first=first)

    shapes = (
        shape((chans, chans), F32),
        shape((rows, plane), BF16),
        shape((rows, face), BF16),
    )
    arrays = [half2, fade1, scale1, field]
    return call(body, shapes, info, [ODD_Y], arrays, flops=10**9, name="second_fade")


def faded_maps(info, voxel_maps, fades):
    layers, plane, chans = voxel_maps.shape

    def body(_, maps_ref, fades_ref, out):
        for x in range(layers):
            out[x] = dot_nt(maps_ref[x], fades_ref[...], FULL)

    shapes = shape((layers, plane, chans), F32)
    return call(body, shapes, info, [], [voxel_maps, fades], flops=10**9, name="faded_maps")


def whole_gradient(info, acc, first, second, table):
    def body(info_ref, start, first_ref, second_ref, weights, out):
        value = start[...] + swapped_dot(info_ref, ODD_Z, first_ref, [], second_ref, weights)
        out[...] = value.astype(BF16)

    arrays = [acc, first, second, table]
    return call(body, shape(acc.shape, BF16), info, [ODD_Z], arrays, name="whole_gradient")


def gradient_energy(info, acc, first, second, table, peers, after=()):
    rows, plane = acc.shape
    tall = min(rows, 128)

    def body(info_ref, start, first_ref, second_ref, weights, out, energy):
        total = jnp.zeros((tall, plane), F32)
        for r in range(0, rows, tall):
            at = slice(r, r + tall)
            value = start[at, :] + swapped_dot(info_ref, ODD_Z, first_ref, [], second_ref, weights, at)
            total = total + value * value
            out[at, :] = value
        energy[...] = jnp.broadcast_to(total_of(total).reshape(1, 1, 1), energy.shape)

    shapes = (shape((rows, plane), F32), shape((peers, 1, 128), F32))
    arrays = [acc, first, second, table]
    return call(body, shapes, info, [ODD_Z], arrays, name="gradient_energy", after=after)


def final_maps(info, energies, base, acc, first, second, table, grad, all_cells):
    layers, plane, chans = base.shape
    rows = acc.shape[0]
    peers = energies.shape[0]

    def body(info_ref, energies_ref, base_ref, start, first_ref, second_ref, weights, grad_ref, out, held, sems):
        energy = energies_ref[0]
        for d in range(1, peers):
            energy = energy + energies_ref[d]
        scale = 0.5 * lax.rsqrt(energy[:, :1] * (1.0 / all_cells) + 1e-06)
        copies = []
        for x in range(layers):
            at = slice(x * chans, (x + 1) * chans)
            below = slice(rows + x * chans, rows + (x + 1) * chans)
            value = start[at, :] + swapped_dot(info_ref, ODD_Z, first_ref, [], second_ref, weights, below)
            held[x] = base_ref[x] + (value + scale * grad_ref[at, :]).T
            copies.append(pltpu.make_async_copy(held.at[x], out.at[x], sems.at[x]))
            copies[-1].start()
        for copy in copies:
            copy.wait()

    return call(
        body,
        shape(base.shape, F32),
        info,
        [ODD_Z],
        [energies, base, acc, first, second, table, grad],
        name="final_maps",
        outs=pl.BlockSpec(memory_space=pl.ANY),
        scratch=(pltpu.VMEM(base.shape, F32), pltpu.SemaphoreType.DMA((layers,))),
    )


def swapped(first, second, axis, inner_first=False):
    peers = lax.axis_size(axis)
    got = {}
    for start in (1, 0) if inner_first else (0, 1):
        pairs = [(i, i + 1) for i in range(start, peers - 1, 2)]
        pairs += [(j, i) for i, j in pairs]
        got[start] = lax.ppermute((first, second)[start], axis, pairs)
    return got[0], got[1]


def shifted(lower, upper, axis):
    peers = lax.axis_size(axis)
    up = [(i, i + 1) for i in range(peers - 1)]
    down = [(j, i) for i, j in up]
    return lax.ppermute(upper, axis, up), lax.ppermute(lower, axis, down)


def exchanged(parts):
    return lax.all_to_all(parts, AXES, 0, 0, tiled=True)


def hypercube_sum(value):
    rounds = []
    for axis in AXES:
        peers = lax.axis_size(axis)
        if peers & (peers - 1):
            return lax.psum(value, AXES)
        if axis == "gz" and peers == 4:
            rounds.append((axis, (1, 2, 3)))
        else:
            rounds += [(axis, (1 << b,)) for b in range(peers.bit_length() - 1)]
    for axis, masks in rounds:
        value = lax.reduce_precision(value, 8, 7)
        sent = value.astype(BF16)
        got = []
        for mask in masks:
            pairs = [(i, i ^ mask) for i in range(lax.axis_size(axis))]
            got.append(lax.ppermute(sent, axis, pairs).astype(F32))
        value = value + got[0]
        if len(got) == 3:
            value = value + (got[1] + got[2])
    return value


def per_device(bold_data, spatial_maps, live_blocks):
    chans, size_x, size_y, size_z = spatial_maps.shape
    frames = bold_data.shape[3]
    plane = size_y * size_z
    parts_x, parts_y, parts_z = (lax.axis_size(a) for a in AXES)
    peers = parts_x * parts_y * parts_z
    places = [lax.axis_index(a).astype(jnp.int32) for a in AXES]
    numbers = [*places, places[1] % 2, places[2] % 2, live_blocks]
    info = [number.reshape(1) for number in numbers]
    bold = bold_data.reshape(size_x * plane, frames)
    voxel_maps = jnp.transpose(spatial_maps, (1, 2, 3, 0)).reshape(size_x, plane, chans)
    all_cells = float(chans * size_x * plane * peers)

    win_x, win_y, win_z = (inner_window(s) for s in (size_x, size_y, size_z))
    unit_y, unit_z = np.eye(size_y), np.eye(size_z)
    ends = np.concatenate([np.kron(win_y.T, unit_z[:, :RADIUS]), np.kron(win_y.T, unit_z[:, -RADIUS:])], 1)
    table_ends = jnp.asarray(half(ends))
    table_own = jnp.asarray(half(np.kron(win_y.T, win_z[:, RADIUS:-RADIUS].T)))
    table_z = jnp.asarray(
        half(np.concatenate([np.kron(unit_y, win_z[:, :RADIUS].T), np.kron(unit_y, win_z[:, -RADIUS:].T)]))
    )
    face_y = RADIUS * size_z

    reach = 2 * RADIUS
    twice = parts_x == 2 and size_y == reach and size_z == 2 * reach
    full_x = band(size_x * parts_x)
    own_x = [slice(p * size_x, (p + 1) * size_x) for p in range(parts_x)]

    def along_x(block, matrices, beside=(), face=face_y):
        kinds = [BF16] * len(matrices)
        if parts_x == 2:
            mine = [[[m[own_x[p], own_x[p]]] for m in matrices] for p in range(2)]
            other = [[[m[own_x[p], own_x[1 - p]]] for m in matrices] for p in range(2)]
            got = lax.ppermute(block, "gx", [(0, 1), (1, 0)])
            sums = mix_layers(info, mine, chans, [block], [], [F32] * len(matrices))
            return mix_layers(info, other, chans, [got], list(sums), kinds, face=face, after=beside)
        depth = RADIUS * chans
        before, after = shifted(block[:depth], block[-depth:], "gx")
        rest = jnp.zeros((block.shape[0] - depth, plane), BF16)
        before, after = jnp.concatenate([rest, before]), jnp.concatenate([after, rest])
        tables = []
        for lo in (-size_x, 0, size_x):
            columns = np.arange(size_x) + lo + RADIUS
            inside = (columns >= 0) & (columns < win_x.shape[1])
            tables.append(np.where(inside[None], win_x[:, np.clip(columns, 0, win_x.shape[1] - 1)], 0.0))
        return mix_layers(info, [[tables]], chans, [before, block, after], [], kinds, face=face_y)

    def along_y(field, first):
        return swapped(first, cut_face(info, field, face_y), "gy", inner_first=True)

    def along_rest(field, first):
        first, second = along_y(field, first)
        ends = swapped(*filter_faces(info, first, field, second, table_ends), "gz")
        return filter_lanes(info, first, field, second, table_own), *ends

    def all_courses(acc, first, second, table):
        return hypercube_sum(courses_of(info, acc, first, second, table, bold, chans, size_y, size_z))

    plain = pack_maps(info, voxel_maps)
    acc, first, second = along_rest(*along_x(plain, [full_x]))
    courses1 = all_courses(acc, first, second, table_z)
    raw1, half1 = first_gradient(info, courses1, bold, chans, size_y, size_z)
    kept, fade1 = first_fade(info, half1)
    if twice:
        square_y = windows(np.linalg.matrix_power(band(size_y * parts_y), 2), size_y, parts_y, reach)
        square_z = windows(np.linalg.matrix_power(band(size_z * parts_z), 2), size_z, parts_z, reach)
        ordered = np.concatenate([unit_z[:, :reach], unit_z[:, reach:]], 1).reshape(size_z, 2, reach)
        tables_y = np.stack([
            np.concatenate([np.kron(w.T, ordered[:, h]) for h in range(2)], 1) for w in square_y
        ])
        tables_z = np.stack([
            np.concatenate([np.kron(unit_y, w[:, h * reach : (h + 1) * reach].T) for h in range(4)])
            for w in square_z
        ])
        table_y2, table_z2 = pick_tables(info, jnp.asarray(half(tables_y)), jnp.asarray(half(tables_z)))
        twice_x, once_x = along_x(raw1, [full_x @ full_x, full_x], [kept], 0)
        first, second = swapped(twice_x, twice_x, "gy", inner_first=True)
        sent = filter_faces(info, first, twice_x, second, table_y2)
        first, second = swapped(*sent, "gz")
        change = all_courses(filter_sent(info, sent, table_z2), first, second, table_z2)
    else:
        once_x, face1 = along_x(raw1, [full_x])
        again = whole_gradient(info, *along_rest(once_x, face1), table_z)
        acc2, first, second = along_rest(*along_x(again, [full_x]))
        change = all_courses(acc2, first, second, table_z)

    raw2, half2, scale1 = second_gradient(
        info, change, half1, kept, bold, chans, size_y, size_z, all_cells
    )
    fades, field1, face1 = second_fade(info, half2, fade1, scale1, once_x, face_y)
    first1, second1 = along_y(field1, face1)
    below = filter_faces(info, first1, field1, second1, table_ends)
    acc1 = filter_lanes(info, first1, field1, second1, table_own)
    base = faded_maps(info, voxel_maps, fades)

    field2, face2 = along_x(raw2, [full_x], [base])
    first2, second2 = along_y(field2, face2)
    ends = swapped(*filter_faces(info, first2, field2, second2, table_ends, below, [acc1]), "gz")
    acc2 = filter_lanes(info, first2, field2, second2, table_own)
    grad2, energies = gradient_energy(info, acc2, *ends, table_z, peers)
    maps = final_maps(info, exchanged(energies), base, acc1, *ends, table_z, grad2, all_cells)
    maps = maps.reshape(size_x, size_y, size_z, chans)
    return (jnp.transpose(maps, (3, 0, 1, 2)), half2)


def solution(mesh):
    return jax.shard_map(
        per_device,
        mesh=mesh,
        in_specs=(P("gx", "gy", "gz", None), P(None, "gx", "gy", "gz"), P("gx", "gy", "gz")),
        out_specs=(P(None, "gx", "gy", "gz"), P()),
        check_vma=False,
    )
```

```python
import functools
import math

import jax
import jax.numpy as jnp
import ml_dtypes
import numpy as np
from jax import lax
from jax.experimental import pallas as pl
from jax.experimental.pallas import tpu as pltpu
from jax.sharding import PartitionSpec as P

RADIUS = 8
F32 = jnp.float32
BF16 = jnp.bfloat16
AXES = ("gx", "gy", "gz")


def band(length):
    total = sum(math.exp(-float(d * d) / 32.0) for d in range(-RADIUS, RADIUS + 1))
    gap = np.abs(np.arange(length)[:, None] - np.arange(length)[None, :])
    return np.where(gap <= RADIUS, np.exp(-(gap.astype(np.float64) ** 2) / 32.0) / total, 0.0)


def windows(matrix, size, parts, reach):
    padded = np.pad(matrix, ((0, 0), (reach, reach)))
    return np.stack(
        [padded[p * size : (p + 1) * size, p * size : (p + 1) * size + 2 * reach] for p in range(parts)]
    )


def half(array):
    return np.asarray(array, dtype=ml_dtypes.bfloat16)


def inner_window(size):
    return windows(band(3 * size), size, 3, RADIUS)[1]


PLACE_X, PLACE_Y, PLACE_Z, ODD_Y, ODD_Z, COUNT = range(6)
NT = (((1,), (1,)), ((), ()))
FULL = lax.Precision.HIGHEST


def shape(dims, kind):
    return jax.ShapeDtypeStruct(dims, kind)


def call(body, shapes, info, needs, arrays, flops=10**8, name=None, spaces=None, outs=None, scratch=(), after=()):
    total = sum(a.size * a.dtype.itemsize for a in arrays)
    whole, anywhere = pl.BlockSpec(memory_space=pltpu.VMEM), pl.BlockSpec(memory_space=pl.ANY)
    count, ends = len(needs), len(needs) + len(arrays)

    def wrapped(*refs):
        numbers = {need: ref for need, ref in zip(needs, refs)}
        body(Numbers(numbers), *refs[count:ends], *refs[ends + len(after) :])

    return pl.pallas_call(
        wrapped,
        out_shape=shapes,
        in_specs=[pl.BlockSpec(memory_space=pltpu.SMEM)] * count
        + [spaces or whole] * len(arrays)
        + [anywhere] * len(after),
        out_specs=jax.tree.map(lambda _: outs or whole, shapes),
        scratch_shapes=scratch,
        compiler_params=pltpu.CompilerParams(vmem_limit_bytes=16 * 1024 * 1024),
        cost_estimate=pl.CostEstimate(flops=flops, bytes_accessed=total, transcendentals=0),
        name=name,
    )(*(info[need] for need in needs), *arrays, *after)


class Numbers:
    def __init__(self, refs):
        self.refs = refs

    def __getitem__(self, need):
        return self.refs[need][0]


def dot(a, b):
    return jnp.dot(a, b, preferred_element_type=F32)


def dot_nt(a, b, precision=None):
    return lax.dot_general(a, b, NT, precision=precision, preferred_element_type=F32)


def unit_of(size):
    return (
        lax.broadcasted_iota(jnp.int32, (size, size), 0) == lax.broadcasted_iota(jnp.int32, (size, size), 1)
    ).astype(F32)


def total_of(value):
    return jnp.sum(jnp.sum(value, axis=1, keepdims=True), axis=0, keepdims=True)


def pack_maps(info, voxel_maps):
    layers, plane, chans = voxel_maps.shape

    def body(_, src, out):
        unit = unit_of(chans).astype(BF16)
        for x in range(layers):
            out[x * chans : (x + 1) * chans, :] = dot_nt(unit, src[x].astype(BF16)).astype(BF16)

    return call(body, shape((layers * chans, plane), BF16), info, [], [voxel_maps], name="pack_maps")


def pick_tables(info, table_y, table_z):
    def body(info_ref, all_y, all_z, out_y, out_z, sem_y, sem_z):
        copies = [
            pltpu.make_async_copy(all_y.at[info_ref[PLACE_Y]], out_y, sem_y),
            pltpu.make_async_copy(all_z.at[info_ref[PLACE_Z]], out_z, sem_z),
        ]
        for copy in copies:
            copy.start()
        for copy in copies:
            copy.wait()

    shapes = (shape(table_y.shape[1:], BF16), shape(table_z.shape[1:], BF16))
    return call(
        body,
        shapes,
        info,
        [PLACE_Y, PLACE_Z],
        [table_y, table_z],
        name="pick_tables",
        spaces=pl.BlockSpec(memory_space=pl.ANY),
        scratch=(pltpu.SemaphoreType.DMA, pltpu.SemaphoreType.DMA),
    )


def send_faces(info_ref, odd, field, face, first=None, second=None):
    plane = field.shape[1]
    low, high = slice(0, face), slice(plane - face, plane)

    def write(of_first, of_second):
        for ref, lanes in ((first, of_first), (second, of_second)):
            if ref is not None:
                ref[...] = field[:, lanes].astype(ref.dtype)

    pl.when(info_ref[odd] == 0)(lambda: write(high, low))
    pl.when(info_ref[odd] != 0)(lambda: write(low, high))


def cut_face(info, field, face):
    def body(info_ref, field_ref, out):
        send_faces(info_ref, ODD_Y, field_ref, face, second=out)

    shapes = shape((field.shape[0], face), field.dtype)
    return call(body, shapes, info, [ODD_Y], [field], flops=10**9, name="cut_face")


def swapped_dot(info_ref, odd, first, middle, second, weights, rows=slice(None)):
    width = first.shape[1]
    end = weights.shape[0] - width
    even = info_ref[odd] == 0

    def at(when_even, when_odd):
        return weights[pl.ds(pl.multiple_of(jnp.where(even, when_even, when_odd), width), width), :]

    total = dot(first[rows, :], at(end, 0)) + dot(second[rows, :], at(0, end))
    for piece in middle:
        total = total + dot(piece[rows, :], weights[width : width + piece.shape[1], :])
    return total


def mix_layers(info, coefs, chans, sources, sums, out_types, face=0, after=()):
    rows, plane = sources[0].shape
    outs = len(out_types)
    base = len(sources)
    tall, wide = 16, 128

    def body(info_ref, *refs):
        ins, adds, results = refs[:base], refs[base : base + len(sums)], refs[base + len(sums) :]

        def run(tables):
            layers = tables[0][0].shape[0]
            for r in range(0, chans, tall):
                for c in range(0, plane, wide):
                    tiles = [
                        [
                            src[s * chans + r : s * chans + r + tall, c : c + wide].astype(F32)
                            for s in range(layers)
                        ]
                        for src in ins
                    ]
                    for o in range(outs):
                        for x in range(layers):
                            at = slice(x * chans + r, x * chans + r + tall)
                            total = adds[o][at, c : c + wide] if adds else None
                            for tile, table in zip(tiles, tables[o]):
                                for s in range(layers):
                                    weight = float(table[x, s])
                                    if weight != 0.0:
                                        term = tile[s] * weight
                                        total = term if total is None else total + term
                            if total is None:
                                total = jnp.zeros((tall, wide), F32)
                            results[o][at, c : c + wide] = total.astype(results[o].dtype)

        if len(coefs) == 1:
            run(coefs[0])
        else:
            for v in range(len(coefs)):
                pl.when(info_ref[PLACE_X] == v)(functools.partial(run, coefs[v]))
        if face:
            send_faces(info_ref, ODD_Y, results[0], face, first=results[outs])

    shapes = tuple(shape((rows, plane), t) for t in out_types)
    if face:
        shapes += (shape((rows, face), out_types[0]),)
    needs = ([PLACE_X] if len(coefs) > 1 else []) + ([ODD_Y] if face else [])
    return call(body, shapes, info, needs, [*sources, *sums], name="mix_layers", after=after)


def filter_lanes(info, first, middle, second, table):
    def body(info_ref, first_ref, middle_ref, second_ref, weights, out):
        out[...] = swapped_dot(info_ref, ODD_Y, first_ref, [middle_ref], second_ref, weights)

    shapes = shape((first.shape[0], table.shape[1]), F32)
    return call(body, shapes, info, [ODD_Y], [first, middle, second, table], name="filter_lanes")


def filter_faces(info, first, middle, second, table, below=(), after=()):
    rows, face = first.shape[0], table.shape[1] // 2
    extra = below[0].shape[0] if below else 0

    def body(info_ref, first_ref, middle_ref, second_ref, weights, *refs):
        outs = refs[-2:]
        total = swapped_dot(info_ref, ODD_Y, first_ref, [middle_ref], second_ref, weights)
        send_faces(info_ref, ODD_Z, total, face, *(out.at[:rows, :] for out in outs))
        for src, out in zip(refs[:-2], outs):
            out[rows:, :] = src[...]

    shapes = (shape((rows + extra, face), BF16),) * 2
    arrays = [first, middle, second, table, *below]
    return call(body, shapes, info, [ODD_Y, ODD_Z], arrays, name="filter_faces", after=after)


def filter_sent(info, sent, table):
    def body(info_ref, first_ref, second_ref, weights, out):
        width = first_ref.shape[1]
        even = info_ref[ODD_Z] == 0
        of_first = pl.multiple_of(jnp.where(even, 2 * width, width), width)
        of_second = pl.multiple_of(jnp.where(even, width, 2 * width), width)
        total = dot(first_ref[...], weights[pl.ds(of_first, width), :])
        out[...] = total + dot(second_ref[...], weights[pl.ds(of_second, width), :])

    shapes = shape((sent[0].shape[0], table.shape[1]), F32)
    return call(body, shapes, info, [ODD_Z], [*sent, table], name="filter_sent")


def live_lanes(info_ref, layer, dims, size_y, size_z):
    row = layer * size_y + lax.broadcasted_iota(jnp.int32, dims, 1) // size_z
    return row < info_ref[COUNT]


def courses_of(info, acc, first, second, table, bold, chans, size_y, size_z):
    frames = bold.shape[1]
    plane = size_y * size_z
    layers = bold.shape[0] // plane

    def body(info_ref, start, first_ref, second_ref, weights, frames_ref, mine, other):
        total = jnp.zeros((chans, frames), F32)
        for x in range(layers):
            rows = slice(x * chans, (x + 1) * chans)
            value = start[rows, :] + swapped_dot(info_ref, ODD_Z, first_ref, [], second_ref, weights, rows)
            keep = live_lanes(info_ref, x, value.shape, size_y, size_z)
            value = jnp.where(keep, value, 0.0).astype(BF16)
            total = total + dot(value, frames_ref[x * plane : (x + 1) * plane, :])
        part = chans // 2

        @pl.when(info_ref[ODD_Y] == 0)
        def _():
            mine[...] = total[:part]
            other[...] = total[part:].astype(BF16)

        @pl.when(info_ref[ODD_Y] != 0)
        def _():
            mine[...] = total[part:]
            other[...] = total[:part].astype(BF16)

    arrays = [acc, first, second, table, bold]
    shapes = (shape((chans // 2, frames), F32), shape((chans // 2, frames), BF16))
    return call(body, shapes, info, [COUNT, ODD_Y, ODD_Z], arrays, flops=10**9, name="courses_of")


def whole_courses(info_ref, mine, other):
    even = info_ref[ODD_Y] == 0
    mine, other = mine[...].astype(F32), other[...].astype(F32)
    return jnp.concatenate([jnp.where(even, mine, other), jnp.where(even, other, mine)], axis=0)


def write_gradient(info_ref, courses, frames_ref, out, chans, size_y, size_z):
    plane = size_y * size_z
    for x in range(frames_ref.shape[0] // plane):
        value = dot_nt(courses, frames_ref[x * plane : (x + 1) * plane, :])
        keep = live_lanes(info_ref, x, value.shape, size_y, size_z)
        out[x * chans : (x + 1) * chans, :] = jnp.where(keep, value, 0.0).astype(BF16)


def first_gradient(info, halves, bold, chans, size_y, size_z):
    cells, frames = bold.shape

    def body(info_ref, mine, other, frames_ref, out, half_ref):
        courses = whole_courses(info_ref, mine, other).astype(BF16)
        half_ref[...] = courses
        write_gradient(info_ref, courses, frames_ref, out, chans, size_y, size_z)

    shapes = (shape((cells * chans // (size_y * size_z), size_y * size_z), BF16), shape((chans, frames), BF16))
    return call(body, shapes, info, [COUNT, ODD_Y], [*halves, bold], flops=10**9, name="first_gradient")


def fade_of(courses):
    chans = courses.shape[0]
    wide = courses.astype(F32)
    scale = (0.5 * chans) / total_of(wide * wide)
    return unit_of(chans) - dot_nt(courses, courses) * scale


def first_fade(info, half1):
    chans, frames = half1.shape

    def body(_, half_ref, kept_ref, fade_ref):
        fade = fade_of(half_ref[...])
        fade_ref[...] = fade
        kept_ref[...] = jnp.dot(fade, half_ref[...].astype(F32), precision=FULL, preferred_element_type=F32)

    shapes = (shape((chans, frames), F32), shape((chans, chans), F32))
    return call(body, shapes, info, [], [half1], name="first_fade")


def second_gradient(info, halves, half1, kept, bold, chans, size_y, size_z, all_cells):
    cells, frames = bold.shape

    def body(info_ref, mine, other, half1_ref, kept_ref, frames_ref, out, half_ref, scale_ref):
        change = whole_courses(info_ref, mine, other)
        energy = jnp.maximum(total_of(half1_ref[...].astype(F32) * change), 0.0) * (1.0 / all_cells)
        scale = 0.5 * lax.rsqrt(energy + 1e-06)
        scale_ref[...] = scale
        courses = (kept_ref[...] + scale * change).astype(BF16)
        half_ref[...] = courses
        write_gradient(info_ref, courses, frames_ref, out, chans, size_y, size_z)

    shapes = (
        shape((cells * chans // (size_y * size_z), size_y * size_z), BF16),
        shape((chans, frames), BF16),
        shape((1, 1), F32),
    )
    arrays = [*halves, half1, kept, bold]
    return call(body, shapes, info, [COUNT, ODD_Y], arrays, flops=10**9, name="second_gradient")


def second_fade(info, half2, fade1, scale1, field, face):
    chans = half2.shape[0]
    rows, plane = field.shape

    def body(info_ref, half_ref, fade_ref, scale_ref, field_ref, fades_ref, out, first):
        fade = fade_of(half_ref[...])
        fades_ref[...] = jnp.dot(fade, fade_ref[...], precision=FULL, preferred_element_type=F32)
        weights = fade * scale_ref[...]
        high = weights.astype(BF16)
        low = (weights - high.astype(F32)).astype(BF16)
        for x in range(rows // chans):
            at = slice(x * chans, (x + 1) * chans)
            block = field_ref[at, :]
            out[at, :] = (dot(high, block) + dot(low, block)).astype(BF16)
        send_faces(info_ref, ODD_Y, out, face, first=first)

    shapes = (
        shape((chans, chans), F32),
        shape((rows, plane), BF16),
        shape((rows, face), BF16),
    )
    arrays = [half2, fade1, scale1, field]
    return call(body, shapes, info, [ODD_Y], arrays, flops=10**9, name="second_fade")


def faded_maps(info, voxel_maps, fades):
    layers, plane, chans = voxel_maps.shape

    def body(_, maps_ref, fades_ref, out):
        for x in range(layers):
            out[x] = dot_nt(maps_ref[x], fades_ref[...], FULL)

    shapes = shape((layers, plane, chans), F32)
    return call(body, shapes, info, [], [voxel_maps, fades], flops=10**9, name="faded_maps")


def whole_gradient(info, acc, first, second, table):
    def body(info_ref, start, first_ref, second_ref, weights, out):
        value = start[...] + swapped_dot(info_ref, ODD_Z, first_ref, [], second_ref, weights)
        out[...] = value.astype(BF16)

    arrays = [acc, first, second, table]
    return call(body, shape(acc.shape, BF16), info, [ODD_Z], arrays, name="whole_gradient")


def gradient_energy(info, acc, first, second, table, peers, after=()):
    rows, plane = acc.shape
    tall = min(rows, 128)

    def body(info_ref, start, first_ref, second_ref, weights, out, energy):
        total = jnp.zeros((tall, plane), F32)
        for r in range(0, rows, tall):
            at = slice(r, r + tall)
            value = start[at, :] + swapped_dot(info_ref, ODD_Z, first_ref, [], second_ref, weights, at)
            total = total + value * value
            out[at, :] = value
        energy[...] = jnp.broadcast_to(total_of(total).reshape(1, 1, 1), energy.shape)

    shapes = (shape((rows, plane), F32), shape((peers, 1, 128), F32))
    arrays = [acc, first, second, table]
    return call(body, shapes, info, [ODD_Z], arrays, name="gradient_energy", after=after)


def final_maps(info, energies, base, acc, first, second, table, grad, all_cells):
    layers, plane, chans = base.shape
    rows = acc.shape[0]
    peers = energies.shape[0]

    def body(info_ref, energies_ref, base_ref, start, first_ref, second_ref, weights, grad_ref, out, held, sems):
        energy = energies_ref[0]
        for d in range(1, peers):
            energy = energy + energies_ref[d]
        scale = 0.5 * lax.rsqrt(energy[:, :1] * (1.0 / all_cells) + 1e-06)
        copies = []
        for x in range(layers):
            at = slice(x * chans, (x + 1) * chans)
            below = slice(rows + x * chans, rows + (x + 1) * chans)
            value = start[at, :] + swapped_dot(info_ref, ODD_Z, first_ref, [], second_ref, weights, below)
            held[x] = base_ref[x] + (value + scale * grad_ref[at, :]).T
            copies.append(pltpu.make_async_copy(held.at[x], out.at[x], sems.at[x]))
            copies[-1].start()
        for copy in copies:
            copy.wait()

    return call(
        body,
        shape(base.shape, F32),
        info,
        [ODD_Z],
        [energies, base, acc, first, second, table, grad],
        name="final_maps",
        outs=pl.BlockSpec(memory_space=pl.ANY),
        scratch=(pltpu.VMEM(base.shape, F32), pltpu.SemaphoreType.DMA((layers,))),
    )


def swapped(first, second, axis, inner_first=False):
    peers = lax.axis_size(axis)
    got = {}
    for start in (1, 0) if inner_first else (0, 1):
        pairs = [(i, i + 1) for i in range(start, peers - 1, 2)]
        pairs += [(j, i) for i, j in pairs]
        got[start] = lax.ppermute((first, second)[start], axis, pairs)
    return got[0], got[1]


def shifted(lower, upper, axis):
    peers = lax.axis_size(axis)
    up = [(i, i + 1) for i in range(peers - 1)]
    down = [(j, i) for i, j in up]
    return lax.ppermute(upper, axis, up), lax.ppermute(lower, axis, down)


def exchanged(parts):
    return lax.all_to_all(parts, AXES, 0, 0, tiled=True)


def hypercube_sum(mine, other):
    sizes = [lax.axis_size(axis) for axis in AXES]
    if any(size & (size - 1) for size in sizes) or sizes[1] < 2:
        odd = lax.axis_index("gy") % 2
        place = jnp.arange(2)[:, None, None] == odd
        sums = lax.psum(jnp.where(place, mine[None], other[None].astype(F32)), AXES).astype(BF16)
        return sums[odd], sums[1 - odd]

    def across(value, axis, bit):
        return lax.ppermute(value, axis, [(i, i ^ bit) for i in range(lax.axis_size(axis))])

    value = lax.reduce_precision(mine, 8, 7) + across(other, "gy", 1).astype(F32)
    for axis, size in zip(AXES, sizes):
        for step in range(axis == "gy", size.bit_length() - 1):
            value = lax.reduce_precision(value, 8, 7)
            value = value + across(value.astype(BF16), axis, 1 << step).astype(F32)
    mine = value.astype(BF16)
    return mine, across(mine, "gy", 1)


def per_device(bold_data, spatial_maps, live_blocks):
    chans, size_x, size_y, size_z = spatial_maps.shape
    frames = bold_data.shape[3]
    plane = size_y * size_z
    parts_x, parts_y, parts_z = (lax.axis_size(a) for a in AXES)
    peers = parts_x * parts_y * parts_z
    places = [lax.axis_index(a).astype(jnp.int32) for a in AXES]
    numbers = [*places, places[1] % 2, places[2] % 2, live_blocks]
    info = [number.reshape(1) for number in numbers]
    bold = bold_data.reshape(size_x * plane, frames)
    voxel_maps = jnp.transpose(spatial_maps, (1, 2, 3, 0)).reshape(size_x, plane, chans)
    all_cells = float(chans * size_x * plane * peers)

    win_x, win_y, win_z = (inner_window(s) for s in (size_x, size_y, size_z))
    unit_y, unit_z = np.eye(size_y), np.eye(size_z)
    ends = np.concatenate([np.kron(win_y.T, unit_z[:, :RADIUS]), np.kron(win_y.T, unit_z[:, -RADIUS:])], 1)
    table_ends = jnp.asarray(half(ends))
    table_own = jnp.asarray(half(np.kron(win_y.T, win_z[:, RADIUS:-RADIUS].T)))
    table_z = jnp.asarray(
        half(np.concatenate([np.kron(unit_y, win_z[:, :RADIUS].T), np.kron(unit_y, win_z[:, -RADIUS:].T)]))
    )
    face_y = RADIUS * size_z

    reach = 2 * RADIUS
    twice = parts_x == 2 and size_y == reach and size_z == 2 * reach
    full_x = band(size_x * parts_x)
    own_x = [slice(p * size_x, (p + 1) * size_x) for p in range(parts_x)]

    def along_x(block, matrices, beside=(), face=face_y):
        kinds = [BF16] * len(matrices)
        if parts_x == 2:
            mine = [[[m[own_x[p], own_x[p]]] for m in matrices] for p in range(2)]
            other = [[[m[own_x[p], own_x[1 - p]]] for m in matrices] for p in range(2)]
            got = lax.ppermute(block, "gx", [(0, 1), (1, 0)])
            sums = mix_layers(info, mine, chans, [block], [], [F32] * len(matrices))
            return mix_layers(info, other, chans, [got], list(sums), kinds, face=face, after=beside)
        depth = RADIUS * chans
        before, after = shifted(block[:depth], block[-depth:], "gx")
        rest = jnp.zeros((block.shape[0] - depth, plane), BF16)
        before, after = jnp.concatenate([rest, before]), jnp.concatenate([after, rest])
        tables = []
        for lo in (-size_x, 0, size_x):
            columns = np.arange(size_x) + lo + RADIUS
            inside = (columns >= 0) & (columns < win_x.shape[1])
            tables.append(np.where(inside[None], win_x[:, np.clip(columns, 0, win_x.shape[1] - 1)], 0.0))
        return mix_layers(info, [[tables]], chans, [before, block, after], [], kinds, face=face_y)

    def along_y(field, first):
        return swapped(first, cut_face(info, field, face_y), "gy", inner_first=True)

    def along_rest(field, first):
        first, second = along_y(field, first)
        ends = swapped(*filter_faces(info, first, field, second, table_ends), "gz")
        return filter_lanes(info, first, field, second, table_own), *ends

    def all_courses(acc, first, second, table):
        return hypercube_sum(*courses_of(info, acc, first, second, table, bold, chans, size_y, size_z))

    plain = pack_maps(info, voxel_maps)
    acc, first, second = along_rest(*along_x(plain, [full_x]))
    courses1 = all_courses(acc, first, second, table_z)
    raw1, half1 = first_gradient(info, courses1, bold, chans, size_y, size_z)
    kept, fade1 = first_fade(info, half1)
    if twice:
        square_y = windows(np.linalg.matrix_power(band(size_y * parts_y), 2), size_y, parts_y, reach)
        square_z = windows(np.linalg.matrix_power(band(size_z * parts_z), 2), size_z, parts_z, reach)
        ordered = np.concatenate([unit_z[:, :reach], unit_z[:, reach:]], 1).reshape(size_z, 2, reach)
        tables_y = np.stack([
            np.concatenate([np.kron(w.T, ordered[:, h]) for h in range(2)], 1) for w in square_y
        ])
        tables_z = np.stack([
            np.concatenate([np.kron(unit_y, w[:, h * reach : (h + 1) * reach].T) for h in range(4)])
            for w in square_z
        ])
        table_y2, table_z2 = pick_tables(info, jnp.asarray(half(tables_y)), jnp.asarray(half(tables_z)))
        twice_x, once_x = along_x(raw1, [full_x @ full_x, full_x], [kept], 0)
        first, second = swapped(twice_x, twice_x, "gy", inner_first=True)
        sent = filter_faces(info, first, twice_x, second, table_y2)
        first, second = swapped(*sent, "gz")
        change = all_courses(filter_sent(info, sent, table_z2), first, second, table_z2)
    else:
        once_x, face1 = along_x(raw1, [full_x])
        again = whole_gradient(info, *along_rest(once_x, face1), table_z)
        acc2, first, second = along_rest(*along_x(again, [full_x]))
        change = all_courses(acc2, first, second, table_z)

    raw2, half2, scale1 = second_gradient(
        info, change, half1, kept, bold, chans, size_y, size_z, all_cells
    )
    fades, field1, face1 = second_fade(info, half2, fade1, scale1, once_x, face_y)
    first1, second1 = along_y(field1, face1)
    below = filter_faces(info, first1, field1, second1, table_ends)
    acc1 = filter_lanes(info, first1, field1, second1, table_own)
    base = faded_maps(info, voxel_maps, fades)

    field2, face2 = along_x(raw2, [full_x], [base])
    first2, second2 = along_y(field2, face2)
    ends = swapped(*filter_faces(info, first2, field2, second2, table_ends, below, [acc1]), "gz")
    acc2 = filter_lanes(info, first2, field2, second2, table_own)
    grad2, energies = gradient_energy(info, acc2, *ends, table_z, peers)
    maps = final_maps(info, exchanged(energies), base, acc1, *ends, table_z, grad2, all_cells)
    maps = maps.reshape(size_x, size_y, size_z, chans)
    return (jnp.transpose(maps, (3, 0, 1, 2)), half2)


def solution(mesh):
    return jax.shard_map(
        per_device,
        mesh=mesh,
        in_specs=(P("gx", "gy", "gz", None), P(None, "gx", "gy", "gz"), P("gx", "gy", "gz")),
        out_specs=(P(None, "gx", "gy", "gz"), P()),
        check_vma=False,
    )
```

```python
import functools
import math

import jax
import jax.numpy as jnp
import ml_dtypes
import numpy as np
from jax import lax
from jax.experimental import pallas as pl
from jax.experimental.pallas import tpu as pltpu
from jax.sharding import PartitionSpec as P

RADIUS = 8
F32 = jnp.float32
BF16 = jnp.bfloat16
AXES = ("gx", "gy", "gz")


def band(length):
    total = sum(math.exp(-float(d * d) / 32.0) for d in range(-RADIUS, RADIUS + 1))
    gap = np.abs(np.arange(length)[:, None] - np.arange(length)[None, :])
    return np.where(gap <= RADIUS, np.exp(-(gap.astype(np.float64) ** 2) / 32.0) / total, 0.0)


def windows(matrix, size, parts, reach):
    padded = np.pad(matrix, ((0, 0), (reach, reach)))
    return np.stack(
        [padded[p * size : (p + 1) * size, p * size : (p + 1) * size + 2 * reach] for p in range(parts)]
    )


def half(array):
    return np.asarray(array, dtype=ml_dtypes.bfloat16)


def inner_window(size):
    return windows(band(3 * size), size, 3, RADIUS)[1]


PLACE_X, PLACE_Y, PLACE_Z, ODD_Y, ODD_Z, COUNT = range(6)
NT = (((1,), (1,)), ((), ()))
FULL = lax.Precision.HIGHEST


def shape(dims, kind):
    return jax.ShapeDtypeStruct(dims, kind)


def call(body, shapes, info, needs, arrays, flops=10**8, name=None, spaces=None, outs=None, scratch=(), after=()):
    total = sum(a.size * a.dtype.itemsize for a in arrays)
    whole, anywhere = pl.BlockSpec(memory_space=pltpu.VMEM), pl.BlockSpec(memory_space=pl.ANY)
    count, ends = len(needs), len(needs) + len(arrays)

    def wrapped(*refs):
        numbers = {need: ref for need, ref in zip(needs, refs)}
        body(Numbers(numbers), *refs[count:ends], *refs[ends + len(after) :])

    return pl.pallas_call(
        wrapped,
        out_shape=shapes,
        in_specs=[pl.BlockSpec(memory_space=pltpu.SMEM)] * count
        + [spaces or whole] * len(arrays)
        + [anywhere] * len(after),
        out_specs=jax.tree.map(lambda _: outs or whole, shapes),
        scratch_shapes=scratch,
        compiler_params=pltpu.CompilerParams(vmem_limit_bytes=16 * 1024 * 1024),
        cost_estimate=pl.CostEstimate(flops=flops, bytes_accessed=total, transcendentals=0),
        name=name,
    )(*(info[need] for need in needs), *arrays, *after)


class Numbers:
    def __init__(self, refs):
        self.refs = refs

    def __getitem__(self, need):
        return self.refs[need][0]


def dot(a, b):
    return jnp.dot(a, b, preferred_element_type=F32)


def dot_nt(a, b, precision=None):
    return lax.dot_general(a, b, NT, precision=precision, preferred_element_type=F32)


def unit_of(size):
    return (
        lax.broadcasted_iota(jnp.int32, (size, size), 0) == lax.broadcasted_iota(jnp.int32, (size, size), 1)
    ).astype(F32)


def total_of(value):
    return jnp.sum(jnp.sum(value, axis=1, keepdims=True), axis=0, keepdims=True)


def pack_maps(info, voxel_maps, face):
    layers, plane, chans = voxel_maps.shape
    part = chans // 2

    def body(info_ref, src, one, two, first):
        unit = unit_of(chans).astype(BF16)
        for x in range(layers):
            turned = dot_nt(unit, src[x].astype(BF16)).astype(BF16)
            one[x * part : (x + 1) * part, :] = turned[:part]
            two[x * part : (x + 1) * part, :] = turned[part:]
        send_faces(info_ref, ODD_Y, two, face, first=first)

    rows = layers * part
    shapes = (shape((rows, plane), BF16), shape((rows, plane), BF16), shape((rows, face), BF16))
    return call(body, shapes, info, [ODD_Y], [voxel_maps], name="pack_maps")


def pick_tables(info, table_y, table_z):
    def body(info_ref, all_y, all_z, out_y, out_z, sem_y, sem_z):
        copies = [
            pltpu.make_async_copy(all_y.at[info_ref[PLACE_Y]], out_y, sem_y),
            pltpu.make_async_copy(all_z.at[info_ref[PLACE_Z]], out_z, sem_z),
        ]
        for copy in copies:
            copy.start()
        for copy in copies:
            copy.wait()

    shapes = (shape(table_y.shape[1:], BF16), shape(table_z.shape[1:], BF16))
    return call(
        body,
        shapes,
        info,
        [PLACE_Y, PLACE_Z],
        [table_y, table_z],
        name="pick_tables",
        spaces=pl.BlockSpec(memory_space=pl.ANY),
        scratch=(pltpu.SemaphoreType.DMA, pltpu.SemaphoreType.DMA),
    )


def send_faces(info_ref, odd, field, face, first=None, second=None):
    plane = field.shape[1]
    low, high = slice(0, face), slice(plane - face, plane)

    def write(of_first, of_second):
        for ref, lanes in ((first, of_first), (second, of_second)):
            if ref is not None:
                ref[...] = field[:, lanes].astype(ref.dtype)

    pl.when(info_ref[odd] == 0)(lambda: write(high, low))
    pl.when(info_ref[odd] != 0)(lambda: write(low, high))


def cut_face(info, field, face):
    def body(info_ref, field_ref, out):
        send_faces(info_ref, ODD_Y, field_ref, face, second=out)

    shapes = shape((field.shape[0], face), field.dtype)
    return call(body, shapes, info, [ODD_Y], [field], flops=10**9, name="cut_face")


def swapped_dot(info_ref, odd, first, middle, second, weights, rows=slice(None)):
    width = first.shape[1]
    end = weights.shape[0] - width
    even = info_ref[odd] == 0

    def at(when_even, when_odd):
        return weights[pl.ds(pl.multiple_of(jnp.where(even, when_even, when_odd), width), width), :]

    total = dot(first[rows, :], at(end, 0)) + dot(second[rows, :], at(0, end))
    for piece in middle:
        total = total + dot(piece[rows, :], weights[width : width + piece.shape[1], :])
    return total


def mix_layers(info, coefs, chans, sources, sums, out_types, face=0, after=()):
    rows, plane = sources[0].shape
    outs = len(out_types)
    base = len(sources)
    tall, wide = 16, 128

    def body(info_ref, *refs):
        ins, adds, results = refs[:base], refs[base : base + len(sums)], refs[base + len(sums) :]

        def run(tables):
            layers = tables[0][0].shape[0]
            for r in range(0, chans, tall):
                for c in range(0, plane, wide):
                    tiles = [
                        [
                            src[s * chans + r : s * chans + r + tall, c : c + wide].astype(F32)
                            for s in range(layers)
                        ]
                        for src in ins
                    ]
                    for o in range(outs):
                        for x in range(layers):
                            at = slice(x * chans + r, x * chans + r + tall)
                            total = adds[o][at, c : c + wide] if adds else None
                            for tile, table in zip(tiles, tables[o]):
                                for s in range(layers):
                                    weight = float(table[x, s])
                                    if weight != 0.0:
                                        term = tile[s] * weight
                                        total = term if total is None else total + term
                            if total is None:
                                total = jnp.zeros((tall, wide), F32)
                            results[o][at, c : c + wide] = total.astype(results[o].dtype)

        if len(coefs) == 1:
            run(coefs[0])
        else:
            for v in range(len(coefs)):
                pl.when(info_ref[PLACE_X] == v)(functools.partial(run, coefs[v]))
        if face:
            send_faces(info_ref, ODD_Y, results[0], face, first=results[outs])

    shapes = tuple(shape((rows, plane), t) for t in out_types)
    if face:
        shapes += (shape((rows, face), out_types[0]),)
    needs = ([PLACE_X] if len(coefs) > 1 else []) + ([ODD_Y] if face else [])
    return call(body, shapes, info, needs, [*sources, *sums], name="mix_layers", after=after)


def filter_lanes(info, first, middle, second, table):
    def body(info_ref, first_ref, middle_ref, second_ref, weights, out):
        out[...] = swapped_dot(info_ref, ODD_Y, first_ref, [middle_ref], second_ref, weights)

    shapes = shape((first.shape[0], table.shape[1]), F32)
    return call(body, shapes, info, [ODD_Y], [first, middle, second, table], name="filter_lanes")


def filter_faces(info, first, middle, second, table, below=(), after=()):
    rows, face = first.shape[0], table.shape[1] // 2
    extra = below[0].shape[0] if below else 0

    def body(info_ref, first_ref, middle_ref, second_ref, weights, *refs):
        outs = refs[-2:]
        total = swapped_dot(info_ref, ODD_Y, first_ref, [middle_ref], second_ref, weights)
        send_faces(info_ref, ODD_Z, total, face, *(out.at[:rows, :] for out in outs))
        for src, out in zip(refs[:-2], outs):
            out[rows:, :] = src[...]

    shapes = (shape((rows + extra, face), BF16),) * 2
    arrays = [first, middle, second, table, *below]
    return call(body, shapes, info, [ODD_Y, ODD_Z], arrays, name="filter_faces", after=after)


def filter_sent(info, sent, table):
    def body(info_ref, first_ref, second_ref, weights, out):
        width = first_ref.shape[1]
        even = info_ref[ODD_Z] == 0
        of_first = pl.multiple_of(jnp.where(even, 2 * width, width), width)
        of_second = pl.multiple_of(jnp.where(even, width, 2 * width), width)
        total = dot(first_ref[...], weights[pl.ds(of_first, width), :])
        out[...] = total + dot(second_ref[...], weights[pl.ds(of_second, width), :])

    shapes = shape((sent[0].shape[0], table.shape[1]), F32)
    return call(body, shapes, info, [ODD_Z], [*sent, table], name="filter_sent")


def live_lanes(info_ref, layer, dims, size_y, size_z):
    row = layer * size_y + lax.broadcasted_iota(jnp.int32, dims, 1) // size_z
    return row < info_ref[COUNT]


def courses_of(info, acc, first, second, table, bold, chans, size_y, size_z, ready=()):
    frames = bold.shape[1]
    plane = size_y * size_z
    layers = bold.shape[0] // plane
    part = acc.shape[0] // layers

    def body(info_ref, start, first_ref, second_ref, weights, frames_ref, *refs):
        total = jnp.zeros((chans, frames), F32)
        for x in range(layers):
            rows = slice(x * part, (x + 1) * part)
            value = start[rows, :] + swapped_dot(info_ref, ODD_Z, first_ref, [], second_ref, weights, rows)
            if ready:
                rows = slice(x * (chans - part), (x + 1) * (chans - part))
                value = jnp.concatenate([value, refs[0][rows, :].astype(F32)], axis=0)
            keep = live_lanes(info_ref, x, value.shape, size_y, size_z)
            value = jnp.where(keep, value, 0.0).astype(BF16)
            total = total + dot(value, frames_ref[x * plane : (x + 1) * plane, :])
        refs[-1][...] = total

    arrays = [acc, first, second, table, bold, *ready]
    shapes = shape((chans, frames), F32)
    return call(body, shapes, info, [COUNT, ODD_Z], arrays, flops=10**9, name="courses_of")


def write_gradient(info_ref, courses, frames_ref, out, chans, size_y, size_z):
    plane = size_y * size_z
    for x in range(frames_ref.shape[0] // plane):
        value = dot_nt(courses, frames_ref[x * plane : (x + 1) * plane, :])
        keep = live_lanes(info_ref, x, value.shape, size_y, size_z)
        out[x * chans : (x + 1) * chans, :] = jnp.where(keep, value, 0.0).astype(BF16)


def first_gradient(info, sums, bold, chans, size_y, size_z):
    cells, frames = bold.shape

    def body(info_ref, sums_ref, frames_ref, out, half_ref):
        courses = sums_ref[...].astype(BF16)
        half_ref[...] = courses
        write_gradient(info_ref, courses, frames_ref, out, chans, size_y, size_z)

    shapes = (shape((cells * chans // (size_y * size_z), size_y * size_z), BF16), shape((chans, frames), BF16))
    return call(body, shapes, info, [COUNT], [sums, bold], flops=10**9, name="first_gradient")


def fade_of(courses):
    chans = courses.shape[0]
    wide = courses.astype(F32)
    scale = (0.5 * chans) / total_of(wide * wide)
    return unit_of(chans) - dot_nt(courses, courses) * scale


def first_fade(info, half1):
    chans, frames = half1.shape

    def body(_, half_ref, kept_ref, fade_ref):
        fade = fade_of(half_ref[...])
        fade_ref[...] = fade
        kept_ref[...] = jnp.dot(fade, half_ref[...].astype(F32), precision=FULL, preferred_element_type=F32)

    shapes = (shape((chans, frames), F32), shape((chans, chans), F32))
    return call(body, shapes, info, [], [half1], name="first_fade")


def second_gradient(info, change, half1, kept, bold, chans, size_y, size_z, all_cells):
    cells, frames = bold.shape

    def body(info_ref, change_ref, half1_ref, kept_ref, frames_ref, out, half_ref, scale_ref):
        change = change_ref[...]
        energy = jnp.maximum(total_of(half1_ref[...].astype(F32) * change), 0.0) * (1.0 / all_cells)
        scale = 0.5 * lax.rsqrt(energy + 1e-06)
        scale_ref[...] = scale
        courses = (kept_ref[...] + scale * change).astype(BF16)
        half_ref[...] = courses
        write_gradient(info_ref, courses, frames_ref, out, chans, size_y, size_z)

    shapes = (
        shape((cells * chans // (size_y * size_z), size_y * size_z), BF16),
        shape((chans, frames), BF16),
        shape((1, 1), F32),
    )
    arrays = [change, half1, kept, bold]
    return call(body, shapes, info, [COUNT], arrays, flops=10**9, name="second_gradient")


def second_fade(info, half2, fade1, scale1, field, face):
    chans = half2.shape[0]
    rows, plane = field.shape

    def body(info_ref, half_ref, fade_ref, scale_ref, field_ref, fades_ref, out, first):
        fade = fade_of(half_ref[...])
        fades_ref[...] = jnp.dot(fade, fade_ref[...], precision=FULL, preferred_element_type=F32)
        weights = fade * scale_ref[...]
        high = weights.astype(BF16)
        low = (weights - high.astype(F32)).astype(BF16)
        for x in range(rows // chans):
            at = slice(x * chans, (x + 1) * chans)
            block = field_ref[at, :]
            out[at, :] = (dot(high, block) + dot(low, block)).astype(BF16)
        send_faces(info_ref, ODD_Y, out, face, first=first)

    shapes = (
        shape((chans, chans), F32),
        shape((rows, plane), BF16),
        shape((rows, face), BF16),
    )
    arrays = [half2, fade1, scale1, field]
    return call(body, shapes, info, [ODD_Y], arrays, flops=10**9, name="second_fade")


def faded_maps(info, voxel_maps, fades):
    layers, plane, chans = voxel_maps.shape

    def body(_, maps_ref, fades_ref, out):
        for x in range(layers):
            out[x] = dot_nt(maps_ref[x], fades_ref[...], FULL)

    shapes = shape((layers, plane, chans), F32)
    return call(body, shapes, info, [], [voxel_maps, fades], flops=10**9, name="faded_maps")


def whole_gradient(info, acc, first, second, table):
    def body(info_ref, start, first_ref, second_ref, weights, out):
        value = start[...] + swapped_dot(info_ref, ODD_Z, first_ref, [], second_ref, weights)
        out[...] = value.astype(BF16)

    arrays = [acc, first, second, table]
    return call(body, shape(acc.shape, BF16), info, [ODD_Z], arrays, name="whole_gradient")


def gradient_energy(info, acc, first, second, table, peers, after=()):
    rows, plane = acc.shape
    tall = min(rows, 128)

    def body(info_ref, start, first_ref, second_ref, weights, out, energy):
        total = jnp.zeros((tall, plane), F32)
        for r in range(0, rows, tall):
            at = slice(r, r + tall)
            value = start[at, :] + swapped_dot(info_ref, ODD_Z, first_ref, [], second_ref, weights, at)
            total = total + value * value
            out[at, :] = value
        energy[...] = jnp.broadcast_to(total_of(total).reshape(1, 1, 1), energy.shape)

    shapes = (shape((rows, plane), F32), shape((peers, 1, 128), F32))
    arrays = [acc, first, second, table]
    return call(body, shapes, info, [ODD_Z], arrays, name="gradient_energy", after=after)


def final_maps(info, energies, base, acc, first, second, table, grad, all_cells):
    layers, plane, chans = base.shape
    rows = acc.shape[0]
    peers = energies.shape[0]

    def body(info_ref, energies_ref, base_ref, start, first_ref, second_ref, weights, grad_ref, out, held, sems):
        energy = energies_ref[0]
        for d in range(1, peers):
            energy = energy + energies_ref[d]
        scale = 0.5 * lax.rsqrt(energy[:, :1] * (1.0 / all_cells) + 1e-06)
        copies = []
        for x in range(layers):
            at = slice(x * chans, (x + 1) * chans)
            below = slice(rows + x * chans, rows + (x + 1) * chans)
            value = start[at, :] + swapped_dot(info_ref, ODD_Z, first_ref, [], second_ref, weights, below)
            held[x] = base_ref[x] + (value + scale * grad_ref[at, :]).T
            copies.append(pltpu.make_async_copy(held.at[x], out.at[x], sems.at[x]))
            copies[-1].start()
        for copy in copies:
            copy.wait()

    return call(
        body,
        shape(base.shape, F32),
        info,
        [ODD_Z],
        [energies, base, acc, first, second, table, grad],
        name="final_maps",
        outs=pl.BlockSpec(memory_space=pl.ANY),
        scratch=(pltpu.VMEM(base.shape, F32), pltpu.SemaphoreType.DMA((layers,))),
    )


def swapped(first, second, axis, inner_first=False):
    peers = lax.axis_size(axis)
    got = {}
    for start in (1, 0) if inner_first else (0, 1):
        pairs = [(i, i + 1) for i in range(start, peers - 1, 2)]
        pairs += [(j, i) for i, j in pairs]
        got[start] = lax.ppermute((first, second)[start], axis, pairs)
    return got[0], got[1]


def shifted(lower, upper, axis):
    peers = lax.axis_size(axis)
    up = [(i, i + 1) for i in range(peers - 1)]
    down = [(j, i) for i, j in up]
    return lax.ppermute(upper, axis, up), lax.ppermute(lower, axis, down)


def exchanged(parts):
    return lax.all_to_all(parts, AXES, 0, 0, tiled=True)


def hypercube_sum(value):
    steps = []
    for axis in AXES:
        peers = lax.axis_size(axis)
        if peers & (peers - 1):
            return lax.psum(value, AXES)
        steps += [(axis, 1 << b) for b in range(peers.bit_length() - 1)]
    for axis, bit in steps:
        pairs = [(i, i ^ bit) for i in range(lax.axis_size(axis))]
        value = lax.reduce_precision(value, 8, 7)
        value = value + lax.ppermute(value.astype(BF16), axis, pairs).astype(F32)
    return value


def per_device(bold_data, spatial_maps, live_blocks):
    chans, size_x, size_y, size_z = spatial_maps.shape
    frames = bold_data.shape[3]
    plane = size_y * size_z
    parts_x, parts_y, parts_z = (lax.axis_size(a) for a in AXES)
    peers = parts_x * parts_y * parts_z
    places = [lax.axis_index(a).astype(jnp.int32) for a in AXES]
    numbers = [*places, places[1] % 2, places[2] % 2, live_blocks]
    info = [number.reshape(1) for number in numbers]
    bold = bold_data.reshape(size_x * plane, frames)
    voxel_maps = jnp.transpose(spatial_maps, (1, 2, 3, 0)).reshape(size_x, plane, chans)
    all_cells = float(chans * size_x * plane * peers)

    win_x, win_y, win_z = (inner_window(s) for s in (size_x, size_y, size_z))
    unit_y, unit_z = np.eye(size_y), np.eye(size_z)
    ends = np.concatenate([np.kron(win_y.T, unit_z[:, :RADIUS]), np.kron(win_y.T, unit_z[:, -RADIUS:])], 1)
    table_ends = jnp.asarray(half(ends))
    table_own = jnp.asarray(half(np.kron(win_y.T, win_z[:, RADIUS:-RADIUS].T)))
    table_z = jnp.asarray(
        half(np.concatenate([np.kron(unit_y, win_z[:, :RADIUS].T), np.kron(unit_y, win_z[:, -RADIUS:].T)]))
    )
    face_y = RADIUS * size_z

    reach = 2 * RADIUS
    twice = parts_x == 2 and size_y == reach and size_z == 2 * reach
    full_x = band(size_x * parts_x)
    own_x = [slice(p * size_x, (p + 1) * size_x) for p in range(parts_x)]

    def along_x(block, matrices, beside=(), face=face_y):
        chans = block.shape[0] // size_x
        kinds = [BF16] * len(matrices)
        if parts_x == 2:
            mine = [[[m[own_x[p], own_x[p]]] for m in matrices] for p in range(2)]
            other = [[[m[own_x[p], own_x[1 - p]]] for m in matrices] for p in range(2)]
            got = lax.ppermute(block, "gx", [(0, 1), (1, 0)])
            sums = mix_layers(info, mine, chans, [block], [], [F32] * len(matrices))
            return mix_layers(info, other, chans, [got], list(sums), kinds, face=face, after=beside)
        depth = RADIUS * chans
        before, after = shifted(block[:depth], block[-depth:], "gx")
        rest = jnp.zeros((block.shape[0] - depth, plane), BF16)
        before, after = jnp.concatenate([rest, before]), jnp.concatenate([after, rest])
        tables = []
        for lo in (-size_x, 0, size_x):
            columns = np.arange(size_x) + lo + RADIUS
            inside = (columns >= 0) & (columns < win_x.shape[1])
            tables.append(np.where(inside[None], win_x[:, np.clip(columns, 0, win_x.shape[1] - 1)], 0.0))
        return mix_layers(info, [[tables]], chans, [before, block, after], [], kinds, face=face)

    def along_y(field, first):
        return swapped(first, cut_face(info, field, face_y), "gy", inner_first=True)

    def along_rest(field, first):
        first, second = along_y(field, first)
        ends = swapped(*filter_faces(info, first, field, second, table_ends), "gz")
        return filter_lanes(info, first, field, second, table_own), *ends

    def all_courses(acc, first, second, table, ready=()):
        return hypercube_sum(
            courses_of(info, acc, first, second, table, bold, chans, size_y, size_z, ready)
        )

    one, two, face2 = pack_maps(info, voxel_maps, face_y)
    acc, first, second = along_rest(*along_x(one, [full_x]))
    two = whole_gradient(info, *along_rest(two, face2), table_z)
    two = along_x(two, [full_x], face=0)
    courses1 = all_courses(acc, first, second, table_z, two)
    raw1, half1 = first_gradient(info, courses1, bold, chans, size_y, size_z)
    kept, fade1 = first_fade(info, half1)
    if twice:
        square_y = windows(np.linalg.matrix_power(band(size_y * parts_y), 2), size_y, parts_y, reach)
        square_z = windows(np.linalg.matrix_power(band(size_z * parts_z), 2), size_z, parts_z, reach)
        ordered = np.concatenate([unit_z[:, :reach], unit_z[:, reach:]], 1).reshape(size_z, 2, reach)
        tables_y = np.stack([
            np.concatenate([np.kron(w.T, ordered[:, h]) for h in range(2)], 1) for w in square_y
        ])
        tables_z = np.stack([
            np.concatenate([np.kron(unit_y, w[:, h * reach : (h + 1) * reach].T) for h in range(4)])
            for w in square_z
        ])
        table_y2, table_z2 = pick_tables(info, jnp.asarray(half(tables_y)), jnp.asarray(half(tables_z)))
        twice_x, once_x = along_x(raw1, [full_x @ full_x, full_x], [kept], 0)
        first, second = swapped(twice_x, twice_x, "gy", inner_first=True)
        sent = filter_faces(info, first, twice_x, second, table_y2)
        first, second = swapped(*sent, "gz")
        change = all_courses(filter_sent(info, sent, table_z2), first, second, table_z2)
    else:
        once_x, face1 = along_x(raw1, [full_x])
        again = whole_gradient(info, *along_rest(once_x, face1), table_z)
        acc2, first, second = along_rest(*along_x(again, [full_x]))
        change = all_courses(acc2, first, second, table_z)

    raw2, half2, scale1 = second_gradient(
        info, change, half1, kept, bold, chans, size_y, size_z, all_cells
    )
    fades, field1, face1 = second_fade(info, half2, fade1, scale1, once_x, face_y)
    first1, second1 = along_y(field1, face1)
    below = filter_faces(info, first1, field1, second1, table_ends)
    acc1 = filter_lanes(info, first1, field1, second1, table_own)
    base = faded_maps(info, voxel_maps, fades)

    field2, face2 = along_x(raw2, [full_x], [base])
    first2, second2 = along_y(field2, face2)
    ends = swapped(*filter_faces(info, first2, field2, second2, table_ends, below, [acc1]), "gz")
    acc2 = filter_lanes(info, first2, field2, second2, table_own)
    grad2, energies = gradient_energy(info, acc2, *ends, table_z, peers)
    maps = final_maps(info, exchanged(energies), base, acc1, *ends, table_z, grad2, all_cells)
    maps = maps.reshape(size_x, size_y, size_z, chans)
    return (jnp.transpose(maps, (3, 0, 1, 2)), half2)


def solution(mesh):
    return jax.shard_map(
        per_device,
        mesh=mesh,
        in_specs=(P("gx", "gy", "gz", None), P(None, "gx", "gy", "gz"), P("gx", "gy", "gz")),
        out_specs=(P(None, "gx", "gy", "gz"), P()),
        check_vma=False,
    )
```

```python
import functools
import math

import jax
import jax.numpy as jnp
import ml_dtypes
import numpy as np
from jax import lax
from jax.experimental import pallas as pl
from jax.experimental.pallas import tpu as pltpu
from jax.sharding import PartitionSpec as P

RADIUS = 8
F32 = jnp.float32
BF16 = jnp.bfloat16
AXES = ("gx", "gy", "gz")


def band(length):
    total = sum(math.exp(-float(d * d) / 32.0) for d in range(-RADIUS, RADIUS + 1))
    gap = np.abs(np.arange(length)[:, None] - np.arange(length)[None, :])
    return np.where(gap <= RADIUS, np.exp(-(gap.astype(np.float64) ** 2) / 32.0) / total, 0.0)


def windows(matrix, size, parts, reach):
    padded = np.pad(matrix, ((0, 0), (reach, reach)))
    return np.stack(
        [padded[p * size : (p + 1) * size, p * size : (p + 1) * size + 2 * reach] for p in range(parts)]
    )


def half(array):
    return np.asarray(array, dtype=ml_dtypes.bfloat16)


def inner_window(size):
    return windows(band(3 * size), size, 3, RADIUS)[1]


PLACE_X, PLACE_Y, PLACE_Z, ODD_Y, ODD_Z, COUNT = range(6)
NT = (((1,), (1,)), ((), ()))
FULL = lax.Precision.HIGHEST


def shape(dims, kind):
    return jax.ShapeDtypeStruct(dims, kind)


def call(body, shapes, info, needs, arrays, flops=10**8, name=None, spaces=None, outs=None, scratch=(), after=()):
    total = sum(a.size * a.dtype.itemsize for a in arrays)
    whole, anywhere = pl.BlockSpec(memory_space=pltpu.VMEM), pl.BlockSpec(memory_space=pl.ANY)
    count, ends = len(needs), len(needs) + len(arrays)

    def wrapped(*refs):
        numbers = {need: ref for need, ref in zip(needs, refs)}
        body(Numbers(numbers), *refs[count:ends], *refs[ends + len(after) :])

    return pl.pallas_call(
        wrapped,
        out_shape=shapes,
        in_specs=[pl.BlockSpec(memory_space=pltpu.SMEM)] * count
        + [spaces or whole] * len(arrays)
        + [anywhere] * len(after),
        out_specs=jax.tree.map(lambda _: outs or whole, shapes),
        scratch_shapes=scratch,
        compiler_params=pltpu.CompilerParams(vmem_limit_bytes=16 * 1024 * 1024),
        cost_estimate=pl.CostEstimate(flops=flops, bytes_accessed=total, transcendentals=0),
        name=name,
    )(*(info[need] for need in needs), *arrays, *after)


class Numbers:
    def __init__(self, refs):
        self.refs = refs

    def __getitem__(self, need):
        return self.refs[need][0]


def dot(a, b):
    return jnp.dot(a, b, preferred_element_type=F32)


def dot_nt(a, b, precision=None):
    return lax.dot_general(a, b, NT, precision=precision, preferred_element_type=F32)


def unit_of(size):
    return (
        lax.broadcasted_iota(jnp.int32, (size, size), 0) == lax.broadcasted_iota(jnp.int32, (size, size), 1)
    ).astype(F32)


def total_of(value):
    return jnp.sum(jnp.sum(value, axis=1, keepdims=True), axis=0, keepdims=True)


def pack_maps(info, voxel_maps, face):
    layers, plane, chans = voxel_maps.shape
    part = chans // 2

    def body(info_ref, src, one, two, first):
        unit = unit_of(chans).astype(BF16)
        for x in range(layers):
            turned = dot_nt(unit, src[x].astype(BF16)).astype(BF16)
            one[x * part : (x + 1) * part, :] = turned[:part]
            two[x * part : (x + 1) * part, :] = turned[part:]
        send_faces(info_ref, ODD_Y, two, face, first=first)

    rows = layers * part
    shapes = (shape((rows, plane), BF16), shape((rows, plane), BF16), shape((rows, face), BF16))
    return call(body, shapes, info, [ODD_Y], [voxel_maps], name="pack_maps")


def pick_tables(info, table_y, table_z):
    def body(info_ref, all_y, all_z, out_y, out_z, sem_y, sem_z):
        copies = [
            pltpu.make_async_copy(all_y.at[info_ref[PLACE_Y]], out_y, sem_y),
            pltpu.make_async_copy(all_z.at[info_ref[PLACE_Z]], out_z, sem_z),
        ]
        for copy in copies:
            copy.start()
        for copy in copies:
            copy.wait()

    shapes = (shape(table_y.shape[1:], BF16), shape(table_z.shape[1:], BF16))
    return call(
        body,
        shapes,
        info,
        [PLACE_Y, PLACE_Z],
        [table_y, table_z],
        name="pick_tables",
        spaces=pl.BlockSpec(memory_space=pl.ANY),
        scratch=(pltpu.SemaphoreType.DMA, pltpu.SemaphoreType.DMA),
    )


def send_faces(info_ref, odd, field, face, first=None, second=None):
    plane = field.shape[1]
    low, high = slice(0, face), slice(plane - face, plane)

    def write(of_first, of_second):
        for ref, lanes in ((first, of_first), (second, of_second)):
            if ref is not None:
                ref[...] = field[:, lanes].astype(ref.dtype)

    pl.when(info_ref[odd] == 0)(lambda: write(high, low))
    pl.when(info_ref[odd] != 0)(lambda: write(low, high))


def cut_face(info, field, face):
    def body(info_ref, field_ref, out):
        send_faces(info_ref, ODD_Y, field_ref, face, second=out)

    shapes = shape((field.shape[0], face), field.dtype)
    return call(body, shapes, info, [ODD_Y], [field], flops=10**9, name="cut_face")


def swapped_dot(info_ref, odd, first, middle, second, weights, rows=slice(None)):
    width = first.shape[1]
    end = weights.shape[0] - width
    even = info_ref[odd] == 0

    def at(when_even, when_odd):
        return weights[pl.ds(pl.multiple_of(jnp.where(even, when_even, when_odd), width), width), :]

    total = dot(first[rows, :], at(end, 0)) + dot(second[rows, :], at(0, end))
    for piece in middle:
        total = total + dot(piece[rows, :], weights[width : width + piece.shape[1], :])
    return total


def mix_layers(info, coefs, chans, sources, sums, out_types, face=0, after=()):
    rows, plane = sources[0].shape
    outs = len(out_types)
    base = len(sources)
    tall, wide = 16, 128

    def body(info_ref, *refs):
        ins, adds, results = refs[:base], refs[base : base + len(sums)], refs[base + len(sums) :]

        def run(tables):
            layers = tables[0][0].shape[0]
            for r in range(0, chans, tall):
                for c in range(0, plane, wide):
                    tiles = [
                        [
                            src[s * chans + r : s * chans + r + tall, c : c + wide].astype(F32)
                            for s in range(layers)
                        ]
                        for src in ins
                    ]
                    for o in range(outs):
                        for x in range(layers):
                            at = slice(x * chans + r, x * chans + r + tall)
                            total = adds[o][at, c : c + wide] if adds else None
                            for tile, table in zip(tiles, tables[o]):
                                for s in range(layers):
                                    weight = float(table[x, s])
                                    if weight != 0.0:
                                        term = tile[s] * weight
                                        total = term if total is None else total + term
                            if total is None:
                                total = jnp.zeros((tall, wide), F32)
                            results[o][at, c : c + wide] = total.astype(results[o].dtype)

        if len(coefs) == 1:
            run(coefs[0])
        else:
            for v in range(len(coefs)):
                pl.when(info_ref[PLACE_X] == v)(functools.partial(run, coefs[v]))
        if face:
            send_faces(info_ref, ODD_Y, results[0], face, first=results[outs])

    shapes = tuple(shape((rows, plane), t) for t in out_types)
    if face:
        shapes += (shape((rows, face), out_types[0]),)
    needs = ([PLACE_X] if len(coefs) > 1 else []) + ([ODD_Y] if face else [])
    return call(body, shapes, info, needs, [*sources, *sums], name="mix_layers", after=after)


def filter_lanes(info, first, middle, second, table):
    def body(info_ref, first_ref, middle_ref, second_ref, weights, out):
        out[...] = swapped_dot(info_ref, ODD_Y, first_ref, [middle_ref], second_ref, weights)

    shapes = shape((first.shape[0], table.shape[1]), F32)
    return call(body, shapes, info, [ODD_Y], [first, middle, second, table], name="filter_lanes")


def filter_faces(info, first, middle, second, table, below=(), after=()):
    rows, face = first.shape[0], table.shape[1] // 2
    extra = below[0].shape[0] if below else 0

    def body(info_ref, first_ref, middle_ref, second_ref, weights, *refs):
        outs = refs[-2:]
        total = swapped_dot(info_ref, ODD_Y, first_ref, [middle_ref], second_ref, weights)
        send_faces(info_ref, ODD_Z, total, face, *(out.at[:rows, :] for out in outs))
        for src, out in zip(refs[:-2], outs):
            out[rows:, :] = src[...]

    shapes = (shape((rows + extra, face), BF16),) * 2
    arrays = [first, middle, second, table, *below]
    return call(body, shapes, info, [ODD_Y, ODD_Z], arrays, name="filter_faces", after=after)


def filter_sent(info, sent, table):
    def body(info_ref, first_ref, second_ref, weights, out):
        width = first_ref.shape[1]
        even = info_ref[ODD_Z] == 0
        of_first = pl.multiple_of(jnp.where(even, 2 * width, width), width)
        of_second = pl.multiple_of(jnp.where(even, width, 2 * width), width)
        total = dot(first_ref[...], weights[pl.ds(of_first, width), :])
        out[...] = total + dot(second_ref[...], weights[pl.ds(of_second, width), :])

    shapes = shape((sent[0].shape[0], table.shape[1]), F32)
    return call(body, shapes, info, [ODD_Z], [*sent, table], name="filter_sent")


def live_lanes(info_ref, layer, dims, size_y, size_z):
    row = layer * size_y + lax.broadcasted_iota(jnp.int32, dims, 1) // size_z
    return row < info_ref[COUNT]


def courses_of(info, acc, first, second, table, bold, chans, size_y, size_z, ready=()):
    frames = bold.shape[1]
    plane = size_y * size_z
    layers = bold.shape[0] // plane
    part = acc.shape[0] // layers

    def body(info_ref, start, first_ref, second_ref, weights, frames_ref, *refs):
        total = jnp.zeros((chans, frames), F32)
        for x in range(layers):
            rows = slice(x * part, (x + 1) * part)
            value = start[rows, :] + swapped_dot(info_ref, ODD_Z, first_ref, [], second_ref, weights, rows)
            if ready:
                rows = slice(x * (chans - part), (x + 1) * (chans - part))
                value = jnp.concatenate([value, refs[0][rows, :].astype(F32)], axis=0)
            keep = live_lanes(info_ref, x, value.shape, size_y, size_z)
            value = jnp.where(keep, value, 0.0).astype(BF16)
            total = total + dot(value, frames_ref[x * plane : (x + 1) * plane, :])
        refs[-1][...] = total

    arrays = [acc, first, second, table, bold, *ready]
    shapes = shape((chans, frames), F32)
    return call(body, shapes, info, [COUNT, ODD_Z], arrays, flops=10**9, name="courses_of")


def write_gradient(info_ref, courses, frames_ref, out, chans, size_y, size_z):
    plane = size_y * size_z
    for x in range(frames_ref.shape[0] // plane):
        value = dot_nt(courses, frames_ref[x * plane : (x + 1) * plane, :])
        keep = live_lanes(info_ref, x, value.shape, size_y, size_z)
        out[x * chans : (x + 1) * chans, :] = jnp.where(keep, value, 0.0).astype(BF16)


def first_gradient(info, sums, bold, chans, size_y, size_z):
    cells, frames = bold.shape

    def body(info_ref, sums_ref, frames_ref, out, half_ref):
        courses = sums_ref[...].astype(BF16)
        half_ref[...] = courses
        write_gradient(info_ref, courses, frames_ref, out, chans, size_y, size_z)

    shapes = (shape((cells * chans // (size_y * size_z), size_y * size_z), BF16), shape((chans, frames), BF16))
    return call(body, shapes, info, [COUNT], [sums, bold], flops=10**9, name="first_gradient")


def fade_of(courses):
    chans = courses.shape[0]
    wide = courses.astype(F32)
    scale = (0.5 * chans) / total_of(wide * wide)
    return unit_of(chans) - dot_nt(courses, courses) * scale


def first_fade(info, half1):
    chans, frames = half1.shape

    def body(_, half_ref, kept_ref, fade_ref):
        fade = fade_of(half_ref[...])
        fade_ref[...] = fade
        kept_ref[...] = jnp.dot(fade, half_ref[...].astype(F32), precision=FULL, preferred_element_type=F32)

    shapes = (shape((chans, frames), F32), shape((chans, chans), F32))
    return call(body, shapes, info, [], [half1], name="first_fade")


def second_gradient(info, change, half1, kept, bold, chans, size_y, size_z, all_cells):
    cells, frames = bold.shape

    def body(info_ref, change_ref, half1_ref, kept_ref, frames_ref, out, half_ref, scale_ref):
        change = change_ref[...]
        energy = jnp.maximum(total_of(half1_ref[...].astype(F32) * change), 0.0) * (1.0 / all_cells)
        scale = 0.5 * lax.rsqrt(energy + 1e-06)
        scale_ref[...] = scale
        courses = (kept_ref[...] + scale * change).astype(BF16)
        half_ref[...] = courses
        write_gradient(info_ref, courses, frames_ref, out, chans, size_y, size_z)

    shapes = (
        shape((cells * chans // (size_y * size_z), size_y * size_z), BF16),
        shape((chans, frames), BF16),
        shape((1, 1), F32),
    )
    arrays = [change, half1, kept, bold]
    return call(body, shapes, info, [COUNT], arrays, flops=10**9, name="second_gradient")


def second_fade(info, half2, fade1, scale1, field, face):
    chans = half2.shape[0]
    rows, plane = field.shape

    def body(info_ref, half_ref, fade_ref, scale_ref, field_ref, fades_ref, out, first):
        fade = fade_of(half_ref[...])
        fades_ref[...] = jnp.dot(fade, fade_ref[...], precision=FULL, preferred_element_type=F32)
        weights = fade * scale_ref[...]
        high = weights.astype(BF16)
        low = (weights - high.astype(F32)).astype(BF16)
        for x in range(rows // chans):
            at = slice(x * chans, (x + 1) * chans)
            block = field_ref[at, :]
            out[at, :] = (dot(high, block) + dot(low, block)).astype(BF16)
        send_faces(info_ref, ODD_Y, out, face, first=first)

    shapes = (
        shape((chans, chans), F32),
        shape((rows, plane), BF16),
        shape((rows, face), BF16),
    )
    arrays = [half2, fade1, scale1, field]
    return call(body, shapes, info, [ODD_Y], arrays, flops=10**9, name="second_fade")


def faded_maps(info, voxel_maps, fades):
    layers, plane, chans = voxel_maps.shape

    def body(_, maps_ref, fades_ref, out):
        for x in range(layers):
            out[x] = dot_nt(maps_ref[x], fades_ref[...], FULL)

    shapes = shape((layers, plane, chans), F32)
    return call(body, shapes, info, [], [voxel_maps, fades], flops=10**9, name="faded_maps")


def whole_gradient(info, acc, first, second, table, after=()):
    def body(info_ref, start, first_ref, second_ref, weights, out):
        value = start[...] + swapped_dot(info_ref, ODD_Z, first_ref, [], second_ref, weights)
        out[...] = value.astype(BF16)

    arrays = [acc, first, second, table]
    return call(body, shape(acc.shape, BF16), info, [ODD_Z], arrays, name="whole_gradient", after=after)


def gradient_energy(info, acc, first, second, table, peers, after=()):
    rows, plane = acc.shape
    tall = min(rows, 128)

    def body(info_ref, start, first_ref, second_ref, weights, out, energy):
        total = jnp.zeros((tall, plane), F32)
        for r in range(0, rows, tall):
            at = slice(r, r + tall)
            value = start[at, :] + swapped_dot(info_ref, ODD_Z, first_ref, [], second_ref, weights, at)
            total = total + value * value
            out[at, :] = value
        energy[...] = jnp.broadcast_to(total_of(total).reshape(1, 1, 1), energy.shape)

    shapes = (shape((rows, plane), F32), shape((peers, 1, 128), F32))
    arrays = [acc, first, second, table]
    return call(body, shapes, info, [ODD_Z], arrays, name="gradient_energy", after=after)


def final_maps(info, energies, base, acc, first, second, table, grad, all_cells):
    layers, plane, chans = base.shape
    rows = acc.shape[0]
    peers = energies.shape[0]

    def body(info_ref, energies_ref, base_ref, start, first_ref, second_ref, weights, grad_ref, out, held, sems):
        energy = energies_ref[0]
        for d in range(1, peers):
            energy = energy + energies_ref[d]
        scale = 0.5 * lax.rsqrt(energy[:, :1] * (1.0 / all_cells) + 1e-06)
        copies = []
        for x in range(layers):
            at = slice(x * chans, (x + 1) * chans)
            below = slice(rows + x * chans, rows + (x + 1) * chans)
            value = start[at, :] + swapped_dot(info_ref, ODD_Z, first_ref, [], second_ref, weights, below)
            held[x] = base_ref[x] + (value + scale * grad_ref[at, :]).T
            copies.append(pltpu.make_async_copy(held.at[x], out.at[x], sems.at[x]))
            copies[-1].start()
        for copy in copies:
            copy.wait()

    return call(
        body,
        shape(base.shape, F32),
        info,
        [ODD_Z],
        [energies, base, acc, first, second, table, grad],
        name="final_maps",
        outs=pl.BlockSpec(memory_space=pl.ANY),
        scratch=(pltpu.VMEM(base.shape, F32), pltpu.SemaphoreType.DMA((layers,))),
    )


def swapped(first, second, axis, inner_first=False):
    peers = lax.axis_size(axis)
    got = {}
    for start in (1, 0) if inner_first else (0, 1):
        pairs = [(i, i + 1) for i in range(start, peers - 1, 2)]
        pairs += [(j, i) for i, j in pairs]
        got[start] = lax.ppermute((first, second)[start], axis, pairs)
    return got[0], got[1]


def shifted(lower, upper, axis):
    peers = lax.axis_size(axis)
    up = [(i, i + 1) for i in range(peers - 1)]
    down = [(j, i) for i, j in up]
    return lax.ppermute(upper, axis, up), lax.ppermute(lower, axis, down)


def exchanged(parts):
    return lax.all_to_all(parts, AXES, 0, 0, tiled=True)


def hypercube_sum(value):
    steps = []
    for axis in AXES:
        peers = lax.axis_size(axis)
        if peers & (peers - 1):
            return lax.psum(value, AXES)
        steps += [(axis, 1 << b) for b in range(peers.bit_length() - 1)]
    for axis, bit in steps:
        pairs = [(i, i ^ bit) for i in range(lax.axis_size(axis))]
        value = lax.reduce_precision(value, 8, 7)
        value = value + lax.ppermute(value.astype(BF16), axis, pairs).astype(F32)
    return value


def per_device(bold_data, spatial_maps, live_blocks):
    chans, size_x, size_y, size_z = spatial_maps.shape
    frames = bold_data.shape[3]
    plane = size_y * size_z
    parts_x, parts_y, parts_z = (lax.axis_size(a) for a in AXES)
    peers = parts_x * parts_y * parts_z
    places = [lax.axis_index(a).astype(jnp.int32) for a in AXES]
    numbers = [*places, places[1] % 2, places[2] % 2, live_blocks]
    info = [number.reshape(1) for number in numbers]
    bold = bold_data.reshape(size_x * plane, frames)
    voxel_maps = jnp.transpose(spatial_maps, (1, 2, 3, 0)).reshape(size_x, plane, chans)
    all_cells = float(chans * size_x * plane * peers)

    win_x, win_y, win_z = (inner_window(s) for s in (size_x, size_y, size_z))
    unit_y, unit_z = np.eye(size_y), np.eye(size_z)
    ends = np.concatenate([np.kron(win_y.T, unit_z[:, :RADIUS]), np.kron(win_y.T, unit_z[:, -RADIUS:])], 1)
    table_ends = jnp.asarray(half(ends))
    table_own = jnp.asarray(half(np.kron(win_y.T, win_z[:, RADIUS:-RADIUS].T)))
    table_z = jnp.asarray(
        half(np.concatenate([np.kron(unit_y, win_z[:, :RADIUS].T), np.kron(unit_y, win_z[:, -RADIUS:].T)]))
    )
    face_y = RADIUS * size_z

    reach = 2 * RADIUS
    twice = parts_x == 2 and size_y == reach and size_z == 2 * reach
    full_x = band(size_x * parts_x)
    own_x = [slice(p * size_x, (p + 1) * size_x) for p in range(parts_x)]

    def along_x(block, matrices, beside=(), face=face_y):
        chans = block.shape[0] // size_x
        kinds = [BF16] * len(matrices)
        if parts_x == 2:
            mine = [[[m[own_x[p], own_x[p]]] for m in matrices] for p in range(2)]
            other = [[[m[own_x[p], own_x[1 - p]]] for m in matrices] for p in range(2)]
            got = lax.ppermute(block, "gx", [(0, 1), (1, 0)])
            sums = mix_layers(info, mine, chans, [block], [], [F32] * len(matrices))
            return mix_layers(info, other, chans, [got], list(sums), kinds, face=face, after=beside)
        depth = RADIUS * chans
        before, after = shifted(block[:depth], block[-depth:], "gx")
        rest = jnp.zeros((block.shape[0] - depth, plane), BF16)
        before, after = jnp.concatenate([rest, before]), jnp.concatenate([after, rest])
        tables = []
        for lo in (-size_x, 0, size_x):
            columns = np.arange(size_x) + lo + RADIUS
            inside = (columns >= 0) & (columns < win_x.shape[1])
            tables.append(np.where(inside[None], win_x[:, np.clip(columns, 0, win_x.shape[1] - 1)], 0.0))
        return mix_layers(info, [[tables]], chans, [before, block, after], [], kinds, face=face)

    def along_y(field, first):
        return swapped(first, cut_face(info, field, face_y), "gy", inner_first=True)

    def along_rest(field, first):
        return along_z(field, *along_y(field, first))

    def along_z(field, first, second):
        ends = swapped(*filter_faces(info, first, field, second, table_ends), "gz")
        return filter_lanes(info, first, field, second, table_own), *ends

    def all_courses(acc, first, second, table, ready=()):
        return hypercube_sum(
            courses_of(info, acc, first, second, table, bold, chans, size_y, size_z, ready)
        )

    one, two, face2 = pack_maps(info, voxel_maps, face_y)
    one, face1 = along_x(one, [full_x])
    first, second = along_y(one, face1)
    two = whole_gradient(info, *along_rest(two, face2), table_z, [first, second])
    acc, first, second = along_z(one, first, second)
    two = along_x(two, [full_x], face=0)
    courses1 = all_courses(acc, first, second, table_z, two)
    raw1, half1 = first_gradient(info, courses1, bold, chans, size_y, size_z)
    kept, fade1 = first_fade(info, half1)
    if twice:
        square_y = windows(np.linalg.matrix_power(band(size_y * parts_y), 2), size_y, parts_y, reach)
        square_z = windows(np.linalg.matrix_power(band(size_z * parts_z), 2), size_z, parts_z, reach)
        ordered = np.concatenate([unit_z[:, :reach], unit_z[:, reach:]], 1).reshape(size_z, 2, reach)
        tables_y = np.stack([
            np.concatenate([np.kron(w.T, ordered[:, h]) for h in range(2)], 1) for w in square_y
        ])
        tables_z = np.stack([
            np.concatenate([np.kron(unit_y, w[:, h * reach : (h + 1) * reach].T) for h in range(4)])
            for w in square_z
        ])
        table_y2, table_z2 = pick_tables(info, jnp.asarray(half(tables_y)), jnp.asarray(half(tables_z)))
        twice_x, once_x = along_x(raw1, [full_x @ full_x, full_x], [kept], 0)
        first, second = swapped(twice_x, twice_x, "gy", inner_first=True)
        sent = filter_faces(info, first, twice_x, second, table_y2)
        first, second = swapped(*sent, "gz")
        change = all_courses(filter_sent(info, sent, table_z2), first, second, table_z2)
    else:
        once_x, face1 = along_x(raw1, [full_x])
        again = whole_gradient(info, *along_rest(once_x, face1), table_z)
        acc2, first, second = along_rest(*along_x(again, [full_x]))
        change = all_courses(acc2, first, second, table_z)

    raw2, half2, scale1 = second_gradient(
        info, change, half1, kept, bold, chans, size_y, size_z, all_cells
    )
    fades, field1, face1 = second_fade(info, half2, fade1, scale1, once_x, face_y)
    first1, second1 = along_y(field1, face1)
    below = filter_faces(info, first1, field1, second1, table_ends)
    acc1 = filter_lanes(info, first1, field1, second1, table_own)
    base = faded_maps(info, voxel_maps, fades)

    field2, face2 = along_x(raw2, [full_x], [base])
    first2, second2 = along_y(field2, face2)
    ends = swapped(*filter_faces(info, first2, field2, second2, table_ends, below, [acc1]), "gz")
    acc2 = filter_lanes(info, first2, field2, second2, table_own)
    grad2, energies = gradient_energy(info, acc2, *ends, table_z, peers)
    maps = final_maps(info, exchanged(energies), base, acc1, *ends, table_z, grad2, all_cells)
    maps = maps.reshape(size_x, size_y, size_z, chans)
    return (jnp.transpose(maps, (3, 0, 1, 2)), half2)


def solution(mesh):
    return jax.shard_map(
        per_device,
        mesh=mesh,
        in_specs=(P("gx", "gy", "gz", None), P(None, "gx", "gy", "gz"), P("gx", "gy", "gz")),
        out_specs=(P(None, "gx", "gy", "gz"), P()),
        check_vma=False,
    )
```

```python
import functools
import math

import jax
import jax.numpy as jnp
import ml_dtypes
import numpy as np
from jax import lax
from jax.experimental import pallas as pl
from jax.experimental.pallas import tpu as pltpu
from jax.sharding import PartitionSpec as P

RADIUS = 8
F32 = jnp.float32
BF16 = jnp.bfloat16
AXES = ("gx", "gy", "gz")


def band(length):
    total = sum(math.exp(-float(d * d) / 32.0) for d in range(-RADIUS, RADIUS + 1))
    gap = np.abs(np.arange(length)[:, None] - np.arange(length)[None, :])
    return np.where(gap <= RADIUS, np.exp(-(gap.astype(np.float64) ** 2) / 32.0) / total, 0.0)


def windows(matrix, size, parts, reach):
    padded = np.pad(matrix, ((0, 0), (reach, reach)))
    return np.stack(
        [padded[p * size : (p + 1) * size, p * size : (p + 1) * size + 2 * reach] for p in range(parts)]
    )


def half(array):
    return np.asarray(array, dtype=ml_dtypes.bfloat16)


def inner_window(size):
    return windows(band(3 * size), size, 3, RADIUS)[1]


PLACE_X, PLACE_Y, PLACE_Z, ODD_Y, ODD_Z, COUNT = range(6)
NT = (((1,), (1,)), ((), ()))
FULL = lax.Precision.HIGHEST


def shape(dims, kind):
    return jax.ShapeDtypeStruct(dims, kind)


def call(body, shapes, info, needs, arrays, flops=10**8, name=None, spaces=None, outs=None, scratch=(), after=()):
    total = sum(a.size * a.dtype.itemsize for a in arrays)
    whole, anywhere = pl.BlockSpec(memory_space=pltpu.VMEM), pl.BlockSpec(memory_space=pl.ANY)
    count, ends = len(needs), len(needs) + len(arrays)

    def wrapped(*refs):
        numbers = {need: ref for need, ref in zip(needs, refs)}
        body(Numbers(numbers), *refs[count:ends], *refs[ends + len(after) :])

    return pl.pallas_call(
        wrapped,
        out_shape=shapes,
        in_specs=[pl.BlockSpec(memory_space=pltpu.SMEM)] * count
        + [spaces or whole] * len(arrays)
        + [anywhere] * len(after),
        out_specs=jax.tree.map(lambda _: outs or whole, shapes),
        scratch_shapes=scratch,
        compiler_params=pltpu.CompilerParams(vmem_limit_bytes=16 * 1024 * 1024),
        cost_estimate=pl.CostEstimate(flops=flops, bytes_accessed=total, transcendentals=0),
        name=name,
    )(*(info[need] for need in needs), *arrays, *after)


class Numbers:
    def __init__(self, refs):
        self.refs = refs

    def __getitem__(self, need):
        return self.refs[need][0]


def dot(a, b):
    return jnp.dot(a, b, preferred_element_type=F32)


def dot_nt(a, b, precision=None):
    return lax.dot_general(a, b, NT, precision=precision, preferred_element_type=F32)


def unit_of(size):
    return (
        lax.broadcasted_iota(jnp.int32, (size, size), 0) == lax.broadcasted_iota(jnp.int32, (size, size), 1)
    ).astype(F32)


def total_of(value):
    return jnp.sum(jnp.sum(value, axis=1, keepdims=True), axis=0, keepdims=True)


def pack_maps(info, voxel_maps, face):
    layers, plane, chans = voxel_maps.shape
    part = chans // 2

    def body(info_ref, src, one, two, first):
        unit = unit_of(chans).astype(BF16)
        for x in range(layers):
            turned = dot_nt(unit, src[x].astype(BF16)).astype(BF16)
            one[x * part : (x + 1) * part, :] = turned[:part]
            two[x * part : (x + 1) * part, :] = turned[part:]
        send_faces(info_ref, ODD_Y, two, face, first=first)

    rows = layers * part
    shapes = (shape((rows, plane), BF16), shape((rows, plane), BF16), shape((rows, face), BF16))
    return call(body, shapes, info, [ODD_Y], [voxel_maps], name="pack_maps")


def pick_tables(info, table_y, table_z):
    def body(info_ref, all_y, all_z, out_y, out_z, sem_y, sem_z):
        copies = [
            pltpu.make_async_copy(all_y.at[info_ref[PLACE_Y]], out_y, sem_y),
            pltpu.make_async_copy(all_z.at[info_ref[PLACE_Z]], out_z, sem_z),
        ]
        for copy in copies:
            copy.start()
        for copy in copies:
            copy.wait()

    shapes = (shape(table_y.shape[1:], BF16), shape(table_z.shape[1:], BF16))
    return call(
        body,
        shapes,
        info,
        [PLACE_Y, PLACE_Z],
        [table_y, table_z],
        name="pick_tables",
        spaces=pl.BlockSpec(memory_space=pl.ANY),
        scratch=(pltpu.SemaphoreType.DMA, pltpu.SemaphoreType.DMA),
    )


def send_faces(info_ref, odd, field, face, first=None, second=None):
    plane = field.shape[1]
    low, high = slice(0, face), slice(plane - face, plane)

    def write(of_first, of_second):
        for ref, lanes in ((first, of_first), (second, of_second)):
            if ref is not None:
                ref[...] = field[:, lanes].astype(ref.dtype)

    pl.when(info_ref[odd] == 0)(lambda: write(high, low))
    pl.when(info_ref[odd] != 0)(lambda: write(low, high))


def cut_face(info, field, face):
    def body(info_ref, field_ref, out):
        send_faces(info_ref, ODD_Y, field_ref, face, second=out)

    shapes = shape((field.shape[0], face), field.dtype)
    return call(body, shapes, info, [ODD_Y], [field], flops=10**9, name="cut_face")


def swapped_dot(info_ref, odd, first, middle, second, weights, rows=slice(None)):
    width = first.shape[1]
    end = weights.shape[0] - width
    even = info_ref[odd] == 0

    def at(when_even, when_odd):
        return weights[pl.ds(pl.multiple_of(jnp.where(even, when_even, when_odd), width), width), :]

    total = dot(first[rows, :], at(end, 0)) + dot(second[rows, :], at(0, end))
    for piece in middle:
        total = total + dot(piece[rows, :], weights[width : width + piece.shape[1], :])
    return total


def mix_layers(info, coefs, chans, sources, sums, out_types, face=0, after=()):
    rows, plane = sources[0].shape
    outs = len(out_types)
    base = len(sources)
    tall, wide = 16, 128

    def body(info_ref, *refs):
        ins, adds, results = refs[:base], refs[base : base + len(sums)], refs[base + len(sums) :]

        def run(tables):
            layers = tables[0][0].shape[0]
            for r in range(0, chans, tall):
                for c in range(0, plane, wide):
                    tiles = [
                        [
                            src[s * chans + r : s * chans + r + tall, c : c + wide].astype(F32)
                            for s in range(layers)
                        ]
                        for src in ins
                    ]
                    for o in range(outs):
                        for x in range(layers):
                            at = slice(x * chans + r, x * chans + r + tall)
                            total = adds[o][at, c : c + wide] if adds else None
                            for tile, table in zip(tiles, tables[o]):
                                for s in range(layers):
                                    weight = float(table[x, s])
                                    if weight != 0.0:
                                        term = tile[s] * weight
                                        total = term if total is None else total + term
                            if total is None:
                                total = jnp.zeros((tall, wide), F32)
                            results[o][at, c : c + wide] = total.astype(results[o].dtype)

        if len(coefs) == 1:
            run(coefs[0])
        else:
            for v in range(len(coefs)):
                pl.when(info_ref[PLACE_X] == v)(functools.partial(run, coefs[v]))
        if face:
            send_faces(info_ref, ODD_Y, results[0], face, first=results[outs])

    shapes = tuple(shape((rows, plane), t) for t in out_types)
    if face:
        shapes += (shape((rows, face), out_types[0]),)
    needs = ([PLACE_X] if len(coefs) > 1 else []) + ([ODD_Y] if face else [])
    return call(body, shapes, info, needs, [*sources, *sums], name="mix_layers", after=after)


def filter_lanes(info, first, middle, second, table):
    def body(info_ref, first_ref, middle_ref, second_ref, weights, out):
        out[...] = swapped_dot(info_ref, ODD_Y, first_ref, [middle_ref], second_ref, weights)

    shapes = shape((first.shape[0], table.shape[1]), F32)
    return call(body, shapes, info, [ODD_Y], [first, middle, second, table], name="filter_lanes")


def filter_faces(info, first, middle, second, table, below=(), after=()):
    rows, face = first.shape[0], table.shape[1] // 2
    extra = below[0].shape[0] if below else 0

    def body(info_ref, first_ref, middle_ref, second_ref, weights, *refs):
        outs = refs[-2:]
        total = swapped_dot(info_ref, ODD_Y, first_ref, [middle_ref], second_ref, weights)
        send_faces(info_ref, ODD_Z, total, face, *(out.at[:rows, :] for out in outs))
        for src, out in zip(refs[:-2], outs):
            out[rows:, :] = src[...]

    shapes = (shape((rows + extra, face), BF16),) * 2
    arrays = [first, middle, second, table, *below]
    return call(body, shapes, info, [ODD_Y, ODD_Z], arrays, name="filter_faces", after=after)


def filter_sent(info, sent, table):
    def body(info_ref, first_ref, second_ref, weights, out):
        width = first_ref.shape[1]
        even = info_ref[ODD_Z] == 0
        of_first = pl.multiple_of(jnp.where(even, 2 * width, width), width)
        of_second = pl.multiple_of(jnp.where(even, width, 2 * width), width)
        total = dot(first_ref[...], weights[pl.ds(of_first, width), :])
        out[...] = total + dot(second_ref[...], weights[pl.ds(of_second, width), :])

    shapes = shape((sent[0].shape[0], table.shape[1]), F32)
    return call(body, shapes, info, [ODD_Z], [*sent, table], name="filter_sent")


def live_lanes(info_ref, layer, dims, size_y, size_z):
    row = layer * size_y + lax.broadcasted_iota(jnp.int32, dims, 1) // size_z
    return row < info_ref[COUNT]


def courses_of(info, acc, first, second, table, bold, chans, size_y, size_z, ready=()):
    frames = bold.shape[1]
    plane = size_y * size_z
    layers = bold.shape[0] // plane
    part = acc.shape[0] // layers

    def body(info_ref, start, first_ref, second_ref, weights, frames_ref, *refs):
        total = jnp.zeros((chans, frames), F32)
        for x in range(layers):
            rows = slice(x * part, (x + 1) * part)
            value = start[rows, :] + swapped_dot(info_ref, ODD_Z, first_ref, [], second_ref, weights, rows)
            if ready:
                rows = slice(x * (chans - part), (x + 1) * (chans - part))
                value = jnp.concatenate([value, refs[0][rows, :].astype(F32)], axis=0)
            keep = live_lanes(info_ref, x, value.shape, size_y, size_z)
            value = jnp.where(keep, value, 0.0).astype(BF16)
            total = total + dot(value, frames_ref[x * plane : (x + 1) * plane, :])
        refs[-1][...] = total

    arrays = [acc, first, second, table, bold, *ready]
    shapes = shape((chans, frames), F32)
    return call(body, shapes, info, [COUNT, ODD_Z], arrays, flops=10**9, name="courses_of")


def write_gradient(info_ref, courses, frames_ref, outs, chans, size_y, size_z):
    plane = size_y * size_z
    for x in range(frames_ref.shape[0] // plane):
        value = dot_nt(courses, frames_ref[x * plane : (x + 1) * plane, :])
        keep = live_lanes(info_ref, x, value.shape, size_y, size_z)
        value = jnp.where(keep, value, 0.0).astype(BF16)
        part = chans // len(outs)
        for p, out in enumerate(outs):
            out[x * part : (x + 1) * part, :] = value[p * part : (p + 1) * part]


def first_gradient(info, sums, bold, chans, size_y, size_z):
    cells, frames = bold.shape

    def body(info_ref, sums_ref, frames_ref, out, half_ref):
        courses = sums_ref[...].astype(BF16)
        half_ref[...] = courses
        write_gradient(info_ref, courses, frames_ref, [out], chans, size_y, size_z)

    shapes = (shape((cells * chans // (size_y * size_z), size_y * size_z), BF16), shape((chans, frames), BF16))
    return call(body, shapes, info, [COUNT], [sums, bold], flops=10**9, name="first_gradient")


def fade_of(courses):
    chans = courses.shape[0]
    wide = courses.astype(F32)
    scale = (0.5 * chans) / total_of(wide * wide)
    return unit_of(chans) - dot_nt(courses, courses) * scale


def first_fade(info, half1):
    chans, frames = half1.shape

    def body(_, half_ref, kept_ref, fade_ref):
        fade = fade_of(half_ref[...])
        fade_ref[...] = fade
        kept_ref[...] = jnp.dot(fade, half_ref[...].astype(F32), precision=FULL, preferred_element_type=F32)

    shapes = (shape((chans, frames), F32), shape((chans, chans), F32))
    return call(body, shapes, info, [], [half1], name="first_fade")


def second_gradient(info, change, half1, kept, bold, chans, size_y, size_z, all_cells):
    cells, frames = bold.shape

    def body(info_ref, change_ref, half1_ref, kept_ref, frames_ref, one, two, half_ref, scale_ref):
        change = change_ref[...]
        energy = jnp.maximum(total_of(half1_ref[...].astype(F32) * change), 0.0) * (1.0 / all_cells)
        scale = 0.5 * lax.rsqrt(energy + 1e-06)
        scale_ref[...] = scale
        courses = (kept_ref[...] + scale * change).astype(BF16)
        half_ref[...] = courses
        write_gradient(info_ref, courses, frames_ref, [one, two], chans, size_y, size_z)

    shapes = (
        shape((cells * chans // (2 * size_y * size_z), size_y * size_z), BF16),
        shape((cells * chans // (2 * size_y * size_z), size_y * size_z), BF16),
        shape((chans, frames), BF16),
        shape((1, 1), F32),
    )
    arrays = [change, half1, kept, bold]
    return call(body, shapes, info, [COUNT], arrays, flops=10**9, name="second_gradient")


def second_fade(info, half2, fade1, scale1, field, face):
    chans = half2.shape[0]
    rows, plane = field.shape

    def body(info_ref, half_ref, fade_ref, scale_ref, field_ref, fades_ref, out, first):
        fade = fade_of(half_ref[...])
        fades_ref[...] = jnp.dot(fade, fade_ref[...], precision=FULL, preferred_element_type=F32)
        weights = fade * scale_ref[...]
        high = weights.astype(BF16)
        low = (weights - high.astype(F32)).astype(BF16)
        for x in range(rows // chans):
            at = slice(x * chans, (x + 1) * chans)
            block = field_ref[at, :]
            out[at, :] = (dot(high, block) + dot(low, block)).astype(BF16)
        send_faces(info_ref, ODD_Y, out, face, first=first)

    shapes = (
        shape((chans, chans), F32),
        shape((rows, plane), BF16),
        shape((rows, face), BF16),
    )
    arrays = [half2, fade1, scale1, field]
    return call(body, shapes, info, [ODD_Y], arrays, flops=10**9, name="second_fade")


def faded_maps(info, voxel_maps, fades):
    layers, plane, chans = voxel_maps.shape

    def body(_, maps_ref, fades_ref, out):
        for x in range(layers):
            out[x] = dot_nt(maps_ref[x], fades_ref[...], FULL)

    shapes = shape((layers, plane, chans), F32)
    return call(body, shapes, info, [], [voxel_maps, fades], flops=10**9, name="faded_maps")


def whole_gradient(info, acc, first, second, table, after=()):
    def body(info_ref, start, first_ref, second_ref, weights, out):
        value = start[...] + swapped_dot(info_ref, ODD_Z, first_ref, [], second_ref, weights)
        out[...] = value.astype(BF16)

    arrays = [acc, first, second, table]
    return call(body, shape(acc.shape, BF16), info, [ODD_Z], arrays, name="whole_gradient", after=after)


def gradient_energy(info, acc, first, second, table, peers, before=()):
    rows, plane = acc.shape
    tall = min(rows, 128)

    def body(info_ref, start, first_ref, second_ref, weights, *refs):
        out, energy = refs[-2:]
        total = jnp.zeros((tall, plane), F32)
        for r in range(0, rows, tall):
            at = slice(r, r + tall)
            value = start[at, :] + swapped_dot(info_ref, ODD_Z, first_ref, [], second_ref, weights, at)
            total = total + value * value
            out[at, :] = value
        value = jnp.broadcast_to(total_of(total).reshape(1, 1, 1), energy.shape)
        energy[...] = value + refs[0][...] if before else value

    shapes = (shape((rows, plane), F32), shape((peers, 1, 128), F32))
    arrays = [acc, first, second, table, *before]
    return call(body, shapes, info, [ODD_Z], arrays, name="gradient_energy")


def final_maps(info, energies, base, acc, first, second, table, grads, all_cells):
    layers, plane, chans = base.shape
    rows = first.shape[0] - acc.shape[0]
    peers = energies.shape[0]
    part = chans // len(grads)

    def body(info_ref, energies_ref, base_ref, start, first_ref, second_ref, weights, *refs):
        *grad_refs, out, held, sems = refs
        energy = energies_ref[0]
        for d in range(1, peers):
            energy = energy + energies_ref[d]
        scale = 0.5 * lax.rsqrt(energy[:, :1] * (1.0 / all_cells) + 1e-06)
        copies = []
        for x in range(layers):
            at = slice(x * chans, (x + 1) * chans)
            below = slice(rows + x * chans, rows + (x + 1) * chans)
            value = start[at, :] + swapped_dot(info_ref, ODD_Z, first_ref, [], second_ref, weights, below)
            grad = jnp.concatenate([ref[x * part : (x + 1) * part, :] for ref in grad_refs], axis=0)
            held[x] = base_ref[x] + (value + scale * grad).T
            copies.append(pltpu.make_async_copy(held.at[x], out.at[x], sems.at[x]))
            copies[-1].start()
        for copy in copies:
            copy.wait()

    return call(
        body,
        shape(base.shape, F32),
        info,
        [ODD_Z],
        [energies, base, acc, first, second, table, *grads],
        name="final_maps",
        outs=pl.BlockSpec(memory_space=pl.ANY),
        scratch=(pltpu.VMEM(base.shape, F32), pltpu.SemaphoreType.DMA((layers,))),
    )


def swapped(first, second, axis, inner_first=False):
    peers = lax.axis_size(axis)
    got = {}
    for start in (1, 0) if inner_first else (0, 1):
        pairs = [(i, i + 1) for i in range(start, peers - 1, 2)]
        pairs += [(j, i) for i, j in pairs]
        got[start] = lax.ppermute((first, second)[start], axis, pairs)
    return got[0], got[1]


def shifted(lower, upper, axis):
    peers = lax.axis_size(axis)
    up = [(i, i + 1) for i in range(peers - 1)]
    down = [(j, i) for i, j in up]
    return lax.ppermute(upper, axis, up), lax.ppermute(lower, axis, down)


def exchanged(parts):
    return lax.all_to_all(parts, AXES, 0, 0, tiled=True)


def hypercube_sum(value):
    steps = []
    for axis in AXES:
        peers = lax.axis_size(axis)
        if peers & (peers - 1):
            return lax.psum(value, AXES)
        steps += [(axis, 1 << b) for b in range(peers.bit_length() - 1)]
    for axis, bit in steps:
        pairs = [(i, i ^ bit) for i in range(lax.axis_size(axis))]
        value = lax.reduce_precision(value, 8, 7)
        value = value + lax.ppermute(value.astype(BF16), axis, pairs).astype(F32)
    return value


def per_device(bold_data, spatial_maps, live_blocks):
    chans, size_x, size_y, size_z = spatial_maps.shape
    frames = bold_data.shape[3]
    plane = size_y * size_z
    parts_x, parts_y, parts_z = (lax.axis_size(a) for a in AXES)
    peers = parts_x * parts_y * parts_z
    places = [lax.axis_index(a).astype(jnp.int32) for a in AXES]
    numbers = [*places, places[1] % 2, places[2] % 2, live_blocks]
    info = [number.reshape(1) for number in numbers]
    bold = bold_data.reshape(size_x * plane, frames)
    voxel_maps = jnp.transpose(spatial_maps, (1, 2, 3, 0)).reshape(size_x, plane, chans)
    all_cells = float(chans * size_x * plane * peers)

    win_x, win_y, win_z = (inner_window(s) for s in (size_x, size_y, size_z))
    unit_y, unit_z = np.eye(size_y), np.eye(size_z)
    ends = np.concatenate([np.kron(win_y.T, unit_z[:, :RADIUS]), np.kron(win_y.T, unit_z[:, -RADIUS:])], 1)
    table_ends = jnp.asarray(half(ends))
    table_own = jnp.asarray(half(np.kron(win_y.T, win_z[:, RADIUS:-RADIUS].T)))
    table_z = jnp.asarray(
        half(np.concatenate([np.kron(unit_y, win_z[:, :RADIUS].T), np.kron(unit_y, win_z[:, -RADIUS:].T)]))
    )
    face_y = RADIUS * size_z

    reach = 2 * RADIUS
    twice = parts_x == 2 and size_y == reach and size_z == 2 * reach
    full_x = band(size_x * parts_x)
    own_x = [slice(p * size_x, (p + 1) * size_x) for p in range(parts_x)]

    def along_x(block, matrices, beside=(), face=face_y):
        chans = block.shape[0] // size_x
        kinds = [BF16] * len(matrices)
        if parts_x == 2:
            mine = [[[m[own_x[p], own_x[p]]] for m in matrices] for p in range(2)]
            other = [[[m[own_x[p], own_x[1 - p]]] for m in matrices] for p in range(2)]
            got = lax.ppermute(block, "gx", [(0, 1), (1, 0)])
            sums = mix_layers(info, mine, chans, [block], [], [F32] * len(matrices))
            return mix_layers(info, other, chans, [got], list(sums), kinds, face=face, after=beside)
        depth = RADIUS * chans
        before, after = shifted(block[:depth], block[-depth:], "gx")
        rest = jnp.zeros((block.shape[0] - depth, plane), BF16)
        before, after = jnp.concatenate([rest, before]), jnp.concatenate([after, rest])
        tables = []
        for lo in (-size_x, 0, size_x):
            columns = np.arange(size_x) + lo + RADIUS
            inside = (columns >= 0) & (columns < win_x.shape[1])
            tables.append(np.where(inside[None], win_x[:, np.clip(columns, 0, win_x.shape[1] - 1)], 0.0))
        return mix_layers(info, [[tables]], chans, [before, block, after], [], kinds, face=face)

    def along_y(field, first):
        return swapped(first, cut_face(info, field, face_y), "gy", inner_first=True)

    def along_rest(field, first):
        return along_z(field, *along_y(field, first))

    def along_z(field, first, second):
        ends = swapped(*filter_faces(info, first, field, second, table_ends), "gz")
        return filter_lanes(info, first, field, second, table_own), *ends

    def all_courses(acc, first, second, table, ready=()):
        return hypercube_sum(
            courses_of(info, acc, first, second, table, bold, chans, size_y, size_z, ready)
        )

    one, two, face2 = pack_maps(info, voxel_maps, face_y)
    one, face1 = along_x(one, [full_x])
    first, second = along_y(one, face1)
    two = whole_gradient(info, *along_rest(two, face2), table_z, [first, second])
    acc, first, second = along_z(one, first, second)
    two = along_x(two, [full_x], face=0)
    courses1 = all_courses(acc, first, second, table_z, two)
    raw1, half1 = first_gradient(info, courses1, bold, chans, size_y, size_z)
    kept, fade1 = first_fade(info, half1)
    if twice:
        square_y = windows(np.linalg.matrix_power(band(size_y * parts_y), 2), size_y, parts_y, reach)
        square_z = windows(np.linalg.matrix_power(band(size_z * parts_z), 2), size_z, parts_z, reach)
        ordered = np.concatenate([unit_z[:, :reach], unit_z[:, reach:]], 1).reshape(size_z, 2, reach)
        tables_y = np.stack([
            np.concatenate([np.kron(w.T, ordered[:, h]) for h in range(2)], 1) for w in square_y
        ])
        tables_z = np.stack([
            np.concatenate([np.kron(unit_y, w[:, h * reach : (h + 1) * reach].T) for h in range(4)])
            for w in square_z
        ])
        table_y2, table_z2 = pick_tables(info, jnp.asarray(half(tables_y)), jnp.asarray(half(tables_z)))
        twice_x, once_x = along_x(raw1, [full_x @ full_x, full_x], [kept], 0)
        first, second = swapped(twice_x, twice_x, "gy", inner_first=True)
        sent = filter_faces(info, first, twice_x, second, table_y2)
        first, second = swapped(*sent, "gz")
        change = all_courses(filter_sent(info, sent, table_z2), first, second, table_z2)
    else:
        once_x, face1 = along_x(raw1, [full_x])
        again = whole_gradient(info, *along_rest(once_x, face1), table_z)
        acc2, first, second = along_rest(*along_x(again, [full_x]))
        change = all_courses(acc2, first, second, table_z)

    *raws2, half2, scale1 = second_gradient(
        info, change, half1, kept, bold, chans, size_y, size_z, all_cells
    )
    fades, field1, face1 = second_fade(info, half2, fade1, scale1, once_x, face_y)
    first1, second1 = along_y(field1, face1)
    below = filter_faces(info, first1, field1, second1, table_ends)
    acc1 = filter_lanes(info, first1, field1, second1, table_own)
    base = faded_maps(info, voxel_maps, fades)

    fields = [along_x(raws2[0], [full_x]), along_x(raws2[1], [full_x], [base])]
    faces = [along_y(*field) for field in fields]
    ends, accs = [], []
    for p in range(2):
        (first, second), field = faces[p], fields[p][0]
        sent = filter_faces(info, first, field, second, table_ends, ((), below)[p == 0], ((), [acc1])[p == 0])
        ends.append(swapped(*sent, "gz"))
        accs.append(filter_lanes(info, first, field, second, table_own))
    grad_one, energies = gradient_energy(info, accs[0], *ends[0], table_z, peers)
    grad_two, energies = gradient_energy(info, accs[1], *ends[1], table_z, peers, [energies])
    grads = [grad_one, grad_two]
    maps = final_maps(info, exchanged(energies), base, acc1, *ends[0], table_z, grads, all_cells)
    maps = maps.reshape(size_x, size_y, size_z, chans)
    return (jnp.transpose(maps, (3, 0, 1, 2)), half2)


def solution(mesh):
    return jax.shard_map(
        per_device,
        mesh=mesh,
        in_specs=(P("gx", "gy", "gz", None), P(None, "gx", "gy", "gz"), P("gx", "gy", "gz")),
        out_specs=(P(None, "gx", "gy", "gz"), P()),
        check_vma=False,
    )
```

```python
import functools
import math

import jax
import jax.numpy as jnp
import ml_dtypes
import numpy as np
from jax import lax
from jax.experimental import pallas as pl
from jax.experimental.pallas import tpu as pltpu
from jax.sharding import PartitionSpec as P

RADIUS = 8
F32 = jnp.float32
BF16 = jnp.bfloat16
AXES = ("gx", "gy", "gz")


def band(length):
    total = sum(math.exp(-float(d * d) / 32.0) for d in range(-RADIUS, RADIUS + 1))
    gap = np.abs(np.arange(length)[:, None] - np.arange(length)[None, :])
    return np.where(gap <= RADIUS, np.exp(-(gap.astype(np.float64) ** 2) / 32.0) / total, 0.0)


def windows(matrix, size, parts, reach):
    padded = np.pad(matrix, ((0, 0), (reach, reach)))
    return np.stack(
        [padded[p * size : (p + 1) * size, p * size : (p + 1) * size + 2 * reach] for p in range(parts)]
    )


def half(array):
    return np.asarray(array, dtype=ml_dtypes.bfloat16)


def inner_window(size):
    return windows(band(3 * size), size, 3, RADIUS)[1]


PLACE_X, PLACE_Y, PLACE_Z, ODD_Y, ODD_Z, COUNT = range(6)
NT = (((1,), (1,)), ((), ()))
FULL = lax.Precision.HIGHEST


def shape(dims, kind):
    return jax.ShapeDtypeStruct(dims, kind)


def call(body, shapes, info, needs, arrays, flops=10**8, name=None, spaces=None, outs=None, scratch=(), after=()):
    total = sum(a.size * a.dtype.itemsize for a in arrays)
    whole, anywhere = pl.BlockSpec(memory_space=pltpu.VMEM), pl.BlockSpec(memory_space=pl.ANY)
    count, ends = len(needs), len(needs) + len(arrays)

    def wrapped(*refs):
        numbers = {need: ref for need, ref in zip(needs, refs)}
        body(Numbers(numbers), *refs[count:ends], *refs[ends + len(after) :])

    return pl.pallas_call(
        wrapped,
        out_shape=shapes,
        in_specs=[pl.BlockSpec(memory_space=pltpu.SMEM)] * count
        + [spaces or whole] * len(arrays)
        + [anywhere] * len(after),
        out_specs=jax.tree.map(lambda _: outs or whole, shapes),
        scratch_shapes=scratch,
        compiler_params=pltpu.CompilerParams(vmem_limit_bytes=16 * 1024 * 1024),
        cost_estimate=pl.CostEstimate(flops=flops, bytes_accessed=total, transcendentals=0),
        name=name,
    )(*(info[need] for need in needs), *arrays, *after)


class Numbers:
    def __init__(self, refs):
        self.refs = refs

    def __getitem__(self, need):
        return self.refs[need][0]


def dot(a, b):
    return jnp.dot(a, b, preferred_element_type=F32)


def dot_nt(a, b, precision=None):
    return lax.dot_general(a, b, NT, precision=precision, preferred_element_type=F32)


def unit_of(size):
    return (
        lax.broadcasted_iota(jnp.int32, (size, size), 0) == lax.broadcasted_iota(jnp.int32, (size, size), 1)
    ).astype(F32)


def total_of(value):
    return jnp.sum(jnp.sum(value, axis=1, keepdims=True), axis=0, keepdims=True)


def pack_maps(info, voxel_maps, face):
    layers, plane, chans = voxel_maps.shape
    part = chans // 2

    def body(info_ref, src, one, two, first):
        unit = unit_of(chans).astype(BF16)
        for x in range(layers):
            turned = dot_nt(unit, src[x].astype(BF16)).astype(BF16)
            one[x * part : (x + 1) * part, :] = turned[:part]
            two[x * part : (x + 1) * part, :] = turned[part:]
        send_faces(info_ref, ODD_Y, two, face, first=first)

    rows = layers * part
    shapes = (shape((rows, plane), BF16), shape((rows, plane), BF16), shape((rows, face), BF16))
    return call(body, shapes, info, [ODD_Y], [voxel_maps], name="pack_maps")


def pick_tables(info, table_y, table_z):
    def body(info_ref, all_y, all_z, out_y, out_z, sem_y, sem_z):
        copies = [
            pltpu.make_async_copy(all_y.at[info_ref[PLACE_Y]], out_y, sem_y),
            pltpu.make_async_copy(all_z.at[info_ref[PLACE_Z]], out_z, sem_z),
        ]
        for copy in copies:
            copy.start()
        for copy in copies:
            copy.wait()

    shapes = (shape(table_y.shape[1:], BF16), shape(table_z.shape[1:], BF16))
    return call(
        body,
        shapes,
        info,
        [PLACE_Y, PLACE_Z],
        [table_y, table_z],
        name="pick_tables",
        spaces=pl.BlockSpec(memory_space=pl.ANY),
        scratch=(pltpu.SemaphoreType.DMA, pltpu.SemaphoreType.DMA),
    )


def send_faces(info_ref, odd, field, face, first=None, second=None):
    plane = field.shape[1]
    low, high = slice(0, face), slice(plane - face, plane)

    def write(of_first, of_second):
        for ref, lanes in ((first, of_first), (second, of_second)):
            if ref is not None:
                ref[...] = field[:, lanes].astype(ref.dtype)

    pl.when(info_ref[odd] == 0)(lambda: write(high, low))
    pl.when(info_ref[odd] != 0)(lambda: write(low, high))


def cut_face(info, field, face):
    def body(info_ref, field_ref, out):
        send_faces(info_ref, ODD_Y, field_ref, face, second=out)

    shapes = shape((field.shape[0], face), field.dtype)
    return call(body, shapes, info, [ODD_Y], [field], flops=10**9, name="cut_face")


def swapped_dot(info_ref, odd, first, middle, second, weights, rows=slice(None)):
    width = first.shape[1]
    end = weights.shape[0] - width
    even = info_ref[odd] == 0

    def at(when_even, when_odd):
        return weights[pl.ds(pl.multiple_of(jnp.where(even, when_even, when_odd), width), width), :]

    total = dot(first[rows, :], at(end, 0)) + dot(second[rows, :], at(0, end))
    for piece in middle:
        total = total + dot(piece[rows, :], weights[width : width + piece.shape[1], :])
    return total


def mix_layers(info, coefs, chans, sources, sums, out_types, face=0, after=()):
    rows, plane = sources[0].shape
    outs = len(out_types)
    base = len(sources)
    tall, wide = 16, 128

    def body(info_ref, *refs):
        ins, adds, results = refs[:base], refs[base : base + len(sums)], refs[base + len(sums) :]

        def run(tables):
            layers = tables[0][0].shape[0]
            for r in range(0, chans, tall):
                for c in range(0, plane, wide):
                    tiles = [
                        [
                            src[s * chans + r : s * chans + r + tall, c : c + wide].astype(F32)
                            for s in range(layers)
                        ]
                        for src in ins
                    ]
                    for o in range(outs):
                        for x in range(layers):
                            at = slice(x * chans + r, x * chans + r + tall)
                            total = adds[o][at, c : c + wide] if adds else None
                            for tile, table in zip(tiles, tables[o]):
                                for s in range(layers):
                                    weight = float(table[x, s])
                                    if weight != 0.0:
                                        term = tile[s] * weight
                                        total = term if total is None else total + term
                            if total is None:
                                total = jnp.zeros((tall, wide), F32)
                            results[o][at, c : c + wide] = total.astype(results[o].dtype)

        if len(coefs) == 1:
            run(coefs[0])
        else:
            for v in range(len(coefs)):
                pl.when(info_ref[PLACE_X] == v)(functools.partial(run, coefs[v]))
        if face:
            send_faces(info_ref, ODD_Y, results[0], face, first=results[outs])

    shapes = tuple(shape((rows, plane), t) for t in out_types)
    if face:
        shapes += (shape((rows, face), out_types[0]),)
    needs = ([PLACE_X] if len(coefs) > 1 else []) + ([ODD_Y] if face else [])
    return call(body, shapes, info, needs, [*sources, *sums], name="mix_layers", after=after)


def filter_lanes(info, first, middle, second, table):
    def body(info_ref, first_ref, middle_ref, second_ref, weights, out):
        out[...] = swapped_dot(info_ref, ODD_Y, first_ref, [middle_ref], second_ref, weights)

    shapes = shape((first.shape[0], table.shape[1]), F32)
    return call(body, shapes, info, [ODD_Y], [first, middle, second, table], name="filter_lanes")


def filter_faces(info, first, middle, second, table, below=(), after=()):
    rows, face = first.shape[0], table.shape[1] // 2
    extra = below[0].shape[0] if below else 0

    def body(info_ref, first_ref, middle_ref, second_ref, weights, *refs):
        outs = refs[-2:]
        total = swapped_dot(info_ref, ODD_Y, first_ref, [middle_ref], second_ref, weights)
        send_faces(info_ref, ODD_Z, total, face, *(out.at[:rows, :] for out in outs))
        for src, out in zip(refs[:-2], outs):
            out[rows:, :] = src[...]

    shapes = (shape((rows + extra, face), BF16),) * 2
    arrays = [first, middle, second, table, *below]
    return call(body, shapes, info, [ODD_Y, ODD_Z], arrays, name="filter_faces", after=after)


def filter_sent(info, sent, table):
    def body(info_ref, first_ref, second_ref, weights, out):
        width = first_ref.shape[1]
        even = info_ref[ODD_Z] == 0
        of_first = pl.multiple_of(jnp.where(even, 2 * width, width), width)
        of_second = pl.multiple_of(jnp.where(even, width, 2 * width), width)
        total = dot(first_ref[...], weights[pl.ds(of_first, width), :])
        out[...] = total + dot(second_ref[...], weights[pl.ds(of_second, width), :])

    shapes = shape((sent[0].shape[0], table.shape[1]), F32)
    return call(body, shapes, info, [ODD_Z], [*sent, table], name="filter_sent")


def live_lanes(info_ref, layer, dims, size_y, size_z):
    row = layer * size_y + lax.broadcasted_iota(jnp.int32, dims, 1) // size_z
    return row < info_ref[COUNT]


def courses_of(info, acc, first, second, table, bold, chans, size_y, size_z, ready=()):
    frames = bold.shape[1]
    plane = size_y * size_z
    layers = bold.shape[0] // plane
    part = acc.shape[0] // layers

    def body(info_ref, start, first_ref, second_ref, weights, frames_ref, *refs):
        total = jnp.zeros((chans, frames), F32)
        for x in range(layers):
            rows = slice(x * part, (x + 1) * part)
            value = start[rows, :] + swapped_dot(info_ref, ODD_Z, first_ref, [], second_ref, weights, rows)
            if ready:
                rows = slice(x * (chans - part), (x + 1) * (chans - part))
                value = jnp.concatenate([value, refs[0][rows, :].astype(F32)], axis=0)
            keep = live_lanes(info_ref, x, value.shape, size_y, size_z)
            value = jnp.where(keep, value, 0.0).astype(BF16)
            total = total + dot(value, frames_ref[x * plane : (x + 1) * plane, :])
        refs[-1][...] = total

    arrays = [acc, first, second, table, bold, *ready]
    shapes = shape((chans, frames), F32)
    return call(body, shapes, info, [COUNT, ODD_Z], arrays, flops=10**9, name="courses_of")


def write_gradient(info_ref, courses, frames_ref, out, chans, size_y, size_z):
    plane = size_y * size_z
    for x in range(frames_ref.shape[0] // plane):
        value = dot_nt(courses, frames_ref[x * plane : (x + 1) * plane, :])
        keep = live_lanes(info_ref, x, value.shape, size_y, size_z)
        out[x * chans : (x + 1) * chans, :] = jnp.where(keep, value, 0.0).astype(BF16)


def first_gradient(info, sums, bold, chans, size_y, size_z):
    cells, frames = bold.shape

    def body(info_ref, sums_ref, frames_ref, out, half_ref):
        courses = sums_ref[...].astype(BF16)
        half_ref[...] = courses
        write_gradient(info_ref, courses, frames_ref, out, chans, size_y, size_z)

    shapes = (shape((cells * chans // (size_y * size_z), size_y * size_z), BF16), shape((chans, frames), BF16))
    return call(body, shapes, info, [COUNT], [sums, bold], flops=10**9, name="first_gradient")


def fade_of(courses):
    chans = courses.shape[0]
    wide = courses.astype(F32)
    scale = (0.5 * chans) / total_of(wide * wide)
    return unit_of(chans) - dot_nt(courses, courses) * scale


def first_fade(info, half1):
    chans, frames = half1.shape

    def body(_, half_ref, kept_ref, fade_ref):
        fade = fade_of(half_ref[...])
        fade_ref[...] = fade
        kept_ref[...] = jnp.dot(fade, half_ref[...].astype(F32), precision=FULL, preferred_element_type=F32)

    shapes = (shape((chans, frames), F32), shape((chans, chans), F32))
    return call(body, shapes, info, [], [half1], name="first_fade")


def second_gradient(info, change, half1, kept, bold, chans, size_y, size_z, all_cells):
    cells, frames = bold.shape

    def body(info_ref, change_ref, half1_ref, kept_ref, frames_ref, out, half_ref, scale_ref):
        change = change_ref[...]
        energy = jnp.maximum(total_of(half1_ref[...].astype(F32) * change), 0.0) * (1.0 / all_cells)
        scale = 0.5 * lax.rsqrt(energy + 1e-06)
        scale_ref[...] = scale
        courses = (kept_ref[...] + scale * change).astype(BF16)
        half_ref[...] = courses
        write_gradient(info_ref, courses, frames_ref, out, chans, size_y, size_z)

    shapes = (
        shape((cells * chans // (size_y * size_z), size_y * size_z), BF16),
        shape((chans, frames), BF16),
        shape((1, 1), F32),
    )
    arrays = [change, half1, kept, bold]
    return call(body, shapes, info, [COUNT], arrays, flops=10**9, name="second_gradient")


def second_fade(info, half2, fade1, scale1, field, face):
    chans = half2.shape[0]
    rows, plane = field.shape

    def body(info_ref, half_ref, fade_ref, scale_ref, field_ref, fades_ref, out, first):
        fade = fade_of(half_ref[...])
        fades_ref[...] = jnp.dot(fade, fade_ref[...], precision=FULL, preferred_element_type=F32)
        weights = fade * scale_ref[...]
        high = weights.astype(BF16)
        low = (weights - high.astype(F32)).astype(BF16)
        for x in range(rows // chans):
            at = slice(x * chans, (x + 1) * chans)
            block = field_ref[at, :]
            out[at, :] = (dot(high, block) + dot(low, block)).astype(BF16)
        send_faces(info_ref, ODD_Y, out, face, first=first)

    shapes = (
        shape((chans, chans), F32),
        shape((rows, plane), BF16),
        shape((rows, face), BF16),
    )
    arrays = [half2, fade1, scale1, field]
    return call(body, shapes, info, [ODD_Y], arrays, flops=10**9, name="second_fade")


def faded_maps(info, voxel_maps, fades):
    layers, plane, chans = voxel_maps.shape

    def body(_, maps_ref, fades_ref, out):
        for x in range(layers):
            out[x] = dot_nt(maps_ref[x], fades_ref[...], FULL)

    shapes = shape((layers, plane, chans), F32)
    return call(body, shapes, info, [], [voxel_maps, fades], flops=10**9, name="faded_maps")


def whole_gradient(info, acc, first, second, table, after=()):
    def body(info_ref, start, first_ref, second_ref, weights, out):
        value = start[...] + swapped_dot(info_ref, ODD_Z, first_ref, [], second_ref, weights)
        out[...] = value.astype(BF16)

    arrays = [acc, first, second, table]
    return call(body, shape(acc.shape, BF16), info, [ODD_Z], arrays, name="whole_gradient", after=after)


def gradient_energy(info, acc, first, second, table, peers, after=()):
    rows, plane = acc.shape
    tall = min(rows, 128)

    def body(info_ref, start, first_ref, second_ref, weights, out, energy):
        total = jnp.zeros((tall, plane), F32)
        for r in range(0, rows, tall):
            at = slice(r, r + tall)
            value = start[at, :] + swapped_dot(info_ref, ODD_Z, first_ref, [], second_ref, weights, at)
            total = total + value * value
            out[at, :] = value
        energy[...] = jnp.broadcast_to(total_of(total).reshape(1, 1, 1), energy.shape)

    shapes = (shape((rows, plane), F32), shape((peers, 1, 128), F32))
    arrays = [acc, first, second, table]
    return call(body, shapes, info, [ODD_Z], arrays, name="gradient_energy", after=after)


def final_maps(info, energies, base, acc, first, second, table, grad, all_cells):
    layers, plane, chans = base.shape
    rows = acc.shape[0]
    peers = energies.shape[0]

    def body(info_ref, energies_ref, base_ref, start, first_ref, second_ref, weights, grad_ref, out, held, sems):
        energy = energies_ref[0]
        for d in range(1, peers):
            energy = energy + energies_ref[d]
        scale = 0.5 * lax.rsqrt(energy[:, :1] * (1.0 / all_cells) + 1e-06)
        copies = []
        for x in range(layers):
            at = slice(x * chans, (x + 1) * chans)
            below = slice(rows + x * chans, rows + (x + 1) * chans)
            value = start[at, :] + swapped_dot(info_ref, ODD_Z, first_ref, [], second_ref, weights, below)
            held[x] = base_ref[x] + (value + scale * grad_ref[at, :]).T
            copies.append(pltpu.make_async_copy(held.at[x], out.at[x], sems.at[x]))
            copies[-1].start()
        for copy in copies:
            copy.wait()

    return call(
        body,
        shape(base.shape, F32),
        info,
        [ODD_Z],
        [energies, base, acc, first, second, table, grad],
        name="final_maps",
        outs=pl.BlockSpec(memory_space=pl.ANY),
        scratch=(pltpu.VMEM(base.shape, F32), pltpu.SemaphoreType.DMA((layers,))),
    )


def swap(face, axis, start):
    pairs = [(i, i + 1) for i in range(start, lax.axis_size(axis) - 1, 2)]
    return lax.ppermute(face, axis, pairs + [(j, i) for i, j in pairs])


def swapped(first, second, axis, inner_first=False):
    peers = lax.axis_size(axis)
    got = {}
    if axis == "gz":
        return swap(first, axis, 1), swap(second, axis, 0)
    for start in (1, 0) if inner_first else (0, 1):
        pairs = [(i, i + 1) for i in range(start, peers - 1, 2)]
        pairs += [(j, i) for i, j in pairs]
        got[start] = lax.ppermute((first, second)[start], axis, pairs)
    return got[0], got[1]


def shifted(lower, upper, axis):
    peers = lax.axis_size(axis)
    up = [(i, i + 1) for i in range(peers - 1)]
    down = [(j, i) for i, j in up]
    return lax.ppermute(upper, axis, up), lax.ppermute(lower, axis, down)


def exchanged(parts):
    return lax.all_to_all(parts, AXES, 0, 0, tiled=True)


def hypercube_sum(value):
    steps = []
    for axis in AXES:
        peers = lax.axis_size(axis)
        if peers & (peers - 1):
            return lax.psum(value, AXES)
        steps += [(axis, 1 << b) for b in range(peers.bit_length() - 1)]
    for axis, bit in steps:
        pairs = [(i, i ^ bit) for i in range(lax.axis_size(axis))]
        value = lax.reduce_precision(value, 8, 7)
        value = value + lax.ppermute(value.astype(BF16), axis, pairs).astype(F32)
    return value


def per_device(bold_data, spatial_maps, live_blocks):
    chans, size_x, size_y, size_z = spatial_maps.shape
    frames = bold_data.shape[3]
    plane = size_y * size_z
    parts_x, parts_y, parts_z = (lax.axis_size(a) for a in AXES)
    peers = parts_x * parts_y * parts_z
    places = [lax.axis_index(a).astype(jnp.int32) for a in AXES]
    numbers = [*places, places[1] % 2, 1 - places[2] % 2, live_blocks]
    info = [number.reshape(1) for number in numbers]
    bold = bold_data.reshape(size_x * plane, frames)
    voxel_maps = jnp.transpose(spatial_maps, (1, 2, 3, 0)).reshape(size_x, plane, chans)
    all_cells = float(chans * size_x * plane * peers)

    win_x, win_y, win_z = (inner_window(s) for s in (size_x, size_y, size_z))
    unit_y, unit_z = np.eye(size_y), np.eye(size_z)
    ends = np.concatenate([np.kron(win_y.T, unit_z[:, :RADIUS]), np.kron(win_y.T, unit_z[:, -RADIUS:])], 1)
    table_ends = jnp.asarray(half(ends))
    table_own = jnp.asarray(half(np.kron(win_y.T, win_z[:, RADIUS:-RADIUS].T)))
    table_z = jnp.asarray(
        half(np.concatenate([np.kron(unit_y, win_z[:, :RADIUS].T), np.kron(unit_y, win_z[:, -RADIUS:].T)]))
    )
    face_y = RADIUS * size_z

    reach = 2 * RADIUS
    twice = parts_x == 2 and size_y == reach and size_z == 2 * reach
    full_x = band(size_x * parts_x)
    own_x = [slice(p * size_x, (p + 1) * size_x) for p in range(parts_x)]

    def along_x(block, matrices, beside=(), face=face_y):
        chans = block.shape[0] // size_x
        kinds = [BF16] * len(matrices)
        if parts_x == 2:
            mine = [[[m[own_x[p], own_x[p]]] for m in matrices] for p in range(2)]
            other = [[[m[own_x[p], own_x[1 - p]]] for m in matrices] for p in range(2)]
            got = lax.ppermute(block, "gx", [(0, 1), (1, 0)])
            sums = mix_layers(info, mine, chans, [block], [], [F32] * len(matrices))
            return mix_layers(info, other, chans, [got], list(sums), kinds, face=face, after=beside)
        depth = RADIUS * chans
        before, after = shifted(block[:depth], block[-depth:], "gx")
        rest = jnp.zeros((block.shape[0] - depth, plane), BF16)
        before, after = jnp.concatenate([rest, before]), jnp.concatenate([after, rest])
        tables = []
        for lo in (-size_x, 0, size_x):
            columns = np.arange(size_x) + lo + RADIUS
            inside = (columns >= 0) & (columns < win_x.shape[1])
            tables.append(np.where(inside[None], win_x[:, np.clip(columns, 0, win_x.shape[1] - 1)], 0.0))
        return mix_layers(info, [[tables]], chans, [before, block, after], [], kinds, face=face)

    def along_y(field, first):
        return swapped(first, cut_face(info, field, face_y), "gy", inner_first=True)

    def along_rest(field, first):
        return along_z(field, *along_y(field, first))

    def along_z(field, first, second):
        ends = swapped(*filter_faces(info, first, field, second, table_ends), "gz")
        return filter_lanes(info, first, field, second, table_own), *ends

    def all_courses(acc, first, second, table, ready=()):
        return hypercube_sum(
            courses_of(info, acc, first, second, table, bold, chans, size_y, size_z, ready)
        )

    one, two, face2 = pack_maps(info, voxel_maps, face_y)
    one, face1 = along_x(one, [full_x])
    first, second = along_y(one, face1)
    two = whole_gradient(info, *along_rest(two, face2), table_z, [first, second])
    acc, first, second = along_z(one, first, second)
    two = along_x(two, [full_x], face=0)
    courses1 = all_courses(acc, first, second, table_z, two)
    raw1, half1 = first_gradient(info, courses1, bold, chans, size_y, size_z)
    kept, fade1 = first_fade(info, half1)
    if twice:
        square_y = windows(np.linalg.matrix_power(band(size_y * parts_y), 2), size_y, parts_y, reach)
        square_z = windows(np.linalg.matrix_power(band(size_z * parts_z), 2), size_z, parts_z, reach)
        ordered = np.concatenate([unit_z[:, :reach], unit_z[:, reach:]], 1).reshape(size_z, 2, reach)
        tables_y = np.stack([
            np.concatenate([np.kron(w.T, ordered[:, h]) for h in range(2)], 1) for w in square_y
        ])
        tables_z = np.stack([
            np.concatenate([np.kron(unit_y, w[:, h * reach : (h + 1) * reach].T) for h in range(4)])
            for w in square_z
        ])
        table_y2, table_z2 = pick_tables(info, jnp.asarray(half(tables_y)), jnp.asarray(half(tables_z)))
        twice_x, once_x = along_x(raw1, [full_x @ full_x, full_x], [kept], 0)
        first, second = swapped(twice_x, twice_x, "gy", inner_first=True)
        sent = filter_faces(info, first, twice_x, second, table_y2)
        first, second = swapped(*sent, "gz")
        change = all_courses(filter_sent(info, sent, table_z2), first, second, table_z2)
    else:
        once_x, face1 = along_x(raw1, [full_x])
        again = whole_gradient(info, *along_rest(once_x, face1), table_z)
        acc2, first, second = along_rest(*along_x(again, [full_x]))
        change = all_courses(acc2, first, second, table_z)

    raw2, half2, scale1 = second_gradient(
        info, change, half1, kept, bold, chans, size_y, size_z, all_cells
    )
    fades, field1, face1 = second_fade(info, half2, fade1, scale1, once_x, face_y)
    first1, second1 = along_y(field1, face1)
    below = filter_faces(info, first1, field1, second1, table_ends)
    acc1 = filter_lanes(info, first1, field1, second1, table_own)
    base = faded_maps(info, voxel_maps, fades)

    field2, face2 = along_x(raw2, [full_x], [base])
    first2, second2 = along_y(field2, face2)
    ends = swapped(*filter_faces(info, first2, field2, second2, table_ends, below, [acc1]), "gz")
    acc2 = filter_lanes(info, first2, field2, second2, table_own)
    grad2, energies = gradient_energy(info, acc2, *ends, table_z, peers)
    maps = final_maps(info, exchanged(energies), base, acc1, *ends, table_z, grad2, all_cells)
    maps = maps.reshape(size_x, size_y, size_z, chans)
    return (jnp.transpose(maps, (3, 0, 1, 2)), half2)


def solution(mesh):
    return jax.shard_map(
        per_device,
        mesh=mesh,
        in_specs=(P("gx", "gy", "gz", None), P(None, "gx", "gy", "gz"), P("gx", "gy", "gz")),
        out_specs=(P(None, "gx", "gy", "gz"), P()),
        check_vma=False,
    )
```
